128 devices in a mesh: section: 2 (over z_hi), seq: 4 (over x), mp: 16 (over z_lo, y, core).
Axes of the slice: x: 4, y: 4, z: 4 (z_hi: 2, z_lo: 2; z = z_hi * 2 + z_lo), core: 2. Of those that a mesh axis runs over, the one named last changes fastest.
Arguments:
- hidden_states: bfloat16 [2, 1024, 4096], P(None, 'seq', 'mp'), may hold values from -6 to 6
- neighbour_ids: int32 [64, 128], replicated, may hold values from 0 to 63999
- neighbour_table: int32 [2, 16, 2], P(None, 'seq'), may hold values from 0 to 63
- enc_embed: bfloat16 [64000, 1024], P('mp'), may hold values from -6 to 6
- enc_norms: float32 [2, 1024], replicated, may hold values from 0.1 to 1.9
- enc_qkv: bfloat16 [1024, 3, 1024], P('mp'), may hold values from -0.1875 to 0.1875
- enc_out: bfloat16 [1024, 1024], P('mp'), may hold values from -0.1875 to 0.1875
- enc_up: bfloat16 [1024, 4096], P('mp'), may hold values from -0.1875 to 0.1875
- enc_down: bfloat16 [4096, 1024], P('mp'), may hold values from -0.09375 to 0.09375
- dec_norms: float32 [2, 2, 4096], P('section'), may hold values from 0.1 to 1.9
- dec_qkv: bfloat16 [2, 4096, 3, 4096], P('section', None, None, 'mp'), may hold values from -0.09375 to 0.09375
- dec_out: bfloat16 [2, 4096, 4096], P('section', 'mp'), may hold values from -0.09375 to 0.09375
- cross_query: bfloat16 [2, 4096, 4096], P('section', None, 'mp'), may hold values from -0.09375 to 0.09375
- cross_pair: bfloat16 [2, 1024, 2, 4096], P('section', None, None, 'mp'), may hold values from -0.1875 to 0.1875
- cross_out: bfloat16 [2, 4096, 4096], P('section', 'mp'), may hold values from -0.09375 to 0.09375
Outputs:
- block_states: bfloat16 [2, 1024, 4096], P('section', 'seq', 'mp')
The draws below stay inside these ranges and needn't reach their ends.
All inputs are finite; a program needn't handle non-finite values.
Results may differ from the reference program's by a relative error of at most 0.035.
Values may be sent and summed in bfloat16 or wider, within the bound.
No kernel may reach another device: no remote copies, remote signals or barrier semaphores. Data moves between devices by JAX's collectives and lax.ppermute only.
A program may use at most 192 MiB of HBM per device.

```python
import math
import jax
import jax.numpy as jnp
import numpy as np
from jax import lax

D = 4096
HEAD = 128
ENC_D = 1024
ENC_HEAD = 64
ENC_FF = 4096
VOCAB = 64000
BLOCK = 64
NB_LEN = 128
NEIGH = 2
LAYERS = 2
BATCH = 2
SEQ_LEN = 1024
BLOCKS = 16
POOL = 64
N_MP = 16


def set_ends(entries, key, low, largest):
    index_at = [jax.random.randint(jax.random.fold_in(key, axis), (), 0, length) for axis, length in enumerate(entries.shape)]
    longest = entries.shape.index(max(entries.shape))
    beside = index_at[:longest] + [(index_at[longest] + 1) % entries.shape[longest]] + index_at[longest + 1:]
    return entries.at[tuple(index_at)].set(low).at[tuple(beside)].set(largest)


def block_levels(stream_key, shape, shards, low, high):
    gain, own = 1.0, jax.random.fold_in(stream_key, 6)
    for axis_at, parts in shards:
        steps = jnp.exp(jax.random.uniform(jax.random.fold_in(own, axis_at), (parts,), jnp.float32, low / len(shards), high / len(shards)))
        gain = gain * jnp.repeat(steps, shape[axis_at] // parts).reshape([-1 if axis == axis_at else 1 for axis in range(len(shape))])
    return gain


def cumulative_ranks(amount, skew):
    loads = [(1 << 20) // math.isqrt(rank ** skew) + 1 for rank in range(1, amount + 1)]
    deviation = 1 + sum(loads) // (1 << 30)
    return np.cumsum(np.array([max(1, weight // deviation) for weight in loads]))


def ranked(stream_key, extent, number_of, lean):
    table = cumulative_ranks(number_of, lean)
    pick = jax.random.randint(jax.random.fold_in(stream_key, 1), extent, 0, int(table[number_of - 1]))
    grade = jnp.searchsorted(jnp.asarray(table, jnp.int32), pick, side="right")
    return jax.random.permutation(jax.random.fold_in(stream_key, 2), number_of)[grade].astype(jnp.int32)


def noise(own_key, dims, deviation, bound, split=(), held_as=jnp.bfloat16):
    array = jax.random.normal(own_key, dims, jnp.float32) * deviation
    if len(split) > 0:
        array = block_levels(own_key, dims, split, -0.22, 0.18) * array
    return jnp.clip(array, min=-bound, max=bound).astype(held_as)


def setup_inputs(seed: int = 0) -> dict:
    seeds = jax.random.split(jax.random.key(seed), 16)
    return {
        "hidden_states": noise(seeds[0], (BATCH, SEQ_LEN, D), 1.0, 6.0, ((1, 4), (2, 16))),
        "neighbour_ids": set_ends(ranked(seeds[1], (POOL, NB_LEN), VOCAB, 2), jax.random.fold_in(seeds[1], 3), 0, VOCAB - 1).astype(jnp.int32),
        "neighbour_table": set_ends(jax.random.randint(seeds[2], (BATCH, BLOCKS, NEIGH), 0, POOL), jax.random.fold_in(seeds[2], 1), 0, POOL - 1).astype(jnp.int32),
        "enc_embed": noise(seeds[3], (VOCAB, ENC_D), 1.0, 6.0, ((0, 16),)),
        "enc_norms": jnp.clip(1.0 + 0.18 * jax.random.normal(seeds[4], (2, ENC_D), jnp.float32), 0.1, 1.9),
        "enc_qkv": noise(seeds[5], (ENC_D, 3, ENC_D), ENC_D ** -0.5, 0.1875, ((0, 16),)),
        "enc_out": noise(seeds[6], (ENC_D, ENC_D), ENC_D ** -0.5, 0.1875, ((0, 16),)),
        "enc_up": noise(seeds[7], (ENC_D, ENC_FF), ENC_D ** -0.5, 0.1875, ((0, 16),)),
        "enc_down": noise(seeds[8], (ENC_FF, ENC_D), ENC_FF ** -0.5, 0.09375, ((0, 16),)),
        "dec_norms": jnp.clip(1.0 + 0.18 * jax.random.normal(seeds[9], (LAYERS, 2, D), jnp.float32), 0.1, 1.9),
        "dec_qkv": noise(seeds[10], (LAYERS, D, 3, D), D ** -0.5, 0.09375, ((0, 2), (3, 16))),
        "dec_out": noise(seeds[11], (LAYERS, D, D), D ** -0.5, 0.09375, ((0, 2), (1, 16))),
        "cross_query": noise(seeds[12], (LAYERS, D, D), D ** -0.5, 0.09375, ((0, 2), (2, 16))),
        "cross_pair": noise(seeds[13], (LAYERS, ENC_D, 2, D), ENC_D ** -0.5, 0.1875, ((0, 2), (3, 16))),
        "cross_out": noise(seeds[14], (LAYERS, D, D), D ** -0.5, 0.09375, ((0, 2), (1, 16))),
    }


epsilon = 1e-05

def normalize(summed, inputs):
    widened = inputs.astype(jnp.float32)
    meansq = lax.optimization_barrier(jnp.mean(widened * widened, axis=-1, keepdims=True))
    return summed / jnp.sqrt(meansq + epsilon)

def scaled_product(inputs, gains, weight):
    scaled = (inputs.astype(jnp.float32) * gains).astype(jnp.bfloat16)
    flat = scaled.reshape(-1, scaled.shape[-1])
    product = jnp.dot(flat, weight, preferred_element_type=jnp.float32)
    return product.reshape(inputs.shape[:-1] + (weight.shape[1],))

def attend(queries, keys, values, scaling, allowed):
    scores = jnp.einsum('bqhd,bkhd->bhqk', queries.astype(jnp.float32), keys.astype(jnp.float32)) * scaling
    weights = jnp.exp(scores)
    if allowed is not None:
        weights = jnp.where(allowed, weights, 0.0)
    rounded = lax.optimization_barrier(weights.astype(jnp.bfloat16))
    numer = jnp.einsum('bhqk,bkhd->bqhd', rounded.astype(jnp.float32), values.astype(jnp.float32))
    denom = jnp.transpose(lax.optimization_barrier(jnp.sum(weights, axis=3)), (0, 2, 1))
    return (numer / denom[..., None]).astype(jnp.bfloat16)

def split_sum(mixed, weight):
    width = mixed.shape[1] // N_MP
    total = jnp.zeros((mixed.shape[0], weight.shape[1]), jnp.float32)
    for group in range(N_MP):
        term = jnp.dot(mixed[:, group * width:(group + 1) * width], weight[group * width:(group + 1) * width], preferred_element_type=jnp.float32)
        total = total + lax.optimization_barrier(term.astype(jnp.bfloat16)).astype(jnp.float32)
    return total

def causal_heads(shaped):
    length = shaped.shape[0]
    where_pos = jnp.arange(length)
    allowed = where_pos[None, :] <= where_pos[:, None]

    def one_head(triple):
        queries, keys, values = triple
        scores = jnp.dot(queries.astype(jnp.float32), jnp.transpose(keys.astype(jnp.float32))) * HEAD ** (-0.5)
        weights = jnp.where(allowed, jnp.exp(scores), 0.0)
        rounded = lax.optimization_barrier(weights.astype(jnp.bfloat16))
        numer = jnp.dot(rounded.astype(jnp.float32), values.astype(jnp.float32))
        denom = lax.optimization_barrier(jnp.sum(weights, axis=1, keepdims=True))
        return (numer / denom).astype(jnp.bfloat16)
    stacked = jnp.transpose(shaped, (1, 2, 0, 3))
    result = lax.map(one_head, (stacked[0], stacked[1], stacked[2]))
    return jnp.transpose(result, (1, 0, 2)).reshape(length, -1)

def encode(neighbour_ids, neighbour_table, enc_embed, enc_norms, enc_qkv, enc_out, enc_up, enc_down):
    token_ids = neighbour_ids[neighbour_table]
    embedded = enc_embed[token_ids]
    leading = embedded.shape[:-1]
    flat_in = embedded.reshape(-1, NB_LEN, ENC_D)
    heads = ENC_D // ENC_HEAD
    triple = normalize(scaled_product(flat_in, enc_norms[0], enc_qkv.reshape(ENC_D, 3 * ENC_D)), flat_in).astype(jnp.bfloat16)
    shaped = triple.reshape(-1, NB_LEN, 3, heads, ENC_HEAD)
    mixed = attend(shaped[:, :, 0], shaped[:, :, 1], shaped[:, :, 2], ENC_HEAD ** (-0.5), None).reshape(-1, ENC_D)
    inner = flat_in.reshape(-1, ENC_D).astype(jnp.float32) + jnp.dot(mixed, enc_out, preferred_element_type=jnp.float32)
    inner = inner.astype(jnp.bfloat16)
    hidden = jax.nn.gelu(normalize(scaled_product(inner, enc_norms[1], enc_up), inner), approximate=True).astype(jnp.bfloat16)
    outer = inner.astype(jnp.float32) + jnp.dot(hidden, enc_down, preferred_element_type=jnp.float32)
    return outer.astype(jnp.bfloat16).reshape(leading + (ENC_D,))

def decoder_layer(states, encoded, norms, triple_w, out_w, query_w, pair_w, back_w):
    length = states.shape[1]
    heads = D // HEAD
    triple = normalize(scaled_product(states, norms[0], triple_w.reshape(D, 3 * D)), states).astype(jnp.bfloat16)
    shaped = triple.reshape(BATCH, length, 3, heads, HEAD)
    mixed_list = []
    for seq_index in range(BATCH):
        mixed_list.append(causal_heads(shaped[seq_index]))
    mixed = jnp.concatenate(mixed_list, axis=0)
    middle = states.reshape(-1, D).astype(jnp.float32) + split_sum(mixed, out_w)
    middle = middle.astype(jnp.bfloat16).reshape(BATCH, length, D)
    asked = normalize(scaled_product(middle, norms[1], query_w), middle).astype(jnp.bfloat16)
    blocks = encoded.shape[1]
    pairs = jnp.dot(encoded.reshape(-1, ENC_D), pair_w.reshape(ENC_D, 2 * D), preferred_element_type=jnp.float32)
    pairs = pairs.astype(jnp.bfloat16).reshape(BATCH, blocks, NEIGH * NB_LEN, 2 * D)
    pairs = jnp.concatenate([jnp.zeros((BATCH, 1, NEIGH * NB_LEN, 2 * D), jnp.bfloat16), pairs], axis=1)
    pairs = pairs.reshape(BATCH * (blocks + 1), NEIGH * NB_LEN, 2, heads, HEAD)
    padded = jnp.concatenate([jnp.zeros((BATCH, 1, D), jnp.bfloat16), asked, jnp.zeros((BATCH, BLOCK - 1, D), jnp.bfloat16)], axis=1)
    padded = padded.reshape(BATCH * (blocks + 1), BLOCK, heads, HEAD)
    crossed = attend(padded, pairs[:, :, 0], pairs[:, :, 1], HEAD ** (-0.5), None)
    crossed = crossed.reshape(BATCH, (blocks + 1) * BLOCK, D)[:, 1:1 + length].reshape(-1, D)
    result = middle.reshape(-1, D).astype(jnp.float32) + split_sum(crossed, back_w)
    return result.astype(jnp.bfloat16).reshape(BATCH, length, D)

def reference(hidden_states, neighbour_ids, neighbour_table, enc_embed, enc_norms, enc_qkv, enc_out, enc_up, enc_down, dec_norms, dec_qkv, dec_out, cross_query, cross_pair, cross_out):
    encoded = encode(neighbour_ids, neighbour_table, enc_embed, enc_norms, enc_qkv, enc_out, enc_up, enc_down)
    states = hidden_states
    for layer in range(LAYERS):
        states = decoder_layer(states, encoded, dec_norms[layer], dec_qkv[layer], dec_out[layer], cross_query[layer], cross_pair[layer], cross_out[layer])
    return states
```

```python
import functools

import jax
import jax.numpy as jnp
from jax import lax
from jax.experimental import pallas as pl
from jax.experimental.pallas import tpu as pltpu
from jax.sharding import Mesh, PartitionSpec as P

D = 4096
HEAD = 128
ENC_D = 1024
ENC_HEADS = 16
ENC_HEAD = 64
BLOCK = 64
NB_LEN = 128
NEIGH = 2
BATCH = 2
CHIPS = 8
ROWS = 256
WIDTH = 256
UNITS = 4
HALF = ROWS // 2
MP = ("z", "y", "core")
KEYS = NEIGH * NB_LEN
VMEM_LIMIT = 48 * 1024 * 1024

epsilon = 1e-05
f32 = jnp.float32
bf16 = jnp.bfloat16


def params():
    return pltpu.CompilerParams(vmem_limit_bytes=VMEM_LIMIT)


def whole(shape):
    return pl.BlockSpec(shape, lambda *_: (0,) * len(shape))


SCALAR = pl.BlockSpec(memory_space=pltpu.SMEM)


def core_swap(value):
    return lax.ppermute(value, "core", [(0, 1), (1, 0)])


def section_swap(value):
    return lax.ppermute(value, "section", [(0, 1), (1, 0)])


def chips_to_chips(value):
    return lax.all_to_all(value, ("z", "y"), 0, 0, tiled=True)


def gather_rows(local):
    same = chips_to_chips(jnp.broadcast_to(local[None], (CHIPS,) + local.shape))
    return same, core_swap(same)


def scatter_sum(own, other):
    paired = (own.astype(f32) + core_swap(other).astype(f32)).astype(bf16)
    return jnp.sum(chips_to_chips(paired).astype(f32), axis=0)


def project_kernel(units, core_ref, same_ref, swap_ref, gain_ref, w_ref, out_ref, acc_ref, sq_ref):
    step = pl.program_id(0)
    core = core_ref[0]
    parts = w_ref.shape[0]

    @pl.when(step == 0)
    def _():
        acc_ref[...] = jnp.zeros_like(acc_ref)
        sq_ref[...] = jnp.zeros_like(sq_ref)

    for ref, at in ((same_ref, core), (swap_ref, 1 - core)):
        wide = ref[0].astype(f32)
        squares = wide * wide
        sq_ref[...] += squares[:, :128] + squares[:, 128:]
        scaled = (wide * gain_ref[0, pl.ds(at, 1), :]).astype(bf16)
        rows = pl.ds(pl.multiple_of(at * WIDTH, WIDTH), WIDTH)
        for part in range(parts):
            acc_ref[part] += jnp.dot(scaled, w_ref[part, rows, :], preferred_element_type=f32)

    @pl.when(step == CHIPS - 1)
    def _():
        mean = jnp.sum(sq_ref[...], axis=1, keepdims=True) / D
        root = jnp.sqrt(mean + epsilon)
        for part in range(parts):
            done = (acc_ref[part] / root).astype(bf16)
            if not units:
                out_ref[...] = done
                continue
            for unit in range(UNITS):
                h, half = divmod(unit, 2)
                cols = slice(h * HEAD, (h + 1) * HEAD)
                if part == 0:
                    out_ref[unit, :HALF, :] = done[half * HALF : (half + 1) * HALF, cols]
                else:
                    at = HALF + (part - 1) * ROWS
                    out_ref[unit, at : at + ROWS, :] = done[:, cols]


def project(core, same, swap, gains, weight, units):
    parts = weight.shape[0]
    out = (UNITS, HALF + 2 * ROWS, HEAD) if units else (ROWS, WIDTH)
    block = pl.BlockSpec((1, ROWS, WIDTH), lambda s: (s, 0, 0))
    return pl.pallas_call(
        functools.partial(project_kernel, units),
        grid=(CHIPS,),
        in_specs=[
            SCALAR,
            block,
            block,
            pl.BlockSpec((1, 2, WIDTH), lambda s: (s, 0, 0)),
            pl.BlockSpec((parts, 2 * WIDTH, WIDTH), lambda s: (0, s, 0)),
        ],
        out_specs=whole(out),
        out_shape=jax.ShapeDtypeStruct(out, bf16),
        scratch_shapes=[pltpu.VMEM((parts, ROWS, WIDTH), f32), pltpu.VMEM((ROWS, 128), f32)],
        compiler_params=params(),
    )(core, same, swap, gains.reshape(CHIPS, 2, WIDTH), weight)


def causal_kernel(half_ref, triple_ref, out_ref):
    scaling = HEAD ** (-0.5)
    row = lax.broadcasted_iota(jnp.int32, (HALF, ROWS), 0) + half_ref[0] * HALF
    col = lax.broadcasted_iota(jnp.int32, (HALF, ROWS), 1)
    for i in range(UNITS):
        queries = triple_ref[i, :HALF, :]
        numer = jnp.zeros((HALF, HEAD), f32)
        denom = jnp.zeros((HALF, 1), f32)
        for j in range(i + 1):
            keys = triple_ref[j, HALF : HALF + ROWS, :]
            values = triple_ref[j, HALF + ROWS :, :]
            scores = lax.dot_general(
                queries, keys, (((1,), (1,)), ((), ())), preferred_element_type=f32
            )
            weights = jnp.exp(scores * scaling)
            if i == j:
                weights = jnp.where(col <= row, weights, 0.0)
            denom += jnp.sum(weights, axis=1, keepdims=True)
            numer += jnp.dot(weights.astype(bf16), values, preferred_element_type=f32)
        out_ref[i] = (numer / denom).astype(bf16)


def causal(half, triple):
    out = (UNITS, HALF, HEAD)
    return pl.pallas_call(
        causal_kernel,
        in_specs=[SCALAR, whole(triple.shape)],
        out_specs=whole(out),
        grid=(1,),
        out_shape=jax.ShapeDtypeStruct(out, bf16),
        compiler_params=params(),
    )(half, triple)


def crossed_kernel(asked_ref, prev_ref, pairs_ref, out_ref):
    scaling = HEAD ** (-0.5)
    row = lax.broadcasted_iota(jnp.int32, (BLOCK, 2 * KEYS), 0)
    col = lax.broadcasted_iota(jnp.int32, (BLOCK, 2 * KEYS), 1)
    allowed = (row < BLOCK - 1) == (col < KEYS)
    for h in range(2):
        kcols = slice(h * HEAD, (h + 1) * HEAD)
        vcols = slice((2 + h) * HEAD, (3 + h) * HEAD)
        for i in range(ROWS // BLOCK):
            queries = asked_ref[i * BLOCK : (i + 1) * BLOCK, kcols]
            if i == 0:
                keys = jnp.concatenate([prev_ref[:, kcols], pairs_ref[0, :, kcols]], axis=0)
                values = jnp.concatenate([prev_ref[:, vcols], pairs_ref[0, :, vcols]], axis=0)
            else:
                keys = pairs_ref[i - 1 : i + 1, :, kcols].reshape(2 * KEYS, HEAD)
                values = pairs_ref[i - 1 : i + 1, :, vcols].reshape(2 * KEYS, HEAD)
            scores = lax.dot_general(
                queries, keys, (((1,), (1,)), ((), ())), preferred_element_type=f32
            )
            weights = jnp.where(allowed, jnp.exp(scores * scaling), 0.0)
            denom = jnp.sum(weights, axis=1, keepdims=True)
            numer = jnp.dot(weights.astype(bf16), values, preferred_element_type=f32)
            half, at = divmod(i, 2)
            out_ref[h * 2 + half, at * BLOCK : (at + 1) * BLOCK, :] = (numer / denom).astype(bf16)


def cross(asked, prev, pairs):
    out = (UNITS, HALF, HEAD)
    return pl.pallas_call(
        crossed_kernel,
        out_shape=jax.ShapeDtypeStruct(out, bf16),
        compiler_params=params(),
    )(asked, prev, pairs)


def terms_kernel(core_ref, mixed_ref, w_ref, own_ref, other_ref, left_ref):
    core = core_ref[0]

    @pl.when(pl.program_id(0) == 0)
    def _():
        for unit in range(UNITS):
            h, half = divmod(unit, 2)
            left_ref[half * HALF : (half + 1) * HALF, h * HEAD : (h + 1) * HEAD] = mixed_ref[unit]

    product = jnp.dot(left_ref[...], w_ref[...], preferred_element_type=f32).astype(bf16)

    @pl.when(core == 0)
    def _():
        for at in range(2):
            own_ref[at] = product[:, 2 * at * WIDTH : (2 * at + 1) * WIDTH]
            other_ref[at] = product[:, (2 * at + 1) * WIDTH : (2 * at + 2) * WIDTH]

    @pl.when(core == 1)
    def _():
        for at in range(2):
            other_ref[at] = product[:, 2 * at * WIDTH : (2 * at + 1) * WIDTH]
            own_ref[at] = product[:, (2 * at + 1) * WIDTH : (2 * at + 2) * WIDTH]


def terms(core, mixed, weight):
    block = pl.BlockSpec((2, ROWS, WIDTH), lambda s: (s, 0, 0))
    out = jax.ShapeDtypeStruct((CHIPS, ROWS, WIDTH), bf16)
    return pl.pallas_call(
        terms_kernel,
        grid=(CHIPS // 2,),
        in_specs=[
            SCALAR,
            whole((UNITS, HALF, HEAD)),
            pl.BlockSpec((WIDTH, 4 * WIDTH), lambda s: (0, s)),
        ],
        out_specs=[block, block],
        out_shape=[out, out],
        scratch_shapes=[pltpu.VMEM((ROWS, WIDTH), bf16)],
        compiler_params=params(),
    )(core, mixed, weight)


def look_up(ids, enc_embed, core, section):
    vocab_here = enc_embed.shape[0]
    mine = lax.dynamic_slice_in_dim(ids, section * (NB_LEN // 2), NB_LEN // 2, axis=1)
    wanted = mine.reshape(CHIPS, 2, NB_LEN // 2) - lax.axis_index(MP) * vocab_here

    def rows(at):
        picks = lax.dynamic_index_in_dim(wanted, at, 1, keepdims=False).reshape(-1)
        inside = (picks >= 0) & (picks < vocab_here)
        found = enc_embed[jnp.clip(picks, 0, vocab_here - 1)]
        found = jnp.where(inside[:, None], found, jnp.zeros((), bf16))
        return found.reshape(CHIPS, NB_LEN // 2, ENC_D)

    paired = core_swap(rows(1 - core)) + rows(core)
    half = jnp.sum(chips_to_chips(paired).astype(f32), axis=0).astype(bf16)
    far = section_swap(half)
    return jnp.where(
        section == 0, jnp.concatenate([half, far], axis=0), jnp.concatenate([far, half], axis=0)
    )


def weight_pieces(section, enc_qkv, enc_out, enc_up, enc_down):
    width = ENC_D // 2
    triple = lax.dynamic_slice_in_dim(enc_qkv, section * width, width, axis=2)
    up = enc_up.reshape(64, 16, 2, 2, 64)
    up = lax.dynamic_index_in_dim(up, section, 2, keepdims=False)
    up = jnp.transpose(up, (2, 0, 1, 3)).reshape(2, 64, 2, width)
    down = lax.dynamic_slice_in_dim(enc_down, section * 128, 128, axis=0)
    down = down.reshape(2, 64, 2, width)
    local = jnp.concatenate(
        [
            jnp.transpose(up, (0, 2, 1, 3)).reshape(4, 64, width),
            jnp.transpose(down, (0, 2, 1, 3)).reshape(4, 64, width),
            jnp.transpose(triple, (1, 0, 2)),
            jnp.transpose(enc_out.reshape(64, 2, width), (1, 0, 2)),
        ],
        axis=0,
    )
    return lax.all_gather(local, MP, axis=1, tiled=True)


def scaled_rows(values, gain):
    wide = values.astype(f32)
    root = jnp.sqrt(jnp.mean(wide * wide, axis=1, keepdims=True) + epsilon)
    return (wide * gain).astype(bf16), root


def enc_mix_kernel(section_ref, x_ref, gain_ref, q_ref, k_ref, v_ref, o0_ref, o1_ref, out_ref, mix_ref):
    scaled, root = scaled_rows(x_ref[...], gain_ref[...])
    triple = [
        (jnp.dot(scaled, ref[0], preferred_element_type=f32) / root).astype(bf16)
        for ref in (q_ref, k_ref, v_ref)
    ]
    for head in range(ENC_HEADS // 2):
        cols = slice(head * ENC_HEAD, (head + 1) * ENC_HEAD)
        scores = lax.dot_general(
            triple[0][:, cols],
            triple[1][:, cols],
            (((1,), (1,)), ((), ())),
            preferred_element_type=f32,
        )
        weights = jnp.exp(scores * ENC_HEAD ** (-0.5))
        denom = jnp.sum(weights, axis=1, keepdims=True)
        numer = jnp.dot(weights.astype(bf16), triple[2][:, cols], preferred_element_type=f32)
        mix_ref[:, cols] = (numer / denom).astype(bf16)
    mixed = mix_ref[...]
    width = ENC_D // 2
    rows = pl.ds(pl.multiple_of(section_ref[0] * width, width), width)
    for at, ref in enumerate((o0_ref, o1_ref)):
        part = jnp.dot(mixed, ref[0, rows, :], preferred_element_type=f32)
        out_ref[:, at * width : (at + 1) * width] = part.astype(bf16)


def enc_feed_kernel(x_ref, gain_ref, w_ref, out_ref):
    scaled, root = scaled_rows(x_ref[...], gain_ref[...])
    width = ENC_D // 2
    hidden = [
        jax.nn.gelu(
            jnp.dot(scaled, w_ref[piece], preferred_element_type=f32) / root, approximate=True
        ).astype(bf16)
        for piece in range(4)
    ]
    for at in range(2):
        part = jnp.zeros((NB_LEN, width), f32)
        for piece in range(4):
            rows = slice((piece % 2) * width, (piece % 2 + 1) * width)
            down = w_ref[4 + 2 * (piece // 2) + at, rows, :]
            part += jnp.dot(hidden[piece], down, preferred_element_type=f32)
        out_ref[:, at * width : (at + 1) * width] = part.astype(bf16)


def encode(embedded, enc_norms, pieces, section):
    out = jax.ShapeDtypeStruct((NB_LEN, ENC_D), bf16)
    width = ENC_D // 2
    full = whole((NB_LEN, ENC_D))
    gain = whole((1, ENC_D))

    def piece(at):
        return pl.BlockSpec((1, ENC_D, width), lambda s: (at, 0, 0))

    mixed = pl.pallas_call(
        enc_mix_kernel,
        grid=(1,),
        in_specs=[SCALAR, full, gain] + [piece(8 + at) for at in range(5)],
        out_specs=full,
        out_shape=out,
        scratch_shapes=[pltpu.VMEM((NB_LEN, width), bf16)],
        compiler_params=params(),
    )(section, embedded, enc_norms[:1], *([pieces] * 5))
    inner = (embedded.astype(f32) + (mixed.astype(f32) + section_swap(mixed).astype(f32))).astype(
        bf16
    )
    fed = pl.pallas_call(
        enc_feed_kernel,
        grid=(1,),
        in_specs=[full, gain, pl.BlockSpec((8, ENC_D, width), lambda s: (0, 0, 0))],
        out_specs=full,
        out_shape=out,
        compiler_params=params(),
    )(inner, enc_norms[1:], pieces)
    return (inner.astype(f32) + (fed.astype(f32) + section_swap(fed).astype(f32))).astype(bf16)


def pairs_kernel(core_ref, same_ref, swap_ref, w_ref, out_ref):
    core = core_ref[0]
    for ref, at in ((same_ref, core), (swap_ref, 1 - core)):
        out_ref[at] = jnp.dot(ref[0], w_ref[...], preferred_element_type=f32).astype(bf16)


def make_pairs(core, same, swap, weight):
    block = pl.BlockSpec((1, NB_LEN, ENC_D), lambda s: (s, 0, 0))
    return pl.pallas_call(
        pairs_kernel,
        grid=(CHIPS,),
        in_specs=[SCALAR, block, block, whole((ENC_D, 2 * WIDTH))],
        out_specs=pl.BlockSpec((2, NB_LEN, 2 * WIDTH), lambda s: (s, 0, 0)),
        out_shape=jax.ShapeDtypeStruct((2 * CHIPS, NB_LEN, 2 * WIDTH), bf16),
        compiler_params=params(),
    )(core, same, swap, weight)


def self_part(core, half, states, weights):
    norms, triple_w, out_w, query_w, back_w = weights
    same, swap = gather_rows(states)
    triple = project(core, same, swap, norms[0], triple_w, True)
    triple = lax.all_to_all(triple, "seq", 0, 0, tiled=True)
    mixed = lax.all_to_all(causal(half, triple), "seq", 0, 0, tiled=True)
    middle = (states.astype(f32) + scatter_sum(*terms(core, mixed, out_w))).astype(bf16)
    same, swap = gather_rows(middle)
    return middle, project(core, same, swap, norms[1], query_w[None], False)


def cross_part(core, middle, asked, prev, pairs, weights):
    crossed = cross(asked, prev, pairs)
    return (middle.astype(f32) + scatter_sum(*terms(core, crossed, weights[4]))).astype(bf16)


def on_device(
    hidden_states,
    neighbour_ids,
    neighbour_table,
    enc_embed,
    enc_norms,
    enc_qkv,
    enc_out,
    enc_up,
    enc_down,
    dec_norms,
    dec_qkv,
    dec_out,
    cross_query,
    cross_pair,
    cross_out,
):
    section = lax.axis_index("section").astype(jnp.int32)
    core_at = lax.axis_index("core").astype(jnp.int32)
    core = jnp.reshape(core_at, (1,))
    half = jnp.reshape(lax.axis_index("seq").astype(jnp.int32) % 2, (1,))
    blocks_here = neighbour_table.shape[1]
    pieces = weight_pieces(section, enc_qkv, enc_out, enc_up, enc_down)
    slot_ids = neighbour_ids[neighbour_table.reshape(-1)]
    embedded = look_up(slot_ids, enc_embed, core_at, section)
    encoded = encode(embedded, enc_norms, pieces, jnp.reshape(section, (1,)))
    same, swap = gather_rows(encoded)
    pairs = make_pairs(core, same, swap, cross_pair[0].reshape(ENC_D, 2 * WIDTH))
    pairs = pairs.reshape(BATCH, blocks_here, KEYS, 2 * WIDTH)
    count = lax.axis_size("seq")
    prev = lax.ppermute(pairs[:, -1], "seq", [(i, i + 1) for i in range(count - 1)])
    weights = (
        dec_norms[0],
        jnp.transpose(dec_qkv[0], (1, 0, 2)),
        dec_out[0],
        cross_query[0],
        cross_out[0],
    )

    def layer(states, at):
        middle, asked = self_part(core, half, states, weights)
        return cross_part(core, middle, asked, prev[at], pairs[at], weights)

    second = []
    for at in range(BATCH):
        first = layer(hidden_states[at], at)
        second.append(layer(section_swap(first), at))
    return jnp.where(section == 0, section_swap(second[0]), second[1])[None]


def solution(mesh):
    devices = mesh.devices
    sections, seqs = devices.shape[:2]
    split = Mesh(
        devices.reshape(sections, seqs, 2, 4, 2), ("section", "seq", "z", "y", "core")
    )
    mp = ("z", "y", "core")
    return jax.shard_map(
        on_device,
        mesh=split,
        in_specs=(
            P(None, "seq", mp),
            P(),
            P(None, "seq", None),
            P(mp, None),
            P(),
            P(mp, None, None),
            P(mp, None),
            P(mp, None),
            P(mp, None),
            P("section", None, None),
            P("section", None, None, mp),
            P("section", mp, None),
            P("section", None, mp),
            P("section", None, None, mp),
            P("section", mp, None),
        ),
        out_specs=P("section", "seq", mp),
        check_vma=False,
    )
```

```python
import functools

import jax
import jax.numpy as jnp
from jax import lax
from jax.experimental import pallas as pl
from jax.experimental.pallas import tpu as pltpu
from jax.sharding import Mesh, PartitionSpec as P

D = 4096
HEAD = 128
ENC_D = 1024
ENC_HEADS = 16
ENC_HEAD = 64
BLOCK = 64
NB_LEN = 128
NEIGH = 2
BATCH = 2
CHIPS = 8
ROWS = 256
WIDTH = 256
UNITS = 4
GROUP = 4
MP = ("z", "y", "core")
KEYS = NEIGH * NB_LEN
VMEM_LIMIT = 48 * 1024 * 1024

epsilon = 1e-05
f32 = jnp.float32
bf16 = jnp.bfloat16


def params():
    return pltpu.CompilerParams(vmem_limit_bytes=VMEM_LIMIT)


def whole(shape):
    return pl.BlockSpec(shape, lambda *_: (0,) * len(shape))


SCALAR = pl.BlockSpec(memory_space=pltpu.SMEM)


def core_swap(value):
    return lax.ppermute(value, "core", [(0, 1), (1, 0)])


def section_swap(value):
    return lax.ppermute(value, "section", [(0, 1), (1, 0)])


def chips_to_chips(value):
    return lax.all_to_all(value, ("z", "y"), 0, 0, tiled=True)


def gather_chips(local):
    return chips_to_chips(jnp.broadcast_to(local[None], (CHIPS,) + local.shape))


def project_kernel(last, units, pick_ref, x_ref, gain_ref, w_ref, *refs):
    if last:
        acc_in, sq_in, out_ref, acc_ref, sq_ref, left_ref = refs
    else:
        acc_ref, sq_ref, left_ref = refs
    step = pl.program_id(0)
    parts = w_ref.shape[0]

    @pl.when(step == 0)
    def _():
        if last:
            acc_ref[...] = acc_in[...]
            sq_ref[...] = sq_in[...]
        else:
            acc_ref[...] = jnp.zeros_like(acc_ref)
            sq_ref[...] = jnp.zeros_like(sq_ref)

    for at in range(GROUP):
        wide = x_ref[at].astype(f32)
        squares = wide * wide
        sq_ref[...] += squares[:, :128] + squares[:, 128:]
        left_ref[:, at * WIDTH : (at + 1) * WIDTH] = (wide * gain_ref[at, 0]).astype(bf16)
    for part in range(parts):
        right = w_ref[part].reshape(GROUP * WIDTH, WIDTH)
        acc_ref[part] += jnp.dot(left_ref[...], right, preferred_element_type=f32)

    if last:

        @pl.when(step == CHIPS // GROUP - 1)
        def _():
            mean = jnp.sum(sq_ref[...], axis=1, keepdims=True) / D
            root = jnp.sqrt(mean + epsilon)
            for part in range(parts):
                done = (acc_ref[part] / root).astype(bf16)
                if units:
                    for unit in range(UNITS):
                        b, h = divmod(unit, 2)
                        out_ref[unit, part] = done[
                            b * ROWS : (b + 1) * ROWS, h * HEAD : (h + 1) * HEAD
                        ]
                else:
                    out_ref[...] = done


def project_half(pick, rows, gains, weight, before, units):
    parts = weight.shape[0]
    count = BATCH * ROWS
    acc = (parts, count, WIDTH)
    sq = (count, 128)
    last = before is not None
    in_specs = [
        pl.BlockSpec((GROUP, count, WIDTH), lambda s, pick: (s, 0, 0)),
        pl.BlockSpec((GROUP, 1, 1, WIDTH), lambda s, pick: (s, pick[0], 0, 0)),
        pl.BlockSpec((parts, GROUP, 1, WIDTH, WIDTH), lambda s, pick: (0, s, pick[0], 0, 0)),
    ]
    scratch = [pltpu.VMEM((count, GROUP * WIDTH), bf16)]
    if last:
        out = (UNITS, parts, ROWS, HEAD) if units else (count, WIDTH)
        in_specs += [whole(acc), whole(sq)]
        out_specs = whole(out)
        out_shape = jax.ShapeDtypeStruct(out, bf16)
        scratch = [pltpu.VMEM(acc, f32), pltpu.VMEM(sq, f32)] + scratch
    else:
        out_specs = [whole(acc), whole(sq)]
        out_shape = [jax.ShapeDtypeStruct(acc, f32), jax.ShapeDtypeStruct(sq, f32)]
    return pl.pallas_call(
        functools.partial(project_kernel, last, units),
        grid_spec=pltpu.PrefetchScalarGridSpec(
            num_scalar_prefetch=1,
            grid=(CHIPS // GROUP,),
            in_specs=in_specs,
            out_specs=out_specs,
            scratch_shapes=scratch,
        ),
        out_shape=out_shape,
        compiler_params=params(),
        cost_estimate=pl.CostEstimate(
            flops=2 * count * (D // 2) * WIDTH * parts,
            bytes_accessed=D * WIDTH * parts + D * count + 4 * count * WIDTH * parts,
            transcendentals=0,
        ),
    )(
        pick,
        rows,
        gains.reshape(CHIPS, 2, 1, WIDTH),
        weight.reshape(parts, CHIPS, 2, WIDTH, WIDTH),
        *(before or ()),
    )


def project(core, local, gains, weight, units):
    same = gather_chips(local)
    swap = core_swap(same)
    before = project_half(core, same, gains, weight, None, units)
    return project_half(1 - core, swap, gains, weight, before, units)


def causal_kernel(triple_ref, out_ref):
    scaling = HEAD ** (-0.5)
    row = lax.broadcasted_iota(jnp.int32, (ROWS, ROWS), 0)
    col = lax.broadcasted_iota(jnp.int32, (ROWS, ROWS), 1)
    for i in range(UNITS):
        queries = triple_ref[i, 0]
        numer = jnp.zeros((ROWS, HEAD), f32)
        denom = jnp.zeros((ROWS, 1), f32)
        for j in range(i + 1):
            scores = lax.dot_general(
                queries, triple_ref[j, 1], (((1,), (1,)), ((), ())), preferred_element_type=f32
            )
            weights = jnp.exp(scores * scaling)
            if i == j:
                weights = jnp.where(col <= row, weights, 0.0)
            denom += jnp.sum(weights, axis=1, keepdims=True)
            numer += jnp.dot(weights.astype(bf16), triple_ref[j, 2], preferred_element_type=f32)
        out_ref[i] = (numer / denom).astype(bf16)


def causal(triple):
    out = (UNITS, ROWS, HEAD)
    return pl.pallas_call(
        causal_kernel,
        out_shape=jax.ShapeDtypeStruct(out, bf16),
        compiler_params=params(),
    )(triple)


def crossed_kernel(asked_ref, prev_ref, pairs_ref, out_ref):
    scaling = HEAD ** (-0.5)
    row = lax.broadcasted_iota(jnp.int32, (BLOCK, 2 * KEYS), 0)
    col = lax.broadcasted_iota(jnp.int32, (BLOCK, 2 * KEYS), 1)
    allowed = (row < BLOCK - 1) == (col < KEYS)
    for unit in range(UNITS):
        b, h = divmod(unit, 2)
        kcols = slice(h * HEAD, (h + 1) * HEAD)
        vcols = slice((2 + h) * HEAD, (3 + h) * HEAD)
        for i in range(ROWS // BLOCK):
            queries = asked_ref[b * ROWS + i * BLOCK : b * ROWS + (i + 1) * BLOCK, kcols]
            if i == 0:
                keys = jnp.concatenate([prev_ref[b, :, kcols], pairs_ref[b, 0, :, kcols]], axis=0)
                values = jnp.concatenate([prev_ref[b, :, vcols], pairs_ref[b, 0, :, vcols]], axis=0)
            else:
                keys = pairs_ref[b, i - 1 : i + 1, :, kcols].reshape(2 * KEYS, HEAD)
                values = pairs_ref[b, i - 1 : i + 1, :, vcols].reshape(2 * KEYS, HEAD)
            scores = lax.dot_general(
                queries, keys, (((1,), (1,)), ((), ())), preferred_element_type=f32
            )
            weights = jnp.where(allowed, jnp.exp(scores * scaling), 0.0)
            denom = jnp.sum(weights, axis=1, keepdims=True)
            numer = jnp.dot(weights.astype(bf16), values, preferred_element_type=f32)
            out_ref[unit, i * BLOCK : (i + 1) * BLOCK, :] = (numer / denom).astype(bf16)


def cross(asked, prev, pairs):
    out = (UNITS, ROWS, HEAD)
    return pl.pallas_call(
        crossed_kernel,
        out_shape=jax.ShapeDtypeStruct(out, bf16),
        compiler_params=params(),
    )(asked, prev, pairs)


def terms_kernel(pick_ref, mixed_ref, *refs):
    *w_refs, out_ref, left_ref = refs

    @pl.when(pl.program_id(0) == 0)
    def _():
        for unit in range(UNITS):
            b, h = divmod(unit, 2)
            left_ref[b * ROWS : (b + 1) * ROWS, h * HEAD : (h + 1) * HEAD] = mixed_ref[unit]

    for at, w_ref in enumerate(w_refs):
        out_ref[at] = jnp.dot(
            left_ref[...], w_ref[...], preferred_element_type=f32
        ).astype(bf16)


def terms(pick, mixed, weight):
    count = BATCH * ROWS

    def columns(at):
        return pl.BlockSpec((WIDTH, WIDTH), lambda s, pick: (0, 2 * (GROUP * s + at) + pick[0]))

    return pl.pallas_call(
        terms_kernel,
        grid_spec=pltpu.PrefetchScalarGridSpec(
            num_scalar_prefetch=1,
            grid=(CHIPS // GROUP,),
            in_specs=[whole((UNITS, ROWS, HEAD))] + [columns(at) for at in range(GROUP)],
            out_specs=pl.BlockSpec((GROUP, count, WIDTH), lambda s, pick: (s, 0, 0)),
            scratch_shapes=[pltpu.VMEM((count, WIDTH), bf16)],
        ),
        out_shape=jax.ShapeDtypeStruct((CHIPS, count, WIDTH), bf16),
        compiler_params=params(),
        cost_estimate=pl.CostEstimate(
            flops=2 * count * WIDTH * D // 2,
            bytes_accessed=D * WIDTH + D * count,
            transcendentals=0,
        ),
    )(pick, mixed, *([weight] * GROUP))


def product_sum(core, mixed, weight):
    far = core_swap(terms(1 - core, mixed, weight))
    paired = (terms(core, mixed, weight).astype(f32) + far.astype(f32)).astype(bf16)
    return jnp.sum(chips_to_chips(paired).astype(f32), axis=0)


def look_up(ids, enc_embed, core, section):
    vocab_here = enc_embed.shape[0]
    mine = lax.dynamic_slice_in_dim(ids, section * (NB_LEN // 2), NB_LEN // 2, axis=1)
    wanted = mine.reshape(CHIPS, 2, NB_LEN // 2) - lax.axis_index(MP) * vocab_here

    def rows(at):
        picks = lax.dynamic_index_in_dim(wanted, at, 1, keepdims=False).reshape(-1)
        inside = (picks >= 0) & (picks < vocab_here)
        found = enc_embed[jnp.clip(picks, 0, vocab_here - 1)]
        found = jnp.where(inside[:, None], found, jnp.zeros((), bf16))
        return found.reshape(CHIPS, NB_LEN // 2, ENC_D)

    paired = core_swap(rows(1 - core)) + rows(core)
    half = jnp.sum(chips_to_chips(paired).astype(f32), axis=0).astype(bf16)
    far = section_swap(half)
    return jnp.where(
        section == 0, jnp.concatenate([half, far], axis=0), jnp.concatenate([far, half], axis=0)
    )


def weight_pieces(section, enc_qkv, enc_out, enc_up, enc_down):
    width = ENC_D // 2
    triple = lax.dynamic_slice_in_dim(enc_qkv, section * width, width, axis=2)
    up = enc_up.reshape(64, 16, 2, 2, 64)
    up = lax.dynamic_index_in_dim(up, section, 2, keepdims=False)
    up = jnp.transpose(up, (2, 0, 1, 3)).reshape(2, 64, 2, width)
    down = lax.dynamic_slice_in_dim(enc_down, section * 128, 128, axis=0)
    down = down.reshape(2, 64, 2, width)
    local = jnp.concatenate(
        [
            jnp.transpose(up, (0, 2, 1, 3)).reshape(4, 64, width),
            jnp.transpose(down, (0, 2, 1, 3)).reshape(4, 64, width),
            jnp.transpose(triple, (1, 0, 2)),
            jnp.transpose(enc_out.reshape(64, 2, width), (1, 0, 2)),
        ],
        axis=0,
    )
    return lax.all_gather(local, MP, axis=1, tiled=True)


def scaled_rows(values, gain):
    wide = values.astype(f32)
    root = jnp.sqrt(jnp.mean(wide * wide, axis=1, keepdims=True) + epsilon)
    return (wide * gain).astype(bf16), root


def enc_mix_kernel(section_ref, x_ref, gain_ref, q_ref, k_ref, v_ref, o0_ref, o1_ref, out_ref, mix_ref):
    scaled, root = scaled_rows(x_ref[...], gain_ref[...])
    triple = [
        (jnp.dot(scaled, ref[0], preferred_element_type=f32) / root).astype(bf16)
        for ref in (q_ref, k_ref, v_ref)
    ]
    for head in range(ENC_HEADS // 2):
        cols = slice(head * ENC_HEAD, (head + 1) * ENC_HEAD)
        scores = lax.dot_general(
            triple[0][:, cols],
            triple[1][:, cols],
            (((1,), (1,)), ((), ())),
            preferred_element_type=f32,
        )
        weights = jnp.exp(scores * ENC_HEAD ** (-0.5))
        denom = jnp.sum(weights, axis=1, keepdims=True)
        numer = jnp.dot(weights.astype(bf16), triple[2][:, cols], preferred_element_type=f32)
        mix_ref[:, cols] = (numer / denom).astype(bf16)
    mixed = mix_ref[...]
    width = ENC_D // 2
    rows = pl.ds(pl.multiple_of(section_ref[0] * width, width), width)
    for at, ref in enumerate((o0_ref, o1_ref)):
        part = jnp.dot(mixed, ref[0, rows, :], preferred_element_type=f32)
        out_ref[:, at * width : (at + 1) * width] = part.astype(bf16)


def enc_feed_kernel(x_ref, gain_ref, w_ref, out_ref):
    scaled, root = scaled_rows(x_ref[...], gain_ref[...])
    width = ENC_D // 2
    hidden = [
        jax.nn.gelu(
            jnp.dot(scaled, w_ref[piece], preferred_element_type=f32) / root, approximate=True
        ).astype(bf16)
        for piece in range(4)
    ]
    for at in range(2):
        part = jnp.zeros((NB_LEN, width), f32)
        for piece in range(4):
            rows = slice((piece % 2) * width, (piece % 2 + 1) * width)
            down = w_ref[4 + 2 * (piece // 2) + at, rows, :]
            part += jnp.dot(hidden[piece], down, preferred_element_type=f32)
        out_ref[:, at * width : (at + 1) * width] = part.astype(bf16)


def encode(embedded, enc_norms, pieces, section):
    out = jax.ShapeDtypeStruct((NB_LEN, ENC_D), bf16)
    width = ENC_D // 2
    full = whole((NB_LEN, ENC_D))
    gain = whole((1, ENC_D))

    def piece(at):
        return pl.BlockSpec((1, ENC_D, width), lambda s: (at, 0, 0))

    mixed = pl.pallas_call(
        enc_mix_kernel,
        grid=(1,),
        in_specs=[SCALAR, full, gain] + [piece(8 + at) for at in range(5)],
        out_specs=full,
        out_shape=out,
        scratch_shapes=[pltpu.VMEM((NB_LEN, width), bf16)],
        compiler_params=params(),
    )(section, embedded, enc_norms[:1], *([pieces] * 5))
    inner = (embedded.astype(f32) + (mixed.astype(f32) + section_swap(mixed).astype(f32))).astype(
        bf16
    )
    fed = pl.pallas_call(
        enc_feed_kernel,
        grid=(1,),
        in_specs=[full, gain, pl.BlockSpec((8, ENC_D, width), lambda s: (0, 0, 0))],
        out_specs=full,
        out_shape=out,
        compiler_params=params(),
    )(inner, enc_norms[1:], pieces)
    return (inner.astype(f32) + (fed.astype(f32) + section_swap(fed).astype(f32))).astype(bf16)


def decoder_layer(core, states, prev, pairs, weights):
    norms, triple_w, out_w, query_w, back_w = weights
    triple = project(core, states, norms[0], triple_w, True)
    triple = lax.all_to_all(triple, "seq", 0, 0, tiled=True)
    mixed = lax.all_to_all(causal(triple), "seq", 0, 0, tiled=True)
    middle = (states.astype(f32) + product_sum(core, mixed, out_w)).astype(bf16)
    asked = project(core, middle, norms[1], query_w[None], False)
    crossed = cross(asked, prev, pairs)
    return (middle.astype(f32) + product_sum(core, crossed, back_w)).astype(bf16)


def on_device(
    hidden_states,
    neighbour_ids,
    neighbour_table,
    enc_embed,
    enc_norms,
    enc_qkv,
    enc_out,
    enc_up,
    enc_down,
    dec_norms,
    dec_qkv,
    dec_out,
    cross_query,
    cross_pair,
    cross_out,
):
    section = lax.axis_index("section").astype(jnp.int32)
    core_at = lax.axis_index("core").astype(jnp.int32)
    core = jnp.reshape(core_at, (1,))
    blocks_here = neighbour_table.shape[1]
    pieces = weight_pieces(section, enc_qkv, enc_out, enc_up, enc_down)
    slot_ids = neighbour_ids[neighbour_table.reshape(-1)]
    embedded = look_up(slot_ids, enc_embed, core_at, section)
    encoded = encode(embedded, enc_norms, pieces, jnp.reshape(section, (1,)))
    encoded = lax.all_gather(encoded, MP, axis=0, tiled=True)
    pairs = jnp.dot(
        encoded, cross_pair[0].reshape(ENC_D, 2 * WIDTH), preferred_element_type=f32
    ).astype(bf16)
    pairs = pairs.reshape(BATCH, blocks_here, KEYS, 2 * WIDTH)
    count = lax.axis_size("seq")
    prev = lax.ppermute(pairs[:, -1], "seq", [(i, i + 1) for i in range(count - 1)])
    weights = (
        dec_norms[0],
        jnp.transpose(dec_qkv[0], (1, 0, 2)),
        dec_out[0],
        cross_query[0],
        cross_out[0],
    )

    states = hidden_states.reshape(BATCH * ROWS, WIDTH)
    first = decoder_layer(core, states, prev, pairs, weights)
    second = decoder_layer(core, section_swap(first), prev, pairs, weights)
    second = second.reshape(BATCH, ROWS, WIDTH)
    return jnp.where(section == 0, section_swap(second[0]), second[1])[None]


def solution(mesh):
    devices = mesh.devices
    sections, seqs = devices.shape[:2]
    split = Mesh(
        devices.reshape(sections, seqs, 2, 4, 2), ("section", "seq", "z", "y", "core")
    )
    mp = ("z", "y", "core")
    return jax.shard_map(
        on_device,
        mesh=split,
        in_specs=(
            P(None, "seq", mp),
            P(),
            P(None, "seq", None),
            P(mp, None),
            P(),
            P(mp, None, None),
            P(mp, None),
            P(mp, None),
            P(mp, None),
            P("section", None, None),
            P("section", None, None, mp),
            P("section", mp, None),
            P("section", None, mp),
            P("section", None, None, mp),
            P("section", mp, None),
        ),
        out_specs=P("section", "seq", mp),
        check_vma=False,
    )
```

```python
import functools

import jax
import jax.numpy as jnp
import numpy as np
from jax import lax
from jax.experimental import pallas as pl
from jax.experimental.pallas import tpu as pltpu
from jax.sharding import Mesh, PartitionSpec as P

D = 4096
HEAD = 128
ENC_D = 1024
ENC_HEADS = 16
ENC_HEAD = 64
BLOCK = 64
NB_LEN = 128
NEIGH = 2
BATCH = 2
CHIPS = 8
ROWS = 256
WIDTH = 256
UNITS = 4
GROUP = 4
MP = ("z", "y", "core")
KEYS = NEIGH * NB_LEN
VMEM_LIMIT = 48 * 1024 * 1024

epsilon = 1e-05
f32 = jnp.float32
bf16 = jnp.bfloat16


def params():
    return pltpu.CompilerParams(vmem_limit_bytes=VMEM_LIMIT)


def whole(shape):
    return pl.BlockSpec(shape, lambda *_: (0,) * len(shape))


SCALAR = pl.BlockSpec(memory_space=pltpu.SMEM)


PARTS = (352, 160)
STARTS = (0, 352)
MASKS = (((4, 1, 3), (1, 3, 4)), ((3, 4, 1), (3, 4, 1)))


def block_offsets(masks):
    return [
        (masks[0] * (b & 1)) ^ (masks[1] * (b >> 1 & 1)) ^ (masks[2] * (b >> 2 & 1))
        for b in range(CHIPS)
    ]


OFFSETS = np.array([[block_offsets(m) for m in part] for part in MASKS], np.int32)
SLOTS = np.argsort(OFFSETS, axis=-1).astype(np.int32)


def core_swap(value):
    return lax.ppermute(value, "core", [(0, 1), (1, 0)])


def section_swap(value):
    return lax.ppermute(value, "section", [(0, 1), (1, 0)])


def chips_to_chips(value):
    return lax.all_to_all(value, ("z", "y"), 0, 0, tiled=True)


def neighbour(value, part, turn):
    route = [
        (2 * chip + core, 2 * (chip ^ MASKS[part][core][turn]) + core)
        for chip in range(CHIPS)
        for core in range(2)
    ]
    return lax.ppermute(value, MP, route)


def places(chip, pick):
    offsets = lax.dynamic_index_in_dim(jnp.asarray(OFFSETS), pick, 1, keepdims=False)
    slots = lax.dynamic_index_in_dim(jnp.asarray(SLOTS), pick, 1, keepdims=False)
    chips = chip ^ offsets
    blocks = jnp.take_along_axis(slots, jnp.arange(CHIPS)[None] ^ chip, axis=1)
    return jnp.concatenate(
        [jnp.reshape(pick, (1,)), chips.reshape(-1), blocks.reshape(-1)]
    ).astype(jnp.int32)


def gather_chips(local):
    near = []
    for part, value in enumerate(local):
        near.append(jnp.stack([value, neighbour(value, part, 0)]))
    near = [
        jnp.concatenate([value, neighbour(value, part, 1)]) for part, value in enumerate(near)
    ]
    far = [neighbour(value, part, 2) for part, value in enumerate(near)]
    return near + far


def scatter_sum(own, other):
    wide = [value.astype(f32) for value in own]
    got = [None] * 4
    for at in (2, 3, 0, 1):
        got[at] = core_swap(other[at]).astype(f32)
    sent = [neighbour((wide[2 + part] + got[2 + part]).astype(bf16), part, 2) for part in range(2)]
    result = []
    for part in range(2):
        low = wide[part] + got[part] + sent[part].astype(f32)
        second = neighbour(low[2:].astype(bf16), part, 1)
        low = low[:2] + second.astype(f32)
        third = neighbour(low[1].astype(bf16), part, 0)
        result.append(low[0] + third.astype(f32))
    return result


def project_kernel(last, units, place_ref, *refs):
    x_refs, (gain_ref, w_ref), refs = refs[:4], refs[4:6], refs[6:]
    if last:
        acc_in, sq_in, out_ref, sq_ref, left_ref = refs
    else:
        acc_ref, sq_ref, left_ref = refs
    step = pl.program_id(0)

    @pl.when(step == 0)
    def _():
        for part in range(2):
            rows = slice(STARTS[part], STARTS[part] + PARTS[part])
            total = sq_in[rows, :] if last else jnp.zeros((PARTS[part], 128), f32)
            for block in range(CHIPS):
                chip = place_ref[1 + part * CHIPS + block]
                wide = x_refs[part + 2 * (block // 4)][block % 4].astype(f32)
                squares = wide * wide
                total += squares[:, :128] + squares[:, 128:]
                cols = pl.ds(pl.multiple_of(chip * WIDTH, WIDTH), WIDTH)
                left_ref[rows, cols] = (wide * gain_ref[chip, 0]).astype(bf16)
            sq_ref[rows, :] = total

    right = w_ref[0].reshape(CHIPS * WIDTH, WIDTH)
    product = jnp.dot(left_ref[...], right, preferred_element_type=f32)
    if not last:
        acc_ref[0] = product
        return
    mean = jnp.sum(sq_ref[...], axis=1, keepdims=True) / D
    done = ((acc_in[0] + product) / jnp.sqrt(mean + epsilon)).astype(bf16)
    if units:
        for unit in range(UNITS):
            b, h = divmod(unit, 2)
            out_ref[unit, 0] = done[b * ROWS : (b + 1) * ROWS, h * HEAD : (h + 1) * HEAD]
    else:
        out_ref[...] = done


def project_half(place, rows, gains, weight, before, units):
    parts = weight.shape[0]
    count = BATCH * ROWS
    acc = (parts, count, WIDTH)
    sq = (count, 128)
    last = before is not None
    acc_spec = pl.BlockSpec((1, count, WIDTH), lambda s, place: (s, 0, 0))
    in_specs = [whole(value.shape) for value in rows] + [
        pl.BlockSpec((CHIPS, 1, 1, WIDTH), lambda s, place: (0, place[0], 0, 0)),
        pl.BlockSpec((1, CHIPS, 1, WIDTH, WIDTH), lambda s, place: (s, 0, place[0], 0, 0)),
    ]
    scratch = [pltpu.VMEM((count, CHIPS * WIDTH), bf16)]
    if last:
        in_specs += [acc_spec, whole(sq)]
        scratch = [pltpu.VMEM(sq, f32)] + scratch
        if units:
            out = (UNITS, parts, ROWS, HEAD)
            out_specs = pl.BlockSpec((UNITS, 1, ROWS, HEAD), lambda s, place: (0, s, 0, 0))
        else:
            out = (count, WIDTH)
            out_specs = whole(out)
        out_shape = jax.ShapeDtypeStruct(out, bf16)
    else:
        out_specs = [acc_spec, whole(sq)]
        out_shape = [jax.ShapeDtypeStruct(acc, f32), jax.ShapeDtypeStruct(sq, f32)]
    return pl.pallas_call(
        functools.partial(project_kernel, last, units),
        grid_spec=pltpu.PrefetchScalarGridSpec(
            num_scalar_prefetch=1,
            grid=(parts,),
            in_specs=in_specs,
            out_specs=out_specs,
            scratch_shapes=scratch,
        ),
        out_shape=out_shape,
        compiler_params=params(),
        cost_estimate=pl.CostEstimate(
            flops=2 * count * (D // 2) * WIDTH * parts,
            bytes_accessed=D * WIDTH * parts + D * count + 4 * count * WIDTH * parts,
            transcendentals=0,
        ),
    )(
        place,
        *rows,
        gains.reshape(CHIPS, 2, 1, WIDTH),
        weight.reshape(parts, CHIPS, 2, WIDTH, WIDTH),
        *(before or ()),
    )


def project(places_both, local, gains, weight, units):
    same = gather_chips(local)
    swap = [core_swap(value) for value in same]
    before = project_half(places_both[0], same, gains, weight, None, units)
    return project_half(places_both[1], swap, gains, weight, before, units)


def causal_kernel(triple_ref, out_ref):
    scaling = HEAD ** (-0.5)
    row = lax.broadcasted_iota(jnp.int32, (ROWS, ROWS), 0)
    col = lax.broadcasted_iota(jnp.int32, (ROWS, ROWS), 1)
    for i in range(UNITS):
        queries = triple_ref[i, 0]
        numer = jnp.zeros((ROWS, HEAD), f32)
        denom = jnp.zeros((ROWS, 1), f32)
        for j in range(i + 1):
            scores = lax.dot_general(
                queries, triple_ref[j, 1], (((1,), (1,)), ((), ())), preferred_element_type=f32
            )
            weights = jnp.exp(scores * scaling)
            if i == j:
                weights = jnp.where(col <= row, weights, 0.0)
            denom += jnp.sum(weights, axis=1, keepdims=True)
            numer += jnp.dot(weights.astype(bf16), triple_ref[j, 2], preferred_element_type=f32)
        out_ref[i] = (numer / denom).astype(bf16)


def causal(triple):
    out = (UNITS, ROWS, HEAD)
    return pl.pallas_call(
        causal_kernel,
        out_shape=jax.ShapeDtypeStruct(out, bf16),
        compiler_params=params(),
    )(triple)


def crossed_kernel(asked_ref, prev_ref, pairs_ref, out_ref):
    scaling = HEAD ** (-0.5)
    row = lax.broadcasted_iota(jnp.int32, (BLOCK, 2 * KEYS), 0)
    col = lax.broadcasted_iota(jnp.int32, (BLOCK, 2 * KEYS), 1)
    allowed = (row < BLOCK - 1) == (col < KEYS)
    for unit in range(UNITS):
        b, h = divmod(unit, 2)
        kcols = slice(h * HEAD, (h + 1) * HEAD)
        vcols = slice((2 + h) * HEAD, (3 + h) * HEAD)
        for i in range(ROWS // BLOCK):
            queries = asked_ref[b * ROWS + i * BLOCK : b * ROWS + (i + 1) * BLOCK, kcols]
            if i == 0:
                keys = jnp.concatenate([prev_ref[b, :, kcols], pairs_ref[b, 0, :, kcols]], axis=0)
                values = jnp.concatenate([prev_ref[b, :, vcols], pairs_ref[b, 0, :, vcols]], axis=0)
            else:
                keys = pairs_ref[b, i - 1 : i + 1, :, kcols].reshape(2 * KEYS, HEAD)
                values = pairs_ref[b, i - 1 : i + 1, :, vcols].reshape(2 * KEYS, HEAD)
            scores = lax.dot_general(
                queries, keys, (((1,), (1,)), ((), ())), preferred_element_type=f32
            )
            weights = jnp.where(allowed, jnp.exp(scores * scaling), 0.0)
            denom = jnp.sum(weights, axis=1, keepdims=True)
            numer = jnp.dot(weights.astype(bf16), values, preferred_element_type=f32)
            out_ref[unit, i * BLOCK : (i + 1) * BLOCK, :] = (numer / denom).astype(bf16)


def cross(asked, prev, pairs):
    out = (UNITS, ROWS, HEAD)
    return pl.pallas_call(
        crossed_kernel,
        out_shape=jax.ShapeDtypeStruct(out, bf16),
        compiler_params=params(),
    )(asked, prev, pairs)


def terms_kernel(place_ref, mixed_ref, *refs):
    w_refs, out_refs, left_ref = refs[:GROUP], refs[GROUP : GROUP + 4], refs[-1]
    step = pl.program_id(0)

    @pl.when(step == 0)
    def _():
        for unit in range(UNITS):
            b, h = divmod(unit, 2)
            left_ref[b * ROWS : (b + 1) * ROWS, h * HEAD : (h + 1) * HEAD] = mixed_ref[unit]

    for at, w_ref in enumerate(w_refs):
        product = jnp.dot(left_ref[...], w_ref[...], preferred_element_type=f32).astype(bf16)
        chip = step * GROUP + at
        for part in range(2):
            block = place_ref[1 + (2 + part) * CHIPS + chip]
            value = product[STARTS[part] : STARTS[part] + PARTS[part], :]

            @pl.when(block < 4)
            def _():
                out_refs[part][block] = value

            @pl.when(block >= 4)
            def _():
                out_refs[2 + part][block - 4] = value


def terms(place, mixed, weight):
    count = BATCH * ROWS

    def columns(at):
        return pl.BlockSpec((WIDTH, WIDTH), lambda s, place: (0, 2 * (GROUP * s + at) + place[0]))

    shapes = [(4, PARTS[at % 2], WIDTH) for at in range(4)]
    return pl.pallas_call(
        terms_kernel,
        grid_spec=pltpu.PrefetchScalarGridSpec(
            num_scalar_prefetch=1,
            grid=(CHIPS // GROUP,),
            in_specs=[whole((UNITS, ROWS, HEAD))] + [columns(at) for at in range(GROUP)],
            out_specs=[whole(shape) for shape in shapes],
            scratch_shapes=[pltpu.VMEM((count, WIDTH), bf16)],
        ),
        out_shape=[jax.ShapeDtypeStruct(shape, bf16) for shape in shapes],
        compiler_params=params(),
        cost_estimate=pl.CostEstimate(
            flops=2 * count * WIDTH * D // 2,
            bytes_accessed=D * WIDTH + D * count,
            transcendentals=0,
        ),
    )(place, mixed, *([weight] * GROUP))


def add_product(places_both, states, mixed, weight):
    other = terms(places_both[1], mixed, weight)
    own = terms(places_both[0], mixed, weight)
    return [
        (state.astype(f32) + total).astype(bf16)
        for state, total in zip(states, scatter_sum(own, other))
    ]


def by_parts(rows):
    return [rows[start : start + count] for start, count in zip(STARTS, PARTS)]


def look_up(ids, enc_embed, core, section):
    vocab_here = enc_embed.shape[0]
    mine = lax.dynamic_slice_in_dim(ids, section * (NB_LEN // 2), NB_LEN // 2, axis=1)
    wanted = mine.reshape(CHIPS, 2, NB_LEN // 2) - lax.axis_index(MP) * vocab_here

    def rows(at):
        picks = lax.dynamic_index_in_dim(wanted, at, 1, keepdims=False).reshape(-1)
        inside = (picks >= 0) & (picks < vocab_here)
        found = enc_embed[jnp.clip(picks, 0, vocab_here - 1)]
        found = jnp.where(inside[:, None], found, jnp.zeros((), bf16))
        return found.reshape(CHIPS, NB_LEN // 2, ENC_D)

    paired = core_swap(rows(1 - core)) + rows(core)
    half = jnp.sum(chips_to_chips(paired).astype(f32), axis=0).astype(bf16)
    far = section_swap(half)
    return jnp.where(
        section == 0, jnp.concatenate([half, far], axis=0), jnp.concatenate([far, half], axis=0)
    )


def weight_pieces(section, enc_qkv, enc_out, enc_up, enc_down):
    width = ENC_D // 2
    triple = lax.dynamic_slice_in_dim(enc_qkv, section * width, width, axis=2)
    up = enc_up.reshape(64, 16, 2, 2, 64)
    up = lax.dynamic_index_in_dim(up, section, 2, keepdims=False)
    up = jnp.transpose(up, (2, 0, 1, 3)).reshape(2, 64, 2, width)
    down = lax.dynamic_slice_in_dim(enc_down, section * 128, 128, axis=0)
    down = down.reshape(2, 64, 2, width)
    local = jnp.concatenate(
        [
            jnp.transpose(up, (0, 2, 1, 3)).reshape(4, 64, width),
            jnp.transpose(down, (0, 2, 1, 3)).reshape(4, 64, width),
            jnp.transpose(triple, (1, 0, 2)),
            jnp.transpose(enc_out.reshape(64, 2, width), (1, 0, 2)),
        ],
        axis=0,
    )
    return lax.all_gather(local, MP, axis=1, tiled=True)


def scaled_rows(values, gain):
    wide = values.astype(f32)
    root = jnp.sqrt(jnp.mean(wide * wide, axis=1, keepdims=True) + epsilon)
    return (wide * gain).astype(bf16), root


def enc_mix_kernel(section_ref, x_ref, gain_ref, q_ref, k_ref, v_ref, o0_ref, o1_ref, out_ref, mix_ref):
    scaled, root = scaled_rows(x_ref[...], gain_ref[...])
    triple = [
        (jnp.dot(scaled, ref[0], preferred_element_type=f32) / root).astype(bf16)
        for ref in (q_ref, k_ref, v_ref)
    ]
    for head in range(ENC_HEADS // 2):
        cols = slice(head * ENC_HEAD, (head + 1) * ENC_HEAD)
        scores = lax.dot_general(
            triple[0][:, cols],
            triple[1][:, cols],
            (((1,), (1,)), ((), ())),
            preferred_element_type=f32,
        )
        weights = jnp.exp(scores * ENC_HEAD ** (-0.5))
        denom = jnp.sum(weights, axis=1, keepdims=True)
        numer = jnp.dot(weights.astype(bf16), triple[2][:, cols], preferred_element_type=f32)
        mix_ref[:, cols] = (numer / denom).astype(bf16)
    mixed = mix_ref[...]
    width = ENC_D // 2
    rows = pl.ds(pl.multiple_of(section_ref[0] * width, width), width)
    for at, ref in enumerate((o0_ref, o1_ref)):
        part = jnp.dot(mixed, ref[0, rows, :], preferred_element_type=f32)
        out_ref[:, at * width : (at + 1) * width] = part.astype(bf16)


def enc_feed_kernel(x_ref, gain_ref, w_ref, out_ref):
    scaled, root = scaled_rows(x_ref[...], gain_ref[...])
    width = ENC_D // 2
    hidden = [
        jax.nn.gelu(
            jnp.dot(scaled, w_ref[piece], preferred_element_type=f32) / root, approximate=True
        ).astype(bf16)
        for piece in range(4)
    ]
    for at in range(2):
        part = jnp.zeros((NB_LEN, width), f32)
        for piece in range(4):
            rows = slice((piece % 2) * width, (piece % 2 + 1) * width)
            down = w_ref[4 + 2 * (piece // 2) + at, rows, :]
            part += jnp.dot(hidden[piece], down, preferred_element_type=f32)
        out_ref[:, at * width : (at + 1) * width] = part.astype(bf16)


def encode(embedded, enc_norms, pieces, section):
    out = jax.ShapeDtypeStruct((NB_LEN, ENC_D), bf16)
    width = ENC_D // 2
    full = whole((NB_LEN, ENC_D))
    gain = whole((1, ENC_D))

    def piece(at):
        return pl.BlockSpec((1, ENC_D, width), lambda s: (at, 0, 0))

    mixed = pl.pallas_call(
        enc_mix_kernel,
        grid=(1,),
        in_specs=[SCALAR, full, gain] + [piece(8 + at) for at in range(5)],
        out_specs=full,
        out_shape=out,
        scratch_shapes=[pltpu.VMEM((NB_LEN, width), bf16)],
        compiler_params=params(),
    )(section, embedded, enc_norms[:1], *([pieces] * 5))
    inner = (embedded.astype(f32) + (mixed.astype(f32) + section_swap(mixed).astype(f32))).astype(
        bf16
    )
    fed = pl.pallas_call(
        enc_feed_kernel,
        grid=(1,),
        in_specs=[full, gain, pl.BlockSpec((8, ENC_D, width), lambda s: (0, 0, 0))],
        out_specs=full,
        out_shape=out,
        compiler_params=params(),
    )(inner, enc_norms[1:], pieces)
    return (inner.astype(f32) + (fed.astype(f32) + section_swap(fed).astype(f32))).astype(bf16)


def after(value, other):
    return lax.optimization_barrier((value, other))[0]


def decoder_layer(places_both, states, make_pairs, weights):
    norms, triple_w, out_w, query_w, back_w = weights
    triple = project(places_both, states, norms[0], triple_w, True)
    triple = lax.all_to_all(triple, "seq", 0, 0, tiled=True)
    mixed = lax.all_to_all(causal(triple), "seq", 0, 0, tiled=True)
    middle = add_product(places_both, states, mixed, out_w)
    asked = project(places_both, middle, norms[1], query_w[None], False)
    crossed = cross(asked, *make_pairs(mixed))
    return add_product(places_both, middle, crossed, back_w)


def on_device(
    hidden_states,
    neighbour_ids,
    neighbour_table,
    enc_embed,
    enc_norms,
    enc_qkv,
    enc_out,
    enc_up,
    enc_down,
    dec_norms,
    dec_qkv,
    dec_out,
    cross_query,
    cross_pair,
    cross_out,
):
    section = lax.axis_index("section").astype(jnp.int32)
    core_at = lax.axis_index("core").astype(jnp.int32)
    chip = lax.axis_index(("z", "y")).astype(jnp.int32)
    places_both = [places(chip, core_at), places(chip, 1 - core_at)]
    blocks_here = neighbour_table.shape[1]
    pieces = weight_pieces(section, enc_qkv, enc_out, enc_up, enc_down)
    slot_ids = neighbour_ids[neighbour_table.reshape(-1)]
    embedded = look_up(slot_ids, enc_embed, core_at, section)
    count = lax.axis_size("seq")

    def make_pairs(mixed):
        ready = after(embedded, mixed[0, 0, :1])
        encoded = encode(ready, enc_norms, pieces, jnp.reshape(section, (1,)))
        encoded = lax.all_gather(encoded, MP, axis=0, tiled=True)
        pairs = jnp.dot(
            encoded, cross_pair[0].reshape(ENC_D, 2 * WIDTH), preferred_element_type=f32
        ).astype(bf16)
        pairs = pairs.reshape(BATCH, blocks_here, KEYS, 2 * WIDTH)
        prev = lax.ppermute(pairs[:, -1], "seq", [(i, i + 1) for i in range(count - 1)])
        return prev, pairs

    made = []

    def once(mixed):
        if not made:
            made.append(make_pairs(mixed))
        return made[0]

    weights = (
        dec_norms[0],
        jnp.transpose(dec_qkv[0], (1, 0, 2)),
        dec_out[0],
        cross_query[0],
        cross_out[0],
    )

    states = hidden_states.reshape(BATCH * ROWS, WIDTH)
    first = decoder_layer(places_both, by_parts(states), once, weights)
    handed = section_swap(jnp.concatenate(first))
    second = jnp.concatenate(decoder_layer(places_both, by_parts(handed), once, weights))
    second = second.reshape(BATCH, ROWS, WIDTH)
    return jnp.where(section == 0, section_swap(second[0]), second[1])[None]


def solution(mesh):
    devices = mesh.devices
    sections, seqs = devices.shape[:2]
    split = Mesh(
        devices.reshape(sections, seqs, 2, 4, 2), ("section", "seq", "z", "y", "core")
    )
    mp = ("z", "y", "core")
    return jax.shard_map(
        on_device,
        mesh=split,
        in_specs=(
            P(None, "seq", mp),
            P(),
            P(None, "seq", None),
            P(mp, None),
            P(),
            P(mp, None, None),
            P(mp, None),
            P(mp, None),
            P(mp, None),
            P("section", None, None),
            P("section", None, None, mp),
            P("section", mp, None),
            P("section", None, mp),
            P("section", None, None, mp),
            P("section", mp, None),
        ),
        out_specs=P("section", "seq", mp),
        check_vma=False,
    )
```

```python
import functools

import jax
import jax.numpy as jnp
import numpy as np
from jax import lax
from jax.experimental import pallas as pl
from jax.experimental.pallas import tpu as pltpu
from jax.sharding import Mesh, PartitionSpec as P

D = 4096
HEAD = 128
ENC_D = 1024
ENC_HEADS = 16
ENC_HEAD = 64
BLOCK = 64
NB_LEN = 128
NEIGH = 2
BATCH = 2
CHIPS = 8
ROWS = 256
WIDTH = 256
UNITS = 4
GROUP = 4
MP = ("z", "y", "core")
KEYS = NEIGH * NB_LEN

epsilon = 1e-05
f32 = jnp.float32
bf16 = jnp.bfloat16


def params(mebibytes=16):
    return pltpu.CompilerParams(vmem_limit_bytes=mebibytes * 1024 * 1024)


def whole(shape):
    return pl.BlockSpec(shape, lambda *_: (0,) * len(shape))


SCALAR = pl.BlockSpec(memory_space=pltpu.SMEM)


PARTS = (352, 160)
STARTS = (0, 352)
MASKS = (((4, 1, 3), (1, 3, 4)), ((3, 4, 1), (3, 4, 1)))


def block_offsets(masks):
    return [
        (masks[0] * (b & 1)) ^ (masks[1] * (b >> 1 & 1)) ^ (masks[2] * (b >> 2 & 1))
        for b in range(CHIPS)
    ]


OFFSETS = np.array([[block_offsets(m) for m in part] for part in MASKS], np.int32)
SLOTS = np.argsort(OFFSETS, axis=-1).astype(np.int32)


def core_swap(value):
    return lax.ppermute(value, "core", [(0, 1), (1, 0)])


def section_swap(value):
    return lax.ppermute(value, "section", [(0, 1), (1, 0)])


def chips_to_chips(value):
    return lax.all_to_all(value, ("z", "y"), 0, 0, tiled=True)


def neighbour(value, part, turn):
    route = [
        (2 * chip + core, 2 * (chip ^ MASKS[part][core][turn]) + core)
        for chip in range(CHIPS)
        for core in range(2)
    ]
    return lax.ppermute(value, MP, route)


def places(chip, pick):
    offsets = lax.dynamic_index_in_dim(jnp.asarray(OFFSETS), pick, 1, keepdims=False)
    slots = lax.dynamic_index_in_dim(jnp.asarray(SLOTS), pick, 1, keepdims=False)
    chips = chip ^ offsets
    blocks = jnp.take_along_axis(slots, jnp.arange(CHIPS)[None] ^ chip, axis=1)
    return jnp.concatenate(
        [jnp.reshape(pick, (1,)), chips.reshape(-1), blocks.reshape(-1)]
    ).astype(jnp.int32)


def together(*values):
    return lax.optimization_barrier(values)


def gather_chips(local):
    got = together(*[neighbour(value, part, 0) for part, value in enumerate(local)])
    near = [jnp.stack([value, other]) for value, other in zip(local, got)]
    got = together(*[neighbour(value, part, 1) for part, value in enumerate(near)])
    near = [jnp.concatenate([value, other]) for value, other in zip(near, got)]
    far = together(*[neighbour(value, part, 2) for part, value in enumerate(near)])
    return near + list(far)


def scatter_sum(own, other):
    wide = [value.astype(f32) for value in own]
    far = together(core_swap(other[2]), core_swap(other[3]))
    near = [core_swap(other[0]), core_swap(other[1])]
    sums = [(wide[2 + part] + far[part].astype(f32)).astype(bf16) for part in range(2)]
    got = together(*[neighbour(sums[part], part, 2) for part in range(2)], *near)
    low = [
        wide[part] + got[2 + part].astype(f32) + got[part].astype(f32) for part in range(2)
    ]
    got = together(*[neighbour(low[part][2:].astype(bf16), part, 1) for part in range(2)])
    low = [low[part][:2] + got[part].astype(f32) for part in range(2)]
    got = together(*[neighbour(low[part][1].astype(bf16), part, 0) for part in range(2)])
    return [low[part][0] + got[part].astype(f32) for part in range(2)]


def project_kernel(last, units, place_ref, *refs):
    x_refs, (gain_ref, w_ref), refs = refs[:4], refs[4:6], refs[6:]
    if last:
        acc_in, sq_in, out_ref, sq_ref, left_ref = refs
    else:
        acc_ref, sq_ref, left_ref = refs
    step = pl.program_id(0)

    @pl.when(step == 0)
    def _():
        for part in range(2):
            rows = slice(STARTS[part], STARTS[part] + PARTS[part])
            total = sq_in[rows, :] if last else jnp.zeros((PARTS[part], 128), f32)
            for block in range(CHIPS):
                chip = place_ref[1 + part * CHIPS + block]
                wide = x_refs[part + 2 * (block // 4)][block % 4].astype(f32)
                squares = wide * wide
                total += squares[:, :128] + squares[:, 128:]
                cols = pl.ds(pl.multiple_of(chip * WIDTH, WIDTH), WIDTH)
                left_ref[rows, cols] = (wide * gain_ref[chip, 0]).astype(bf16)
            sq_ref[rows, :] = total

    right = w_ref[0].reshape(CHIPS * WIDTH, WIDTH)
    product = jnp.dot(left_ref[...], right, preferred_element_type=f32)
    if not last:
        acc_ref[0] = product
        return
    mean = jnp.sum(sq_ref[...], axis=1, keepdims=True) / D
    done = ((acc_in[0] + product) / jnp.sqrt(mean + epsilon)).astype(bf16)
    if units:
        for unit in range(UNITS):
            b, h = divmod(unit, 2)
            out_ref[unit, 0] = done[b * ROWS : (b + 1) * ROWS, h * HEAD : (h + 1) * HEAD]
    else:
        out_ref[...] = done


def project_half(place, rows, gains, weight, before, units):
    parts = weight.shape[0]
    count = BATCH * ROWS
    acc = (parts, count, WIDTH)
    sq = (count, 128)
    last = before is not None
    acc_spec = pl.BlockSpec((1, count, WIDTH), lambda s, place: (s, 0, 0))
    in_specs = [whole(value.shape) for value in rows] + [
        pl.BlockSpec((CHIPS, 1, 1, WIDTH), lambda s, place: (0, place[0], 0, 0)),
        pl.BlockSpec((1, CHIPS, 1, WIDTH, WIDTH), lambda s, place: (s, 0, place[0], 0, 0)),
    ]
    scratch = [pltpu.VMEM((count, CHIPS * WIDTH), bf16)]
    if last:
        in_specs += [acc_spec, whole(sq)]
        scratch = [pltpu.VMEM(sq, f32)] + scratch
        if units:
            out = (UNITS, parts, ROWS, HEAD)
            out_specs = pl.BlockSpec((UNITS, 1, ROWS, HEAD), lambda s, place: (0, s, 0, 0))
        else:
            out = (count, WIDTH)
            out_specs = whole(out)
        out_shape = jax.ShapeDtypeStruct(out, bf16)
    else:
        out_specs = [acc_spec, whole(sq)]
        out_shape = [jax.ShapeDtypeStruct(acc, f32), jax.ShapeDtypeStruct(sq, f32)]
    return pl.pallas_call(
        functools.partial(project_kernel, last, units),
        grid_spec=pltpu.PrefetchScalarGridSpec(
            num_scalar_prefetch=1,
            grid=(parts,),
            in_specs=in_specs,
            out_specs=out_specs,
            scratch_shapes=scratch,
        ),
        out_shape=out_shape,
        compiler_params=params(),
        cost_estimate=pl.CostEstimate(
            flops=2 * count * (D // 2) * WIDTH * parts,
            bytes_accessed=D * WIDTH * parts + D * count + 4 * count * WIDTH * parts,
            transcendentals=0,
        ),
    )(
        place,
        *rows,
        gains.reshape(CHIPS, 2, 1, WIDTH),
        weight.reshape(parts, CHIPS, 2, WIDTH, WIDTH),
        *(before or ()),
    )


def project(places_both, local, gains, weight, units):
    same = gather_chips(local)
    swap = [core_swap(value) for value in same]
    before = project_half(places_both[0], same, gains, weight, None, units)
    return project_half(places_both[1], swap, gains, weight, before, units)


def causal_kernel(triple_ref, out_ref):
    scaling = HEAD ** (-0.5)
    row = lax.broadcasted_iota(jnp.int32, (ROWS, ROWS), 0)
    col = lax.broadcasted_iota(jnp.int32, (ROWS, ROWS), 1)
    for i in range(UNITS):
        queries = triple_ref[i, 0]
        numer = jnp.zeros((ROWS, HEAD), f32)
        denom = jnp.zeros((ROWS, 1), f32)
        for j in range(i + 1):
            scores = lax.dot_general(
                queries, triple_ref[j, 1], (((1,), (1,)), ((), ())), preferred_element_type=f32
            )
            weights = jnp.exp(scores * scaling)
            if i == j:
                weights = jnp.where(col <= row, weights, 0.0)
            denom += jnp.sum(weights, axis=1, keepdims=True)
            numer += jnp.dot(weights.astype(bf16), triple_ref[j, 2], preferred_element_type=f32)
        out_ref[i] = (numer / denom).astype(bf16)


def causal(triple):
    out = (UNITS, ROWS, HEAD)
    return pl.pallas_call(
        causal_kernel,
        out_shape=jax.ShapeDtypeStruct(out, bf16),
        compiler_params=params(),
    )(triple)


def crossed_kernel(asked_ref, prev_ref, pairs_ref, out_ref):
    scaling = HEAD ** (-0.5)
    row = lax.broadcasted_iota(jnp.int32, (BLOCK, 2 * KEYS), 0)
    col = lax.broadcasted_iota(jnp.int32, (BLOCK, 2 * KEYS), 1)
    allowed = (row < BLOCK - 1) == (col < KEYS)
    for unit in range(UNITS):
        b, h = divmod(unit, 2)
        kcols = slice(h * HEAD, (h + 1) * HEAD)
        vcols = slice((2 + h) * HEAD, (3 + h) * HEAD)
        for i in range(ROWS // BLOCK):
            queries = asked_ref[b * ROWS + i * BLOCK : b * ROWS + (i + 1) * BLOCK, kcols]
            if i == 0:
                keys = jnp.concatenate([prev_ref[b, :, kcols], pairs_ref[b, 0, :, kcols]], axis=0)
                values = jnp.concatenate([prev_ref[b, :, vcols], pairs_ref[b, 0, :, vcols]], axis=0)
            else:
                keys = pairs_ref[b, i - 1 : i + 1, :, kcols].reshape(2 * KEYS, HEAD)
                values = pairs_ref[b, i - 1 : i + 1, :, vcols].reshape(2 * KEYS, HEAD)
            scores = lax.dot_general(
                queries, keys, (((1,), (1,)), ((), ())), preferred_element_type=f32
            )
            weights = jnp.where(allowed, jnp.exp(scores * scaling), 0.0)
            denom = jnp.sum(weights, axis=1, keepdims=True)
            numer = jnp.dot(weights.astype(bf16), values, preferred_element_type=f32)
            out_ref[unit, i * BLOCK : (i + 1) * BLOCK, :] = (numer / denom).astype(bf16)


def cross(asked, prev, pairs):
    out = (UNITS, ROWS, HEAD)
    return pl.pallas_call(
        crossed_kernel,
        out_shape=jax.ShapeDtypeStruct(out, bf16),
        compiler_params=params(),
    )(asked, prev, pairs)


def terms_kernel(place_ref, mixed_ref, *refs):
    w_refs, out_refs, left_ref = refs[:GROUP], refs[GROUP : GROUP + 4], refs[-1]
    step = pl.program_id(0)

    @pl.when(step == 0)
    def _():
        for unit in range(UNITS):
            b, h = divmod(unit, 2)
            left_ref[b * ROWS : (b + 1) * ROWS, h * HEAD : (h + 1) * HEAD] = mixed_ref[unit]

    for at, w_ref in enumerate(w_refs):
        product = jnp.dot(left_ref[...], w_ref[...], preferred_element_type=f32).astype(bf16)
        chip = step * GROUP + at
        for part in range(2):
            block = place_ref[1 + (2 + part) * CHIPS + chip]
            value = product[STARTS[part] : STARTS[part] + PARTS[part], :]

            @pl.when(block < 4)
            def _():
                out_refs[part][block] = value

            @pl.when(block >= 4)
            def _():
                out_refs[2 + part][block - 4] = value


def terms(place, mixed, weight):
    count = BATCH * ROWS

    def columns(at):
        return pl.BlockSpec((WIDTH, WIDTH), lambda s, place: (0, 2 * (GROUP * s + at) + place[0]))

    shapes = [(4, PARTS[at % 2], WIDTH) for at in range(4)]
    return pl.pallas_call(
        terms_kernel,
        grid_spec=pltpu.PrefetchScalarGridSpec(
            num_scalar_prefetch=1,
            grid=(CHIPS // GROUP,),
            in_specs=[whole((UNITS, ROWS, HEAD))] + [columns(at) for at in range(GROUP)],
            out_specs=[whole(shape) for shape in shapes],
            scratch_shapes=[pltpu.VMEM((count, WIDTH), bf16)],
        ),
        out_shape=[jax.ShapeDtypeStruct(shape, bf16) for shape in shapes],
        compiler_params=params(),
        cost_estimate=pl.CostEstimate(
            flops=2 * count * WIDTH * D // 2,
            bytes_accessed=D * WIDTH + D * count,
            transcendentals=0,
        ),
    )(place, mixed, *([weight] * GROUP))


def add_product(places_both, states, mixed, weight):
    other = terms(places_both[1], mixed, weight)
    own = terms(places_both[0], mixed, weight)
    return [
        (state.astype(f32) + total).astype(bf16)
        for state, total in zip(states, scatter_sum(own, other))
    ]


def by_parts(rows):
    return [rows[start : start + count] for start, count in zip(STARTS, PARTS)]


def look_up(ids, enc_embed, core, section):
    vocab_here = enc_embed.shape[0]
    mine = lax.dynamic_slice_in_dim(ids, section * (NB_LEN // 2), NB_LEN // 2, axis=1)
    wanted = mine.reshape(CHIPS, 2, NB_LEN // 2) - lax.axis_index(MP) * vocab_here

    def rows(at):
        picks = lax.dynamic_index_in_dim(wanted, at, 1, keepdims=False).reshape(-1)
        inside = (picks >= 0) & (picks < vocab_here)
        found = enc_embed[jnp.clip(picks, 0, vocab_here - 1)]
        found = jnp.where(inside[:, None], found, jnp.zeros((), bf16))
        return found.reshape(CHIPS, NB_LEN // 2, ENC_D)

    paired = core_swap(rows(1 - core)) + rows(core)
    return jnp.sum(chips_to_chips(paired).astype(f32), axis=0).astype(bf16)


def join_halves(half, section):
    far = section_swap(half)
    return jnp.where(
        section == 0, jnp.concatenate([half, far], axis=0), jnp.concatenate([far, half], axis=0)
    )


def weight_pieces(section, enc_qkv, enc_out, enc_up, enc_down):
    width = ENC_D // 2
    triple = lax.dynamic_slice_in_dim(enc_qkv, section * width, width, axis=2)
    up = enc_up.reshape(64, 16, 2, 2, 64)
    up = lax.dynamic_index_in_dim(up, section, 2, keepdims=False)
    up = jnp.transpose(up, (2, 0, 1, 3)).reshape(2, 64, 2, width)
    down = lax.dynamic_slice_in_dim(enc_down, section * 128, 128, axis=0)
    down = down.reshape(2, 64, 2, width)
    local = jnp.concatenate(
        [
            jnp.transpose(up, (0, 2, 1, 3)).reshape(4, 64, width),
            jnp.transpose(down, (0, 2, 1, 3)).reshape(4, 64, width),
            jnp.transpose(triple, (1, 0, 2)),
            jnp.transpose(enc_out.reshape(64, 2, width), (1, 0, 2)),
        ],
        axis=0,
    )
    return lax.all_gather(local, MP, axis=1, tiled=True)


def scaled_rows(values, gain):
    wide = values.astype(f32)
    root = jnp.sqrt(jnp.mean(wide * wide, axis=1, keepdims=True) + epsilon)
    return (wide * gain).astype(bf16), root


def enc_mix_kernel(section_ref, x_ref, gain_ref, q_ref, k_ref, v_ref, o0_ref, o1_ref, out_ref, mix_ref):
    scaled, root = scaled_rows(x_ref[...], gain_ref[...])
    triple = [
        (jnp.dot(scaled, ref[0], preferred_element_type=f32) / root).astype(bf16)
        for ref in (q_ref, k_ref, v_ref)
    ]
    for head in range(ENC_HEADS // 2):
        cols = slice(head * ENC_HEAD, (head + 1) * ENC_HEAD)
        scores = lax.dot_general(
            triple[0][:, cols],
            triple[1][:, cols],
            (((1,), (1,)), ((), ())),
            preferred_element_type=f32,
        )
        weights = jnp.exp(scores * ENC_HEAD ** (-0.5))
        denom = jnp.sum(weights, axis=1, keepdims=True)
        numer = jnp.dot(weights.astype(bf16), triple[2][:, cols], preferred_element_type=f32)
        mix_ref[:, cols] = (numer / denom).astype(bf16)
    mixed = mix_ref[...]
    width = ENC_D // 2
    rows = pl.ds(pl.multiple_of(section_ref[0] * width, width), width)
    for at, ref in enumerate((o0_ref, o1_ref)):
        part = jnp.dot(mixed, ref[0, rows, :], preferred_element_type=f32)
        out_ref[:, at * width : (at + 1) * width] = part.astype(bf16)


def enc_feed_kernel(x_ref, gain_ref, w_ref, out_ref):
    scaled, root = scaled_rows(x_ref[...], gain_ref[...])
    width = ENC_D // 2
    hidden = [
        jax.nn.gelu(
            jnp.dot(scaled, w_ref[piece], preferred_element_type=f32) / root, approximate=True
        ).astype(bf16)
        for piece in range(4)
    ]
    for at in range(2):
        part = jnp.zeros((NB_LEN, width), f32)
        for piece in range(4):
            rows = slice((piece % 2) * width, (piece % 2 + 1) * width)
            down = w_ref[4 + 2 * (piece // 2) + at, rows, :]
            part += jnp.dot(hidden[piece], down, preferred_element_type=f32)
        out_ref[:, at * width : (at + 1) * width] = part.astype(bf16)


def encode(embedded, enc_norms, pieces, section):
    out = jax.ShapeDtypeStruct((NB_LEN, ENC_D), bf16)
    width = ENC_D // 2
    full = whole((NB_LEN, ENC_D))
    gain = whole((1, ENC_D))

    def piece(at):
        return pl.BlockSpec((1, ENC_D, width), lambda s: (at, 0, 0))

    mixed = pl.pallas_call(
        enc_mix_kernel,
        grid=(1,),
        in_specs=[SCALAR, full, gain] + [piece(8 + at) for at in range(5)],
        out_specs=full,
        out_shape=out,
        scratch_shapes=[pltpu.VMEM((NB_LEN, width), bf16)],
        compiler_params=params(),
    )(section, embedded, enc_norms[:1], *([pieces] * 5))
    inner = (embedded.astype(f32) + (mixed.astype(f32) + section_swap(mixed).astype(f32))).astype(
        bf16
    )
    fed = pl.pallas_call(
        enc_feed_kernel,
        grid=(1,),
        in_specs=[full, gain, pl.BlockSpec((8, ENC_D, width), lambda s: (0, 0, 0))],
        out_specs=full,
        out_shape=out,
        compiler_params=params(28),
    )(inner, enc_norms[1:], pieces)
    return (inner.astype(f32) + (fed.astype(f32) + section_swap(fed).astype(f32))).astype(bf16)


def decoder_layer(places_both, states, looked_up, make_pairs, weights):
    norms, triple_w, out_w, query_w, back_w = weights
    triple = project(places_both, states, norms[0], triple_w, True)
    looked_up, embedded = looked_up
    if looked_up is not None:
        triple, half = together(triple, looked_up)
        embedded = embedded(half)
    triple = lax.all_to_all(triple, "seq", 0, 0, tiled=True)
    mixed = lax.all_to_all(causal(triple), "seq", 0, 0, tiled=True)
    if looked_up is not None:
        mixed, embedded = together(mixed, embedded)
    prev, pairs = make_pairs(embedded)
    middle = add_product(places_both, states, mixed, out_w)
    asked = project(places_both, middle, norms[1], query_w[None], False)
    crossed = cross(asked, prev, pairs)
    return add_product(places_both, middle, crossed, back_w), (prev, pairs)


def on_device(
    hidden_states,
    neighbour_ids,
    neighbour_table,
    enc_embed,
    enc_norms,
    enc_qkv,
    enc_out,
    enc_up,
    enc_down,
    dec_norms,
    dec_qkv,
    dec_out,
    cross_query,
    cross_pair,
    cross_out,
):
    section = lax.axis_index("section").astype(jnp.int32)
    core_at = lax.axis_index("core").astype(jnp.int32)
    chip = lax.axis_index(("z", "y")).astype(jnp.int32)
    places_both = [places(chip, core_at), places(chip, 1 - core_at)]
    blocks_here = neighbour_table.shape[1]
    pieces = weight_pieces(section, enc_qkv, enc_out, enc_up, enc_down)
    slot_ids = neighbour_ids[neighbour_table.reshape(-1)]
    half = look_up(slot_ids, enc_embed, core_at, section)
    count = lax.axis_size("seq")
    pair_w = cross_pair[0].reshape(ENC_D, 2 * WIDTH)

    def pair_rows(rows):
        return jnp.dot(rows, pair_w, preferred_element_type=f32).astype(bf16)

    def make_pairs(embedded):
        encoded = encode(embedded, enc_norms, pieces, jnp.reshape(section, (1,)))
        encoded = lax.all_gather(encoded, MP, axis=0, tiled=True)
        edge = encoded.reshape(BATCH, blocks_here, KEYS, ENC_D)[:, -1]
        edge = pair_rows(edge.reshape(BATCH * KEYS, ENC_D)).reshape(BATCH, KEYS, 2 * WIDTH)
        prev = lax.ppermute(edge, "seq", [(i, i + 1) for i in range(count - 1)])
        return prev, pair_rows(encoded).reshape(BATCH, blocks_here, KEYS, 2 * WIDTH)

    weights = (
        dec_norms[0],
        jnp.transpose(dec_qkv[0], (1, 0, 2)),
        dec_out[0],
        cross_query[0],
        cross_out[0],
    )

    states = hidden_states.reshape(BATCH * ROWS, WIDTH)
    first, pairs = decoder_layer(
        places_both,
        by_parts(states),
        (half, lambda half: join_halves(half, section)),
        make_pairs,
        weights,
    )
    handed = section_swap(jnp.concatenate(first))
    second, _ = decoder_layer(
        places_both, by_parts(handed), (None, None), lambda _: pairs, weights
    )
    second = jnp.concatenate(second)
    second = second.reshape(BATCH, ROWS, WIDTH)
    return jnp.where(section == 0, section_swap(second[0]), second[1])[None]


def solution(mesh):
    devices = mesh.devices
    sections, seqs = devices.shape[:2]
    split = Mesh(
        devices.reshape(sections, seqs, 2, 4, 2), ("section", "seq", "z", "y", "core")
    )
    mp = ("z", "y", "core")
    return jax.shard_map(
        on_device,
        mesh=split,
        in_specs=(
            P(None, "seq", mp),
            P(),
            P(None, "seq", None),
            P(mp, None),
            P(),
            P(mp, None, None),
            P(mp, None),
            P(mp, None),
            P(mp, None),
            P("section", None, None),
            P("section", None, None, mp),
            P("section", mp, None),
            P("section", None, mp),
            P("section", None, None, mp),
            P("section", mp, None),
        ),
        out_specs=P("section", "seq", mp),
        check_vma=False,
    )
```

```python
import functools

import jax
import jax.numpy as jnp
import numpy as np
from jax import lax
from jax.experimental import pallas as pl
from jax.experimental.pallas import tpu as pltpu
from jax.sharding import Mesh, PartitionSpec as P

D = 4096
HEAD = 128
ENC_D = 1024
ENC_HEADS = 16
ENC_HEAD = 64
BLOCK = 64
NB_LEN = 128
NEIGH = 2
BATCH = 2
CHIPS = 8
ROWS = 256
WIDTH = 256
UNITS = 4
GROUP = 4
MP = ("z", "y", "core")
KEYS = NEIGH * NB_LEN

epsilon = 1e-05
f32 = jnp.float32
bf16 = jnp.bfloat16


def params(mebibytes=16):
    return pltpu.CompilerParams(vmem_limit_bytes=mebibytes * 1024 * 1024)


def whole(shape):
    return pl.BlockSpec(shape, lambda *_: (0,) * len(shape))


SCALAR = pl.BlockSpec(memory_space=pltpu.SMEM)


PARTS = (352, 160)
STARTS = (0, 352)
MASKS = (((4, 1, 3), (1, 3, 4)), ((3, 4, 1), (3, 4, 1)))


def block_offsets(masks):
    return [
        (masks[0] * (b & 1)) ^ (masks[1] * (b >> 1 & 1)) ^ (masks[2] * (b >> 2 & 1))
        for b in range(CHIPS)
    ]


OFFSETS = np.array([[block_offsets(m) for m in part] for part in MASKS], np.int32)


def core_swap(value):
    return lax.ppermute(value, "core", [(0, 1), (1, 0)])


def section_swap(value):
    return lax.ppermute(value, "section", [(0, 1), (1, 0)])


def chips_to_chips(value):
    return lax.all_to_all(value, ("z", "y"), 0, 0, tiled=True)


def neighbour(value, part, turn):
    route = [
        (2 * chip + core, 2 * (chip ^ MASKS[part][core][turn]) + core)
        for chip in range(CHIPS)
        for core in range(2)
    ]
    return lax.ppermute(value, MP, route)


def places(chip, pick):
    offsets = lax.dynamic_index_in_dim(jnp.asarray(OFFSETS), pick, 1, keepdims=False)
    return jnp.concatenate([jnp.reshape(pick, (1,)), (chip ^ offsets).reshape(-1)]).astype(
        jnp.int32
    )


def together(*values):
    return lax.optimization_barrier(values)


def gather_chips(local, beside):
    side = ()
    near = list(local)
    for turn in range(2):
        sent = [neighbour(value, part, turn) for part, value in enumerate(near)]
        side = beside(turn, side)
        *got, side = together(*sent, side)
        if turn == 0:
            near = [jnp.stack(pair) for pair in zip(near, got)]
        else:
            near = [jnp.concatenate(pair) for pair in zip(near, got)]
    swaps = [core_swap(value) for value in near]
    far = [neighbour(value, part, 2) for part, value in enumerate(near)]
    *swaps, side = together(*swaps, side)
    side = beside(2, side)
    far = list(together(*far))
    return near + far, swaps + [core_swap(value) for value in far], side


def nothing(turn, side):
    return side


def scatter_sum(places_both, mixed, weight):
    own, other = places_both
    other_far = [core_swap(value) for value in terms(other, mixed, weight, 1)]
    other_near = [core_swap(value) for value in terms(other, mixed, weight, 0)]
    own_far = terms(own, mixed, weight, 1)
    own_near = terms(own, mixed, weight, 0)
    other_far = together(*other_far)
    sums = [
        (mine.astype(f32) + got.astype(f32)).astype(bf16)
        for mine, got in zip(own_far, other_far)
    ]
    got = together(*[neighbour(sums[part], part, 2) for part in range(2)], *other_near)
    low = [
        own_near[part].astype(f32) + got[2 + part].astype(f32) + got[part].astype(f32)
        for part in range(2)
    ]
    got = together(*[neighbour(low[part][2:].astype(bf16), part, 1) for part in range(2)])
    low = [low[part][:2] + got[part].astype(f32) for part in range(2)]
    got = [neighbour(low[part][1].astype(bf16), part, 0) for part in range(2)]
    return [low[part][0] for part in range(2)], got


def project_kernel(last, units, place_ref, *refs):
    x_refs, (gain_ref, w_ref), refs = refs[:4], refs[4:6], refs[6:]
    if last:
        acc_in, sq_in, out_ref, sq_ref, left_ref = refs
    else:
        acc_ref, sq_ref, left_ref = refs
    step = pl.program_id(0)

    @pl.when(step == 0)
    def _():
        for part in range(2):
            rows = slice(STARTS[part], STARTS[part] + PARTS[part])
            total = sq_in[rows, :] if last else jnp.zeros((PARTS[part], 128), f32)
            for block in range(CHIPS):
                chip = place_ref[1 + part * CHIPS + block]
                wide = x_refs[part + 2 * (block // 4)][block % 4].astype(f32)
                squares = wide * wide
                total += squares[:, :128] + squares[:, 128:]
                cols = pl.ds(pl.multiple_of(chip * WIDTH, WIDTH), WIDTH)
                left_ref[rows, cols] = (wide * gain_ref[chip, 0]).astype(bf16)
            sq_ref[rows, :] = total

    right = w_ref[0].reshape(CHIPS * WIDTH, WIDTH)
    product = jnp.dot(left_ref[...], right, preferred_element_type=f32)
    if not last:
        acc_ref[0] = product
        return
    mean = jnp.sum(sq_ref[...], axis=1, keepdims=True) / D
    done = ((acc_in[0] + product) / jnp.sqrt(mean + epsilon)).astype(bf16)
    if units:
        for unit in range(UNITS):
            b, h = divmod(unit, 2)
            out_ref[unit, 0] = done[b * ROWS : (b + 1) * ROWS, h * HEAD : (h + 1) * HEAD]
    else:
        out_ref[...] = done


def project_half(place, rows, gains, weight, before, units):
    parts = weight.shape[0]
    count = BATCH * ROWS
    acc = (parts, count, WIDTH)
    sq = (count, 128)
    last = before is not None
    acc_spec = pl.BlockSpec((1, count, WIDTH), lambda s, place: (s, 0, 0))
    in_specs = [whole(value.shape) for value in rows] + [
        pl.BlockSpec((CHIPS, 1, 1, WIDTH), lambda s, place: (0, place[0], 0, 0)),
        pl.BlockSpec((1, CHIPS, 1, WIDTH, WIDTH), lambda s, place: (s, 0, place[0], 0, 0)),
    ]
    scratch = [pltpu.VMEM((count, CHIPS * WIDTH), bf16)]
    if last:
        in_specs += [acc_spec, whole(sq)]
        scratch = [pltpu.VMEM(sq, f32)] + scratch
        if units:
            out = (UNITS, parts, ROWS, HEAD)
            out_specs = pl.BlockSpec((UNITS, 1, ROWS, HEAD), lambda s, place: (0, s, 0, 0))
        else:
            out = (count, WIDTH)
            out_specs = whole(out)
        out_shape = jax.ShapeDtypeStruct(out, bf16)
    else:
        out_specs = [acc_spec, whole(sq)]
        out_shape = [jax.ShapeDtypeStruct(acc, f32), jax.ShapeDtypeStruct(sq, f32)]
    return pl.pallas_call(
        functools.partial(project_kernel, last, units),
        grid_spec=pltpu.PrefetchScalarGridSpec(
            num_scalar_prefetch=1,
            grid=(parts,),
            in_specs=in_specs,
            out_specs=out_specs,
            scratch_shapes=scratch,
        ),
        out_shape=out_shape,
        compiler_params=params(),
        cost_estimate=pl.CostEstimate(
            flops=2 * count * (D // 2) * WIDTH * parts,
            bytes_accessed=D * WIDTH * parts + D * count + 4 * count * WIDTH * parts,
            transcendentals=0,
        ),
    )(
        place,
        *rows,
        gains.reshape(CHIPS, 2, 1, WIDTH),
        weight.reshape(parts, CHIPS, 2, WIDTH, WIDTH),
        *(before or ()),
    )


def project(places_both, local, gains, weight, units, beside=nothing):
    same, swap, side = gather_chips(local, beside)
    before = project_half(places_both[0], same, gains, weight, None, units)
    return project_half(places_both[1], swap, gains, weight, before, units), side


def causal_kernel(triple_ref, out_ref):
    scaling = HEAD ** (-0.5)
    row = lax.broadcasted_iota(jnp.int32, (ROWS, ROWS), 0)
    col = lax.broadcasted_iota(jnp.int32, (ROWS, ROWS), 1)
    for i in range(UNITS):
        queries = triple_ref[i, 0]
        numer = jnp.zeros((ROWS, HEAD), f32)
        denom = jnp.zeros((ROWS, 1), f32)
        for j in range(i + 1):
            scores = lax.dot_general(
                queries, triple_ref[j, 1], (((1,), (1,)), ((), ())), preferred_element_type=f32
            )
            weights = jnp.exp(scores * scaling)
            if i == j:
                weights = jnp.where(col <= row, weights, 0.0)
            denom += jnp.sum(weights, axis=1, keepdims=True)
            numer += jnp.dot(weights.astype(bf16), triple_ref[j, 2], preferred_element_type=f32)
        out_ref[i] = (numer / denom).astype(bf16)


def causal(triple):
    out = (UNITS, ROWS, HEAD)
    return pl.pallas_call(
        causal_kernel,
        out_shape=jax.ShapeDtypeStruct(out, bf16),
        compiler_params=params(),
    )(triple)


def crossed_kernel(asked_ref, prev_ref, pairs_ref, out_ref):
    scaling = HEAD ** (-0.5)
    row = lax.broadcasted_iota(jnp.int32, (BLOCK, 2 * KEYS), 0)
    col = lax.broadcasted_iota(jnp.int32, (BLOCK, 2 * KEYS), 1)
    allowed = (row < BLOCK - 1) == (col < KEYS)
    for unit in range(UNITS):
        b, h = divmod(unit, 2)
        kcols = slice(h * HEAD, (h + 1) * HEAD)
        vcols = slice((2 + h) * HEAD, (3 + h) * HEAD)
        for i in range(ROWS // BLOCK):
            queries = asked_ref[b * ROWS + i * BLOCK : b * ROWS + (i + 1) * BLOCK, kcols]
            if i == 0:
                keys = jnp.concatenate([prev_ref[b, :, kcols], pairs_ref[b, 0, :, kcols]], axis=0)
                values = jnp.concatenate([prev_ref[b, :, vcols], pairs_ref[b, 0, :, vcols]], axis=0)
            else:
                keys = pairs_ref[b, i - 1 : i + 1, :, kcols].reshape(2 * KEYS, HEAD)
                values = pairs_ref[b, i - 1 : i + 1, :, vcols].reshape(2 * KEYS, HEAD)
            scores = lax.dot_general(
                queries, keys, (((1,), (1,)), ((), ())), preferred_element_type=f32
            )
            weights = jnp.where(allowed, jnp.exp(scores * scaling), 0.0)
            denom = jnp.sum(weights, axis=1, keepdims=True)
            numer = jnp.dot(weights.astype(bf16), values, preferred_element_type=f32)
            out_ref[unit, i * BLOCK : (i + 1) * BLOCK, :] = (numer / denom).astype(bf16)


def cross(asked, prev, pairs):
    out = (UNITS, ROWS, HEAD)
    return pl.pallas_call(
        crossed_kernel,
        out_shape=jax.ShapeDtypeStruct(out, bf16),
        compiler_params=params(),
    )(asked, prev, pairs)


def terms_kernel(place_ref, mixed_ref, *refs):
    w_refs, out_refs, left_ref = refs[: 2 * GROUP], refs[2 * GROUP : 2 * GROUP + 2], refs[-1]
    for unit in range(UNITS):
        b, h = divmod(unit, 2)
        left_ref[b * ROWS : (b + 1) * ROWS, h * HEAD : (h + 1) * HEAD] = mixed_ref[unit]
    for part in range(2):
        left = left_ref[STARTS[part] : STARTS[part] + PARTS[part], :]
        for at in range(GROUP):
            right = w_refs[part * GROUP + at][...]
            out_refs[part][at] = jnp.dot(left, right, preferred_element_type=f32).astype(bf16)


def terms(place, mixed, weight, high):
    count = BATCH * ROWS

    def columns(part, at):
        index = 1 + part * CHIPS + GROUP * high + at
        return pl.BlockSpec((WIDTH, WIDTH), lambda s, place: (0, 2 * place[index] + place[0]))

    shapes = [(GROUP, PARTS[part], WIDTH) for part in range(2)]
    return pl.pallas_call(
        terms_kernel,
        grid_spec=pltpu.PrefetchScalarGridSpec(
            num_scalar_prefetch=1,
            grid=(1,),
            in_specs=[whole((UNITS, ROWS, HEAD))]
            + [columns(part, at) for part in range(2) for at in range(GROUP)],
            out_specs=[whole(shape) for shape in shapes],
            scratch_shapes=[pltpu.VMEM((count, WIDTH), bf16)],
        ),
        out_shape=[jax.ShapeDtypeStruct(shape, bf16) for shape in shapes],
        compiler_params=params(8),
        cost_estimate=pl.CostEstimate(
            flops=2 * count * WIDTH * D // 4,
            bytes_accessed=D * WIDTH + D * count // 2,
            transcendentals=0,
        ),
    )(place, mixed, *([weight] * (2 * GROUP)))


def add_product(places_both, states, mixed, weight, side=()):
    low, got = scatter_sum(places_both, mixed, weight)
    *got, side = together(*got, side)
    total = [
        (state.astype(f32) + (mine + far.astype(f32))).astype(bf16)
        for state, mine, far in zip(states, low, got)
    ]
    return total, side


def by_parts(rows):
    return [rows[start : start + count] for start, count in zip(STARTS, PARTS)]


def look_up(ids, enc_embed, places_both, section):
    vocab_here = enc_embed.shape[0]
    mine = lax.dynamic_slice_in_dim(ids, section * (NB_LEN // 2), NB_LEN // 2, axis=1)
    wanted = mine - lax.axis_index(MP) * vocab_here

    def rows(place):
        picks = wanted[2 * place[1 : 1 + CHIPS] + place[0]].reshape(-1)
        inside = (picks >= 0) & (picks < vocab_here)
        found = enc_embed[jnp.clip(picks, 0, vocab_here - 1)]
        found = jnp.where(inside[:, None], found, jnp.zeros((), bf16))
        return found.reshape(CHIPS, NB_LEN // 2, ENC_D)

    far = core_swap(rows(places_both[1]))
    total = rows(places_both[0]) + far
    total = total[:4] + neighbour(total[4:], 0, 2)
    total = total[:2] + neighbour(total[2:], 0, 1)
    return total[0] + neighbour(total[1], 0, 0)


def join_halves(half, section):
    far = section_swap(half)
    return jnp.where(
        section == 0, jnp.concatenate([half, far], axis=0), jnp.concatenate([far, half], axis=0)
    )


def weight_pieces(section, enc_qkv, enc_out, enc_up, enc_down):
    width = ENC_D // 2
    triple = lax.dynamic_slice_in_dim(enc_qkv, section * width, width, axis=2)
    up = enc_up.reshape(64, 16, 2, 2, 64)
    up = lax.dynamic_index_in_dim(up, section, 2, keepdims=False)
    up = jnp.transpose(up, (2, 0, 1, 3)).reshape(2, 64, 2, width)
    down = lax.dynamic_slice_in_dim(enc_down, section * 128, 128, axis=0)
    down = down.reshape(2, 64, 2, width)
    local = jnp.concatenate(
        [
            jnp.transpose(up, (0, 2, 1, 3)).reshape(4, 64, width),
            jnp.transpose(down, (0, 2, 1, 3)).reshape(4, 64, width),
            jnp.transpose(triple, (1, 0, 2)),
            jnp.transpose(enc_out.reshape(64, 2, width), (1, 0, 2)),
        ],
        axis=0,
    )
    return lax.all_gather(local, MP, axis=1, tiled=True)


def scaled_rows(values, gain):
    wide = values.astype(f32)
    root = jnp.sqrt(jnp.mean(wide * wide, axis=1, keepdims=True) + epsilon)
    return (wide * gain).astype(bf16), root


def enc_mix_kernel(section_ref, x_ref, gain_ref, q_ref, k_ref, v_ref, o0_ref, o1_ref, out_ref, mix_ref):
    scaled, root = scaled_rows(x_ref[...], gain_ref[...])
    triple = [
        (jnp.dot(scaled, ref[0], preferred_element_type=f32) / root).astype(bf16)
        for ref in (q_ref, k_ref, v_ref)
    ]
    for head in range(ENC_HEADS // 2):
        cols = slice(head * ENC_HEAD, (head + 1) * ENC_HEAD)
        scores = lax.dot_general(
            triple[0][:, cols],
            triple[1][:, cols],
            (((1,), (1,)), ((), ())),
            preferred_element_type=f32,
        )
        weights = jnp.exp(scores * ENC_HEAD ** (-0.5))
        denom = jnp.sum(weights, axis=1, keepdims=True)
        numer = jnp.dot(weights.astype(bf16), triple[2][:, cols], preferred_element_type=f32)
        mix_ref[:, cols] = (numer / denom).astype(bf16)
    mixed = mix_ref[...]
    width = ENC_D // 2
    rows = pl.ds(pl.multiple_of(section_ref[0] * width, width), width)
    for at, ref in enumerate((o0_ref, o1_ref)):
        part = jnp.dot(mixed, ref[0, rows, :], preferred_element_type=f32)
        out_ref[:, at * width : (at + 1) * width] = part.astype(bf16)


def enc_feed_kernel(x_ref, gain_ref, w_ref, out_ref):
    scaled, root = scaled_rows(x_ref[...], gain_ref[...])
    width = ENC_D // 2
    hidden = [
        jax.nn.gelu(
            jnp.dot(scaled, w_ref[piece], preferred_element_type=f32) / root, approximate=True
        ).astype(bf16)
        for piece in range(4)
    ]
    for at in range(2):
        part = jnp.zeros((NB_LEN, width), f32)
        for piece in range(4):
            rows = slice((piece % 2) * width, (piece % 2 + 1) * width)
            down = w_ref[4 + 2 * (piece // 2) + at, rows, :]
            part += jnp.dot(hidden[piece], down, preferred_element_type=f32)
        out_ref[:, at * width : (at + 1) * width] = part.astype(bf16)


def encode_mix(embedded, enc_norms, pieces, section):
    out = jax.ShapeDtypeStruct((NB_LEN, ENC_D), bf16)
    width = ENC_D // 2
    full = whole((NB_LEN, ENC_D))

    def piece(at):
        return pl.BlockSpec((1, ENC_D, width), lambda s: (at, 0, 0))

    mixed = pl.pallas_call(
        enc_mix_kernel,
        grid=(1,),
        in_specs=[SCALAR, full, whole((1, ENC_D))] + [piece(8 + at) for at in range(5)],
        out_specs=full,
        out_shape=out,
        scratch_shapes=[pltpu.VMEM((NB_LEN, width), bf16)],
        compiler_params=params(),
    )(section, embedded, enc_norms[:1], *([pieces] * 5))
    return embedded, mixed, section_swap(mixed)


def encode_feed(embedded, mixed, far, enc_norms, pieces):
    width = ENC_D // 2
    full = whole((NB_LEN, ENC_D))
    inner = (embedded.astype(f32) + (mixed.astype(f32) + far.astype(f32))).astype(bf16)
    fed = pl.pallas_call(
        enc_feed_kernel,
        grid=(1,),
        in_specs=[full, whole((1, ENC_D)), pl.BlockSpec((8, ENC_D, width), lambda s: (0, 0, 0))],
        out_specs=full,
        out_shape=jax.ShapeDtypeStruct((NB_LEN, ENC_D), bf16),
        compiler_params=params(28),
    )(inner, enc_norms[1:], pieces)
    return inner, fed, section_swap(fed)


def encode_end(inner, fed, far):
    return (inner.astype(f32) + (fed.astype(f32) + far.astype(f32))).astype(bf16)


def decoder_layer(places_both, states, weights, encoder=None):
    norms, triple_w, out_w, query_w, back_w = weights
    idle = encoder is None
    first = nothing if idle else encoder.first
    triple, half = project(places_both, states, norms[0], triple_w, True, first)
    triple = lax.all_to_all(triple, "seq", 0, 0, tiled=True)
    triple, half = together(triple, half)
    embedded = half if idle else encoder.join(half)
    mixed = lax.all_to_all(causal(triple), "seq", 0, 0, tiled=True)
    middle, embedded = add_product(places_both, states, mixed, out_w, embedded)

    def second(turn, side):
        return side if idle else encoder.second(turn, embedded if turn == 0 else side)

    asked, pairs = project(places_both, middle, norms[1], query_w[None], False, second)
    pairs = None if idle else pairs
    return middle, asked, pairs


def cross_layer(places_both, middle, asked, pairs, weights):
    crossed = cross(asked, *pairs)
    return add_product(places_both, middle, crossed, weights[4])[0]


def on_device(
    hidden_states,
    neighbour_ids,
    neighbour_table,
    enc_embed,
    enc_norms,
    enc_qkv,
    enc_out,
    enc_up,
    enc_down,
    dec_norms,
    dec_qkv,
    dec_out,
    cross_query,
    cross_pair,
    cross_out,
):
    section = lax.axis_index("section").astype(jnp.int32)
    core_at = lax.axis_index("core").astype(jnp.int32)
    chip = lax.axis_index(("z", "y")).astype(jnp.int32)
    places_both = [places(chip, core_at), places(chip, 1 - core_at)]
    blocks_here = neighbour_table.shape[1]
    pieces = weight_pieces(section, enc_qkv, enc_out, enc_up, enc_down)
    slot_ids = neighbour_ids[neighbour_table.reshape(-1)]
    count = lax.axis_size("seq")
    pair_w = cross_pair[0].reshape(ENC_D, 2 * WIDTH)
    section_ref = jnp.reshape(section, (1,))

    def pair_rows(rows):
        return jnp.dot(rows, pair_w, preferred_element_type=f32).astype(bf16)

    class Encoder:
        @staticmethod
        def first(turn, side):
            if turn == 0:
                return slot_ids
            if turn == 1:
                return side
            return look_up(side, enc_embed, places_both, section)

        @staticmethod
        def join(half):
            return join_halves(half, section)

        @staticmethod
        def second(turn, side):
            if turn == 0:
                return encode_mix(side, enc_norms, pieces, section_ref)
            if turn == 1:
                return encode_feed(*side, enc_norms, pieces)
            encoded = lax.all_gather(encode_end(*side), MP, axis=0, tiled=True)
            edge = encoded.reshape(BATCH, blocks_here, KEYS, ENC_D)[:, -1]
            edge = pair_rows(edge.reshape(BATCH * KEYS, ENC_D)).reshape(BATCH, KEYS, 2 * WIDTH)
            prev = lax.ppermute(edge, "seq", [(i, i + 1) for i in range(count - 1)])
            return prev, pair_rows(encoded).reshape(BATCH, blocks_here, KEYS, 2 * WIDTH)

    weights = (
        dec_norms[0],
        jnp.transpose(dec_qkv[0], (1, 0, 2)),
        dec_out[0],
        cross_query[0],
        cross_out[0],
    )

    states = hidden_states.reshape(BATCH * ROWS, WIDTH)
    middle, asked, pairs = decoder_layer(places_both, by_parts(states), weights, Encoder)
    first = cross_layer(places_both, middle, asked, pairs, weights)
    handed = section_swap(jnp.concatenate(first))
    middle, asked, _ = decoder_layer(places_both, by_parts(handed), weights)
    second = jnp.concatenate(cross_layer(places_both, middle, asked, pairs, weights))
    second = second.reshape(BATCH, ROWS, WIDTH)
    return jnp.where(section == 0, section_swap(second[0]), second[1])[None]


def solution(mesh):
    devices = mesh.devices
    sections, seqs = devices.shape[:2]
    split = Mesh(
        devices.reshape(sections, seqs, 2, 4, 2), ("section", "seq", "z", "y", "core")
    )
    mp = ("z", "y", "core")
    return jax.shard_map(
        on_device,
        mesh=split,
        in_specs=(
            P(None, "seq", mp),
            P(),
            P(None, "seq", None),
            P(mp, None),
            P(),
            P(mp, None, None),
            P(mp, None),
            P(mp, None),
            P(mp, None),
            P("section", None, None),
            P("section", None, None, mp),
            P("section", mp, None),
            P("section", None, mp),
            P("section", None, None, mp),
            P("section", mp, None),
        ),
        out_specs=P("section", "seq", mp),
        check_vma=False,
    )
```

```python
import functools

import jax
import jax.numpy as jnp
import numpy as np
from jax import lax
from jax.experimental import pallas as pl
from jax.experimental.pallas import tpu as pltpu
from jax.sharding import Mesh, PartitionSpec as P

D = 4096
HEAD = 128
ENC_D = 1024
ENC_HEADS = 16
ENC_HEAD = 64
BLOCK = 64
NB_LEN = 128
NEIGH = 2
BATCH = 2
CHIPS = 8
ROWS = 256
WIDTH = 256
UNITS = 4
GROUP = 4
MP = ("z", "y", "core")
KEYS = NEIGH * NB_LEN

epsilon = 1e-05
f32 = jnp.float32
bf16 = jnp.bfloat16


def params(mebibytes=16):
    return pltpu.CompilerParams(vmem_limit_bytes=mebibytes * 1024 * 1024)


def whole(shape):
    return pl.BlockSpec(shape, lambda *_: (0,) * len(shape))


SCALAR = pl.BlockSpec(memory_space=pltpu.SMEM)


PARTS = (352, 160)
STARTS = (0, 352)
ENC_PARTS = (80, 48)
ENC_STARTS = (0, 80)
MASKS = (((4, 1, 3), (1, 3, 4)), ((3, 4, 1), (3, 4, 1)))


def block_offsets(masks):
    return [
        (masks[0] * (b & 1)) ^ (masks[1] * (b >> 1 & 1)) ^ (masks[2] * (b >> 2 & 1))
        for b in range(CHIPS)
    ]


OFFSETS = np.array([[block_offsets(m) for m in part] for part in MASKS], np.int32)


def core_swap(value):
    return lax.ppermute(value, "core", [(0, 1), (1, 0)])


def section_swap(value):
    return lax.ppermute(value, "section", [(0, 1), (1, 0)])


def chips_to_chips(value):
    return lax.all_to_all(value, ("z", "y"), 0, 0, tiled=True)


def neighbour(value, part, turn):
    route = [
        (2 * chip + core, 2 * (chip ^ MASKS[part][core][turn]) + core)
        for chip in range(CHIPS)
        for core in range(2)
    ]
    return lax.ppermute(value, MP, route)


def places(chip, pick):
    offsets = lax.dynamic_index_in_dim(jnp.asarray(OFFSETS), pick, 1, keepdims=False)
    return jnp.concatenate([jnp.reshape(pick, (1,)), (chip ^ offsets).reshape(-1)]).astype(
        jnp.int32
    )


def together(*values):
    return lax.optimization_barrier(values)


def gather_chips(local, beside):
    side = ()
    near = list(local)
    for turn in range(2):
        sent = [neighbour(value, part, turn) for part, value in enumerate(near)]
        side = beside(turn, side)
        *got, side = together(*sent, side)
        if turn == 0:
            near = [jnp.stack(pair) for pair in zip(near, got)]
        else:
            near = [jnp.concatenate(pair) for pair in zip(near, got)]
    swaps = [core_swap(value) for value in near]
    far = [neighbour(value, part, 2) for part, value in enumerate(near)]
    *swaps, side = together(*swaps, side)
    side = beside(2, side)
    *far, side = together(*far, side)
    return near + far, swaps + [core_swap(value) for value in far], side


def nothing(turn, side):
    return side


def scatter_sum(places_both, mixed, weight):
    own, other = places_both
    other_far = [core_swap(value) for value in terms(other, mixed, weight, 1)]
    other_near = [core_swap(value) for value in terms(other, mixed, weight, 0)]
    own_far = terms(own, mixed, weight, 1)
    own_near = terms(own, mixed, weight, 0)
    other_far = together(*other_far)
    sums = [
        (mine.astype(f32) + got.astype(f32)).astype(bf16)
        for mine, got in zip(own_far, other_far)
    ]
    got = together(*[neighbour(sums[part], part, 2) for part in range(2)], *other_near)
    low = [
        own_near[part].astype(f32) + got[2 + part].astype(f32) + got[part].astype(f32)
        for part in range(2)
    ]
    got = together(*[neighbour(low[part][2:].astype(bf16), part, 1) for part in range(2)])
    low = [low[part][:2] + got[part].astype(f32) for part in range(2)]
    got = [neighbour(low[part][1].astype(bf16), part, 0) for part in range(2)]
    return [low[part][0] for part in range(2)], got


def project_kernel(last, units, place_ref, *refs):
    x_refs, (gain_ref, w_ref), refs = refs[:4], refs[4:6], refs[6:]
    if last:
        acc_in, sq_in, out_ref, sq_ref, left_ref = refs
    else:
        acc_ref, sq_ref, left_ref = refs
    step = pl.program_id(0)

    @pl.when(step == 0)
    def _():
        for part in range(2):
            rows = slice(STARTS[part], STARTS[part] + PARTS[part])
            total = sq_in[rows, :] if last else jnp.zeros((PARTS[part], 128), f32)
            for block in range(CHIPS):
                chip = place_ref[1 + part * CHIPS + block]
                wide = x_refs[part + 2 * (block // 4)][block % 4].astype(f32)
                squares = wide * wide
                total += squares[:, :128] + squares[:, 128:]
                cols = pl.ds(pl.multiple_of(chip * WIDTH, WIDTH), WIDTH)
                left_ref[rows, cols] = (wide * gain_ref[chip, 0]).astype(bf16)
            sq_ref[rows, :] = total

    right = w_ref[0].reshape(CHIPS * WIDTH, WIDTH)
    product = jnp.dot(left_ref[...], right, preferred_element_type=f32)
    if not last:
        acc_ref[0] = product
        return
    mean = jnp.sum(sq_ref[...], axis=1, keepdims=True) / D
    done = ((acc_in[0] + product) / jnp.sqrt(mean + epsilon)).astype(bf16)
    if units:
        for unit in range(UNITS):
            b, h = divmod(unit, 2)
            out_ref[unit, 0] = done[b * ROWS : (b + 1) * ROWS, h * HEAD : (h + 1) * HEAD]
    else:
        out_ref[...] = done


def project_half(place, rows, gains, weight, before, units):
    parts = weight.shape[0]
    count = BATCH * ROWS
    acc = (parts, count, WIDTH)
    sq = (count, 128)
    last = before is not None
    acc_spec = pl.BlockSpec((1, count, WIDTH), lambda s, place: (s, 0, 0))
    in_specs = [whole(value.shape) for value in rows] + [
        pl.BlockSpec((CHIPS, 1, 1, WIDTH), lambda s, place: (0, place[0], 0, 0)),
        pl.BlockSpec((1, CHIPS, 1, WIDTH, WIDTH), lambda s, place: (s, 0, place[0], 0, 0)),
    ]
    scratch = [pltpu.VMEM((count, CHIPS * WIDTH), bf16)]
    if last:
        in_specs += [acc_spec, whole(sq)]
        scratch = [pltpu.VMEM(sq, f32)] + scratch
        if units:
            out = (UNITS, parts, ROWS, HEAD)
            out_specs = pl.BlockSpec((UNITS, 1, ROWS, HEAD), lambda s, place: (0, s, 0, 0))
        else:
            out = (count, WIDTH)
            out_specs = whole(out)
        out_shape = jax.ShapeDtypeStruct(out, bf16)
    else:
        out_specs = [acc_spec, whole(sq)]
        out_shape = [jax.ShapeDtypeStruct(acc, f32), jax.ShapeDtypeStruct(sq, f32)]
    return pl.pallas_call(
        functools.partial(project_kernel, last, units),
        grid_spec=pltpu.PrefetchScalarGridSpec(
            num_scalar_prefetch=1,
            grid=(parts,),
            in_specs=in_specs,
            out_specs=out_specs,
            scratch_shapes=scratch,
        ),
        out_shape=out_shape,
        compiler_params=params(),
        cost_estimate=pl.CostEstimate(
            flops=2 * count * (D // 2) * WIDTH * parts,
            bytes_accessed=D * WIDTH * parts + D * count + 4 * count * WIDTH * parts,
            transcendentals=0,
        ),
    )(
        place,
        *rows,
        gains.reshape(CHIPS, 2, 1, WIDTH),
        weight.reshape(parts, CHIPS, 2, WIDTH, WIDTH),
        *(before or ()),
    )


def project(places_both, local, gains, weight, units, beside=nothing):
    same, swap, side = gather_chips(local, beside)
    before = project_half(places_both[0], same, gains, weight, None, units)
    return project_half(places_both[1], swap, gains, weight, before, units), side


def causal_kernel(triple_ref, out_ref):
    scaling = HEAD ** (-0.5)
    row = lax.broadcasted_iota(jnp.int32, (ROWS, ROWS), 0)
    col = lax.broadcasted_iota(jnp.int32, (ROWS, ROWS), 1)
    for i in range(UNITS):
        queries = triple_ref[i, 0]
        numer = jnp.zeros((ROWS, HEAD), f32)
        denom = jnp.zeros((ROWS, 1), f32)
        for j in range(i + 1):
            scores = lax.dot_general(
                queries, triple_ref[j, 1], (((1,), (1,)), ((), ())), preferred_element_type=f32
            )
            weights = jnp.exp(scores * scaling)
            if i == j:
                weights = jnp.where(col <= row, weights, 0.0)
            denom += jnp.sum(weights, axis=1, keepdims=True)
            numer += jnp.dot(weights.astype(bf16), triple_ref[j, 2], preferred_element_type=f32)
        out_ref[i] = (numer / denom).astype(bf16)


def causal(triple):
    out = (UNITS, ROWS, HEAD)
    return pl.pallas_call(
        causal_kernel,
        out_shape=jax.ShapeDtypeStruct(out, bf16),
        compiler_params=params(),
    )(triple)


def crossed_kernel(asked_ref, *refs):
    (prev_refs, pairs_refs), out_ref = (refs[0:2], refs[2:4]), refs[4]
    scaling = HEAD ** (-0.5)
    row = lax.broadcasted_iota(jnp.int32, (BLOCK, 2 * KEYS), 0)
    col = lax.broadcasted_iota(jnp.int32, (BLOCK, 2 * KEYS), 1)
    allowed = (row < BLOCK - 1) == (col < KEYS)
    for unit in range(UNITS):
        b, h = divmod(unit, 2)

        def both_blocks(i, cols):
            before = [ref[b, :, cols] if i == 0 else pair[b, i - 1, :, cols]
                      for ref, pair in zip(prev_refs, pairs_refs)]
            return jnp.concatenate(before + [pair[b, i, :, cols] for pair in pairs_refs], axis=0)

        for i in range(ROWS // BLOCK):
            queries = asked_ref[
                b * ROWS + i * BLOCK : b * ROWS + (i + 1) * BLOCK, h * HEAD : (h + 1) * HEAD
            ]
            keys = both_blocks(i, slice(h * HEAD, (h + 1) * HEAD))
            values = both_blocks(i, slice((2 + h) * HEAD, (3 + h) * HEAD))
            scores = lax.dot_general(
                queries, keys, (((1,), (1,)), ((), ())), preferred_element_type=f32
            )
            weights = jnp.where(allowed, jnp.exp(scores * scaling), 0.0)
            denom = jnp.sum(weights, axis=1, keepdims=True)
            numer = jnp.dot(weights.astype(bf16), values, preferred_element_type=f32)
            out_ref[unit, i * BLOCK : (i + 1) * BLOCK, :] = (numer / denom).astype(bf16)


def cross(asked, prevs, pairs):
    out = (UNITS, ROWS, HEAD)
    return pl.pallas_call(
        crossed_kernel,
        out_shape=jax.ShapeDtypeStruct(out, bf16),
        compiler_params=params(),
    )(asked, *prevs, *pairs)


def terms_kernel(place_ref, mixed_ref, *refs):
    w_refs, out_refs, left_ref = refs[: 2 * GROUP], refs[2 * GROUP : 2 * GROUP + 2], refs[-1]
    for unit in range(UNITS):
        b, h = divmod(unit, 2)
        left_ref[b * ROWS : (b + 1) * ROWS, h * HEAD : (h + 1) * HEAD] = mixed_ref[unit]
    for part in range(2):
        left = left_ref[STARTS[part] : STARTS[part] + PARTS[part], :]
        for at in range(GROUP):
            right = w_refs[part * GROUP + at][...]
            out_refs[part][at] = jnp.dot(left, right, preferred_element_type=f32).astype(bf16)


def terms(place, mixed, weight, high):
    count = BATCH * ROWS

    def columns(part, at):
        index = 1 + part * CHIPS + GROUP * high + at
        return pl.BlockSpec((WIDTH, WIDTH), lambda s, place: (0, 2 * place[index] + place[0]))

    shapes = [(GROUP, PARTS[part], WIDTH) for part in range(2)]
    return pl.pallas_call(
        terms_kernel,
        grid_spec=pltpu.PrefetchScalarGridSpec(
            num_scalar_prefetch=1,
            grid=(1,),
            in_specs=[whole((UNITS, ROWS, HEAD))]
            + [columns(part, at) for part in range(2) for at in range(GROUP)],
            out_specs=[whole(shape) for shape in shapes],
            scratch_shapes=[pltpu.VMEM((count, WIDTH), bf16)],
        ),
        out_shape=[jax.ShapeDtypeStruct(shape, bf16) for shape in shapes],
        compiler_params=params(8),
        cost_estimate=pl.CostEstimate(
            flops=2 * count * WIDTH * D // 4,
            bytes_accessed=D * WIDTH + D * count // 2,
            transcendentals=0,
        ),
    )(place, mixed, *([weight] * (2 * GROUP)))


def add_product(places_both, states, mixed, weight, side=()):
    low, got = scatter_sum(places_both, mixed, weight)
    *got, side = together(*got, side)
    total = [
        (state.astype(f32) + (mine + far.astype(f32))).astype(bf16)
        for state, mine, far in zip(states, low, got)
    ]
    return total, side


def by_parts(rows):
    return [rows[start : start + count] for start, count in zip(STARTS, PARTS)]


def look_up(ids, enc_embed, places_both, section):
    vocab_here = enc_embed.shape[0]
    mine = lax.dynamic_slice_in_dim(ids, section * (NB_LEN // 2), NB_LEN // 2, axis=1)
    wanted = mine - lax.axis_index(MP) * vocab_here

    def rows(place):
        picks = wanted[2 * place[1 : 1 + CHIPS] + place[0]].reshape(-1)
        inside = (picks >= 0) & (picks < vocab_here)
        found = enc_embed[jnp.clip(picks, 0, vocab_here - 1)]
        found = jnp.where(inside[:, None], found, jnp.zeros((), bf16))
        return found.reshape(CHIPS, NB_LEN // 2, ENC_D)

    return rows(places_both[0]), rows(places_both[1])


def looked_up(own, other):
    total = own + core_swap(other)
    total = total[:4] + neighbour(total[4:], 0, 2)
    total = total[:2] + neighbour(total[2:], 0, 1)
    return total[0] + neighbour(total[1], 0, 0)


def join_halves(half, section):
    far = section_swap(half)
    return jnp.where(
        section == 0, jnp.concatenate([half, far], axis=0), jnp.concatenate([far, half], axis=0)
    )


def weight_parts(section, enc_qkv, enc_out, enc_up, enc_down):
    width = ENC_D // 2
    triple = lax.dynamic_slice_in_dim(enc_qkv, section * width, width, axis=2)
    up = enc_up.reshape(64, 16, 2, 2, 64)
    up = lax.dynamic_index_in_dim(up, section, 2, keepdims=False)
    up = jnp.transpose(up, (2, 0, 1, 3)).reshape(2, 64, 2, width)
    down = lax.dynamic_slice_in_dim(enc_down, section * 128, 128, axis=0)
    down = down.reshape(2, 64, 2, width)
    return jnp.concatenate(
        [
            jnp.transpose(up, (0, 2, 1, 3)).reshape(4, 64, width),
            jnp.transpose(down, (0, 2, 1, 3)).reshape(4, 64, width),
            jnp.transpose(triple, (1, 0, 2)),
            jnp.transpose(enc_out.reshape(64, 2, width), (1, 0, 2)),
        ],
        axis=0,
    )


def scaled_rows(values, gain):
    wide = values.astype(f32)
    root = jnp.sqrt(jnp.mean(wide * wide, axis=1, keepdims=True) + epsilon)
    return (wide * gain).astype(bf16), root


def enc_mix_kernel(section_ref, x_ref, gain_ref, q_ref, k_ref, v_ref, o0_ref, o1_ref, out_ref, mix_ref):
    scaled, root = scaled_rows(x_ref[...], gain_ref[...])
    triple = [
        (jnp.dot(scaled, ref[0], preferred_element_type=f32) / root).astype(bf16)
        for ref in (q_ref, k_ref, v_ref)
    ]
    for head in range(ENC_HEADS // 2):
        cols = slice(head * ENC_HEAD, (head + 1) * ENC_HEAD)
        scores = lax.dot_general(
            triple[0][:, cols],
            triple[1][:, cols],
            (((1,), (1,)), ((), ())),
            preferred_element_type=f32,
        )
        weights = jnp.exp(scores * ENC_HEAD ** (-0.5))
        denom = jnp.sum(weights, axis=1, keepdims=True)
        numer = jnp.dot(weights.astype(bf16), triple[2][:, cols], preferred_element_type=f32)
        mix_ref[:, cols] = (numer / denom).astype(bf16)
    mixed = mix_ref[...]
    width = ENC_D // 2
    rows = pl.ds(pl.multiple_of(section_ref[0] * width, width), width)
    for at, ref in enumerate((o0_ref, o1_ref)):
        part = jnp.dot(mixed, ref[0, rows, :], preferred_element_type=f32)
        out_ref[:, at * width : (at + 1) * width] = part.astype(bf16)


def enc_feed_kernel(x_ref, gain_ref, w_ref, out_ref):
    scaled, root = scaled_rows(x_ref[...], gain_ref[...])
    width = ENC_D // 2
    hidden = [
        jax.nn.gelu(
            jnp.dot(scaled, w_ref[piece], preferred_element_type=f32) / root, approximate=True
        ).astype(bf16)
        for piece in range(4)
    ]
    for at in range(2):
        part = jnp.zeros((NB_LEN, width), f32)
        for piece in range(4):
            rows = slice((piece % 2) * width, (piece % 2 + 1) * width)
            down = w_ref[4 + 2 * (piece // 2) + at, rows, :]
            part += jnp.dot(hidden[piece], down, preferred_element_type=f32)
        out_ref[:, at * width : (at + 1) * width] = part.astype(bf16)


def encode_mix(embedded, enc_norms, pieces, section):
    out = jax.ShapeDtypeStruct((NB_LEN, ENC_D), bf16)
    width = ENC_D // 2
    full = whole((NB_LEN, ENC_D))

    def piece(at):
        return pl.BlockSpec((1, ENC_D, width), lambda s: (at, 0, 0))

    mixed = pl.pallas_call(
        enc_mix_kernel,
        grid=(1,),
        in_specs=[SCALAR, full, whole((1, ENC_D))] + [piece(8 + at) for at in range(5)],
        out_specs=full,
        out_shape=out,
        scratch_shapes=[pltpu.VMEM((NB_LEN, width), bf16)],
        compiler_params=params(),
    )(section, embedded, enc_norms[:1], *([pieces] * 5))
    return embedded, mixed, section_swap(mixed)


def encode_feed(embedded, mixed, far, enc_norms, pieces):
    width = ENC_D // 2
    full = whole((NB_LEN, ENC_D))
    inner = (embedded.astype(f32) + (mixed.astype(f32) + far.astype(f32))).astype(bf16)
    fed = pl.pallas_call(
        enc_feed_kernel,
        grid=(1,),
        in_specs=[full, whole((1, ENC_D)), pl.BlockSpec((8, ENC_D, width), lambda s: (0, 0, 0))],
        out_specs=full,
        out_shape=jax.ShapeDtypeStruct((NB_LEN, ENC_D), bf16),
        compiler_params=params(28),
    )(inner, enc_norms[1:], pieces)
    return inner, fed, section_swap(fed)


def encode_end(inner, fed, far):
    return (inner.astype(f32) + (fed.astype(f32) + far.astype(f32))).astype(bf16)


def pairs_kernel(place_ref, *refs):
    x_refs, (w_ref, out_ref, left_ref) = refs[:4], refs[4:]
    for part in range(2):
        for block in range(CHIPS):
            chip = place_ref[1 + part * CHIPS + block]
            start = pl.multiple_of(chip * NB_LEN + ENC_STARTS[part], 16)
            value = x_refs[part + 2 * (block // 4)][block % 4]
            left_ref[pl.ds(start, ENC_PARTS[part]), :] = value
    out_ref[...] = jnp.dot(left_ref[...], w_ref[...], preferred_element_type=f32).astype(bf16)


def make_pairs(place, rows, weight):
    out = (CHIPS * NB_LEN, 2 * WIDTH)
    pairs = pl.pallas_call(
        pairs_kernel,
        grid_spec=pltpu.PrefetchScalarGridSpec(
            num_scalar_prefetch=1,
            grid=(1,),
            in_specs=[whole(value.shape) for value in rows] + [whole(weight.shape)],
            out_specs=whole(out),
            scratch_shapes=[pltpu.VMEM((CHIPS * NB_LEN, ENC_D), bf16)],
        ),
        out_shape=jax.ShapeDtypeStruct(out, bf16),
        compiler_params=params(20),
        cost_estimate=pl.CostEstimate(
            flops=2 * CHIPS * NB_LEN * ENC_D * 2 * WIDTH,
            bytes_accessed=2 * (CHIPS * NB_LEN + 2 * WIDTH) * ENC_D,
            transcendentals=0,
        ),
    )(place, *rows, weight)
    pairs = pairs.reshape(BATCH, CHIPS // BATCH, NB_LEN, 2 * WIDTH)
    count = lax.axis_size("seq")
    prev = lax.ppermute(pairs[:, -1], "seq", [(i, i + 1) for i in range(count - 1)])
    return prev, pairs


def decoder_layer(places_both, states, weights, encoder=None):
    norms, triple_w, out_w, query_w, back_w = weights
    idle = encoder is None
    first = nothing if idle else encoder.first
    triple, side = project(places_both, states, norms[0], triple_w, True, first)
    if idle:
        triple = lax.all_to_all(triple, "seq", 0, 0, tiled=True)
        embedded = ()
    else:
        found, local = side
        pieces = encoder.gather(local)
        triple, found = together(triple, found)
        triple = lax.all_to_all(triple, "seq", 0, 0, tiled=True)
        triple, half = together(triple, looked_up(*found))
        embedded = encoder.join(half)
    mixed = lax.all_to_all(causal(triple), "seq", 0, 0, tiled=True)
    middle, embedded = add_product(places_both, states, mixed, out_w, embedded)

    def second(turn, side):
        return side if idle else encoder.second(turn, embedded if turn == 0 else side, pieces)

    asked, encoded = project(places_both, middle, norms[1], query_w[None], False, second)
    return middle, asked, None if idle else encoder.pairs(encoded)


def cross_layer(places_both, middle, asked, pairs, weights):
    crossed = cross(asked, *pairs)
    return add_product(places_both, middle, crossed, weights[4])[0]


def on_device(
    hidden_states,
    neighbour_ids,
    neighbour_table,
    enc_embed,
    enc_norms,
    enc_qkv,
    enc_out,
    enc_up,
    enc_down,
    dec_norms,
    dec_qkv,
    dec_out,
    cross_query,
    cross_pair,
    cross_out,
):
    section = lax.axis_index("section").astype(jnp.int32)
    core_at = lax.axis_index("core").astype(jnp.int32)
    chip = lax.axis_index(("z", "y")).astype(jnp.int32)
    places_both = [places(chip, core_at), places(chip, 1 - core_at)]
    local = weight_parts(section, enc_qkv, enc_out, enc_up, enc_down)
    slot_ids = neighbour_ids[neighbour_table.reshape(-1)]
    pair_w = cross_pair[0].reshape(ENC_D, 2 * WIDTH)
    section_ref = jnp.reshape(section, (1,))

    class Encoder:
        @staticmethod
        def first(turn, side):
            if turn == 0:
                return slot_ids
            if turn == 1:
                return side
            return look_up(side, enc_embed, places_both, section), local

        @staticmethod
        def gather(local):
            return lax.all_gather(local, MP, axis=1, tiled=True)

        @staticmethod
        def join(half):
            return join_halves(half, section)

        @staticmethod
        def second(turn, side, pieces):
            if turn == 0:
                return encode_mix(side, enc_norms, pieces, section_ref)
            if turn == 1:
                return encode_feed(*side, enc_norms, pieces)
            return encode_end(*side)

        @staticmethod
        def pairs(encoded):
            parts = [
                encoded[start : start + count] for start, count in zip(ENC_STARTS, ENC_PARTS)
            ]
            both = gather_chips(parts, nothing)[:2]
            made = [make_pairs(place, rows, pair_w) for place, rows in zip(places_both, both)]
            return [prev for prev, _ in made], [pairs for _, pairs in made]

    weights = (
        dec_norms[0],
        jnp.transpose(dec_qkv[0], (1, 0, 2)),
        dec_out[0],
        cross_query[0],
        cross_out[0],
    )

    states = hidden_states.reshape(BATCH * ROWS, WIDTH)
    middle, asked, pairs = decoder_layer(places_both, by_parts(states), weights, Encoder)
    first = cross_layer(places_both, middle, asked, pairs, weights)
    handed = section_swap(jnp.concatenate(first))
    middle, asked, _ = decoder_layer(places_both, by_parts(handed), weights)
    second = jnp.concatenate(cross_layer(places_both, middle, asked, pairs, weights))
    second = second.reshape(BATCH, ROWS, WIDTH)
    return jnp.where(section == 0, section_swap(second[0]), second[1])[None]


def solution(mesh):
    devices = mesh.devices
    sections, seqs = devices.shape[:2]
    split = Mesh(
        devices.reshape(sections, seqs, 2, 4, 2), ("section", "seq", "z", "y", "core")
    )
    mp = ("z", "y", "core")
    return jax.shard_map(
        on_device,
        mesh=split,
        in_specs=(
            P(None, "seq", mp),
            P(),
            P(None, "seq", None),
            P(mp, None),
            P(),
            P(mp, None, None),
            P(mp, None),
            P(mp, None),
            P(mp, None),
            P("section", None, None),
            P("section", None, None, mp),
            P("section", mp, None),
            P("section", None, mp),
            P("section", None, None, mp),
            P("section", mp, None),
        ),
        out_specs=P("section", "seq", mp),
        check_vma=False,
    )
```

```python
import functools

import jax
import jax.numpy as jnp
import numpy as np
from jax import lax
from jax.experimental import pallas as pl
from jax.experimental.pallas import tpu as pltpu
from jax.sharding import Mesh, PartitionSpec as P

D = 4096
HEAD = 128
ENC_D = 1024
ENC_HEADS = 16
ENC_HEAD = 64
BLOCK = 64
NB_LEN = 128
NEIGH = 2
BATCH = 2
CHIPS = 8
ROWS = 256
WIDTH = 256
UNITS = 4
GROUP = 4
MP = ("z", "y", "core")
KEYS = NEIGH * NB_LEN

epsilon = 1e-05
f32 = jnp.float32
bf16 = jnp.bfloat16


def params(mebibytes=16):
    return pltpu.CompilerParams(vmem_limit_bytes=mebibytes * 1024 * 1024)


def whole(shape):
    return pl.BlockSpec(shape, lambda *_: (0,) * len(shape))


SCALAR = pl.BlockSpec(memory_space=pltpu.SMEM)


PARTS = (352, 160)
STARTS = (0, 352)
ENC_PARTS = (80, 48)
ENC_STARTS = (0, 80)
MASKS = (((4, 1, 3), (1, 3, 4)), ((3, 4, 1), (3, 4, 1)))


def block_offsets(masks):
    return [
        (masks[0] * (b & 1)) ^ (masks[1] * (b >> 1 & 1)) ^ (masks[2] * (b >> 2 & 1))
        for b in range(CHIPS)
    ]


OFFSETS = np.array([[block_offsets(m) for m in part] for part in MASKS], np.int32)


def core_swap(value):
    return lax.ppermute(value, "core", [(0, 1), (1, 0)])


def section_swap(value):
    return lax.ppermute(value, "section", [(0, 1), (1, 0)])


def chips_to_chips(value):
    return lax.all_to_all(value, ("z", "y"), 0, 0, tiled=True)


def neighbour(value, part, turn):
    route = [
        (2 * chip + core, 2 * (chip ^ MASKS[part][core][turn]) + core)
        for chip in range(CHIPS)
        for core in range(2)
    ]
    return lax.ppermute(value, MP, route)


def places(chip, pick):
    offsets = lax.dynamic_index_in_dim(jnp.asarray(OFFSETS), pick, 1, keepdims=False)
    return jnp.concatenate([jnp.reshape(pick, (1,)), (chip ^ offsets).reshape(-1)]).astype(
        jnp.int32
    )


def together(*values):
    return lax.optimization_barrier(values)


def first_round(local):
    return [neighbour(value, part, 0) for part, value in enumerate(local)]


def later_rounds(local, got):
    near = [jnp.stack(pair) for pair in zip(local, got)]
    got = together(*[neighbour(value, part, 1) for part, value in enumerate(near)])
    near = [jnp.concatenate(pair) for pair in zip(near, got)]
    swaps = [core_swap(value) for value in near]
    far = [neighbour(value, part, 2) for part, value in enumerate(near)]
    swaps = list(together(*swaps))
    far = list(together(*far))
    return near + far, swaps + [core_swap(value) for value in far]


def gather_chips(local):
    return later_rounds(local, together(*first_round(local)))


def spread(local):
    rows = jnp.concatenate(local)
    return jnp.broadcast_to(rows[None], (CHIPS,) + rows.shape)


def scatter_sum(places_both, mixed, weight):
    own, other = places_both
    other_far = [core_swap(value) for value in terms(other, mixed, weight, 1)]
    other_near = [core_swap(value) for value in terms(other, mixed, weight, 0)]
    own_far = terms(own, mixed, weight, 1)
    own_near = terms(own, mixed, weight, 0)
    other_far = together(*other_far)
    sums = [
        (mine.astype(f32) + got.astype(f32)).astype(bf16)
        for mine, got in zip(own_far, other_far)
    ]
    got = together(*[neighbour(sums[part], part, 2) for part in range(2)], *other_near)
    low = [
        own_near[part].astype(f32) + got[2 + part].astype(f32) + got[part].astype(f32)
        for part in range(2)
    ]
    got = together(*[neighbour(low[part][2:].astype(bf16), part, 1) for part in range(2)])
    low = [low[part][:2] + got[part].astype(f32) for part in range(2)]
    got = [neighbour(low[part][1].astype(bf16), part, 0) for part in range(2)]
    return [low[part][0] for part in range(2)], got


def project_kernel(last, units, place_ref, *refs):
    whole_rows = len(refs) == (8 if last else 6)
    count = 1 if whole_rows else 4
    x_refs, (gain_ref, w_ref), refs = refs[:count], refs[count : count + 2], refs[count + 2 :]
    if last:
        acc_in, sq_in, out_ref, sq_ref, left_ref = refs
    else:
        acc_ref, sq_ref, left_ref = refs
    step = pl.program_id(0)

    def place_rows(rows, blocks):
        total = sq_in[rows, :] if last else jnp.zeros((rows.stop - rows.start, 128), f32)
        for block, chip in blocks:
            wide = block.astype(f32)
            squares = wide * wide
            total += squares[:, :128] + squares[:, 128:]
            cols = pl.ds(pl.multiple_of(chip * WIDTH, WIDTH), WIDTH)
            left_ref[rows, cols] = (wide * gain_ref[chip, 0]).astype(bf16)
        sq_ref[rows, :] = total

    @pl.when(step == 0)
    def _():
        for part in range(2):
            rows = slice(STARTS[part], STARTS[part] + PARTS[part])
            if whole_rows:
                blocks = [(x_refs[0][chip, rows, :], chip) for chip in range(CHIPS)]
            else:
                blocks = [
                    (
                        x_refs[part + 2 * (block // 4)][block % 4],
                        place_ref[1 + part * CHIPS + block],
                    )
                    for block in range(CHIPS)
                ]
            place_rows(rows, blocks)

    right = w_ref[0].reshape(CHIPS * WIDTH, WIDTH)
    product = jnp.dot(left_ref[...], right, preferred_element_type=f32)
    if not last:
        acc_ref[0] = product
        return
    mean = jnp.sum(sq_ref[...], axis=1, keepdims=True) / D
    done = ((acc_in[0] + product) / jnp.sqrt(mean + epsilon)).astype(bf16)
    if units:
        for unit in range(UNITS):
            b, h = divmod(unit, 2)
            out_ref[unit, 0] = done[b * ROWS : (b + 1) * ROWS, h * HEAD : (h + 1) * HEAD]
    else:
        out_ref[...] = done


def project_half(place, rows, gains, weight, before, units):
    parts = weight.shape[0]
    count = BATCH * ROWS
    acc = (parts, count, WIDTH)
    sq = (count, 128)
    last = before is not None
    acc_spec = pl.BlockSpec((1, count, WIDTH), lambda s, place: (s, 0, 0))
    in_specs = [whole(value.shape) for value in rows] + [
        pl.BlockSpec((CHIPS, 1, 1, WIDTH), lambda s, place: (0, place[0], 0, 0)),
        pl.BlockSpec((1, CHIPS, 1, WIDTH, WIDTH), lambda s, place: (s, 0, place[0], 0, 0)),
    ]
    scratch = [pltpu.VMEM((count, CHIPS * WIDTH), bf16)]
    if last:
        in_specs += [acc_spec, whole(sq)]
        scratch = [pltpu.VMEM(sq, f32)] + scratch
        if units:
            out = (UNITS, parts, ROWS, HEAD)
            out_specs = pl.BlockSpec((UNITS, 1, ROWS, HEAD), lambda s, place: (0, s, 0, 0))
        else:
            out = (count, WIDTH)
            out_specs = whole(out)
        out_shape = jax.ShapeDtypeStruct(out, bf16)
    else:
        out_specs = [acc_spec, whole(sq)]
        out_shape = [jax.ShapeDtypeStruct(acc, f32), jax.ShapeDtypeStruct(sq, f32)]
    return pl.pallas_call(
        functools.partial(project_kernel, last, units),
        grid_spec=pltpu.PrefetchScalarGridSpec(
            num_scalar_prefetch=1,
            grid=(parts,),
            in_specs=in_specs,
            out_specs=out_specs,
            scratch_shapes=scratch,
        ),
        out_shape=out_shape,
        compiler_params=params(),
        cost_estimate=pl.CostEstimate(
            flops=2 * count * (D // 2) * WIDTH * parts,
            bytes_accessed=D * WIDTH * parts + D * count + 4 * count * WIDTH * parts,
            transcendentals=0,
        ),
    )(
        place,
        *rows,
        gains.reshape(CHIPS, 2, 1, WIDTH),
        weight.reshape(parts, CHIPS, 2, WIDTH, WIDTH),
        *(before or ()),
    )


def project(places_both, same, swap, gains, weight, units):
    before = project_half(places_both[0], same, gains, weight, None, units)
    return project_half(places_both[1], swap, gains, weight, before, units)


def causal_kernel(triple_ref, out_ref):
    scaling = HEAD ** (-0.5)
    row = lax.broadcasted_iota(jnp.int32, (ROWS, ROWS), 0)
    col = lax.broadcasted_iota(jnp.int32, (ROWS, ROWS), 1)
    for i in range(UNITS):
        queries = triple_ref[i, 0]
        numer = jnp.zeros((ROWS, HEAD), f32)
        denom = jnp.zeros((ROWS, 1), f32)
        for j in range(i + 1):
            scores = lax.dot_general(
                queries, triple_ref[j, 1], (((1,), (1,)), ((), ())), preferred_element_type=f32
            )
            weights = jnp.exp(scores * scaling)
            if i == j:
                weights = jnp.where(col <= row, weights, 0.0)
            denom += jnp.sum(weights, axis=1, keepdims=True)
            numer += jnp.dot(weights.astype(bf16), triple_ref[j, 2], preferred_element_type=f32)
        out_ref[i] = (numer / denom).astype(bf16)


def causal(triple):
    out = (UNITS, ROWS, HEAD)
    return pl.pallas_call(
        causal_kernel,
        out_shape=jax.ShapeDtypeStruct(out, bf16),
        compiler_params=params(),
    )(triple)


def crossed_kernel(asked_ref, *refs):
    (prev_refs, pairs_refs), out_ref = (refs[0:2], refs[2:4]), refs[4]
    scaling = HEAD ** (-0.5)
    row = lax.broadcasted_iota(jnp.int32, (BLOCK, 2 * KEYS), 0)
    col = lax.broadcasted_iota(jnp.int32, (BLOCK, 2 * KEYS), 1)
    allowed = (row < BLOCK - 1) == (col < KEYS)
    for unit in range(UNITS):
        b, h = divmod(unit, 2)

        def both_blocks(i, cols):
            before = [ref[b, :, cols] if i == 0 else pair[b, i - 1, :, cols]
                      for ref, pair in zip(prev_refs, pairs_refs)]
            return jnp.concatenate(before + [pair[b, i, :, cols] for pair in pairs_refs], axis=0)

        for i in range(ROWS // BLOCK):
            queries = asked_ref[
                b * ROWS + i * BLOCK : b * ROWS + (i + 1) * BLOCK, h * HEAD : (h + 1) * HEAD
            ]
            keys = both_blocks(i, slice(h * HEAD, (h + 1) * HEAD))
            values = both_blocks(i, slice((2 + h) * HEAD, (3 + h) * HEAD))
            scores = lax.dot_general(
                queries, keys, (((1,), (1,)), ((), ())), preferred_element_type=f32
            )
            weights = jnp.where(allowed, jnp.exp(scores * scaling), 0.0)
            denom = jnp.sum(weights, axis=1, keepdims=True)
            numer = jnp.dot(weights.astype(bf16), values, preferred_element_type=f32)
            out_ref[unit, i * BLOCK : (i + 1) * BLOCK, :] = (numer / denom).astype(bf16)


def cross(asked, prevs, pairs):
    out = (UNITS, ROWS, HEAD)
    return pl.pallas_call(
        crossed_kernel,
        out_shape=jax.ShapeDtypeStruct(out, bf16),
        compiler_params=params(),
    )(asked, *prevs, *pairs)


def terms_kernel(place_ref, mixed_ref, *refs):
    w_refs, out_refs, left_ref = refs[: 2 * GROUP], refs[2 * GROUP : 2 * GROUP + 2], refs[-1]
    for unit in range(UNITS):
        b, h = divmod(unit, 2)
        left_ref[b * ROWS : (b + 1) * ROWS, h * HEAD : (h + 1) * HEAD] = mixed_ref[unit]
    for part in range(2):
        left = left_ref[STARTS[part] : STARTS[part] + PARTS[part], :]
        for at in range(GROUP):
            right = w_refs[part * GROUP + at][...]
            out_refs[part][at] = jnp.dot(left, right, preferred_element_type=f32).astype(bf16)


def terms(place, mixed, weight, high):
    count = BATCH * ROWS

    def columns(part, at):
        index = 1 + part * CHIPS + GROUP * high + at
        return pl.BlockSpec((WIDTH, WIDTH), lambda s, place: (0, 2 * place[index] + place[0]))

    shapes = [(GROUP, PARTS[part], WIDTH) for part in range(2)]
    return pl.pallas_call(
        terms_kernel,
        grid_spec=pltpu.PrefetchScalarGridSpec(
            num_scalar_prefetch=1,
            grid=(1,),
            in_specs=[whole((UNITS, ROWS, HEAD))]
            + [columns(part, at) for part in range(2) for at in range(GROUP)],
            out_specs=[whole(shape) for shape in shapes],
            scratch_shapes=[pltpu.VMEM((count, WIDTH), bf16)],
        ),
        out_shape=[jax.ShapeDtypeStruct(shape, bf16) for shape in shapes],
        compiler_params=params(8),
        cost_estimate=pl.CostEstimate(
            flops=2 * count * WIDTH * D // 4,
            bytes_accessed=D * WIDTH + D * count // 2,
            transcendentals=0,
        ),
    )(place, mixed, *([weight] * (2 * GROUP)))


def add_product(places_both, states, mixed, weight, side=()):
    low, got = scatter_sum(places_both, mixed, weight)
    *got, side = together(*got, side)
    total = [
        (state.astype(f32) + (mine + far.astype(f32))).astype(bf16)
        for state, mine, far in zip(states, low, got)
    ]
    return total, side


def by_parts(rows):
    return [rows[start : start + count] for start, count in zip(STARTS, PARTS)]


def look_up(ids, enc_embed, core, section):
    vocab_here = enc_embed.shape[0]
    mine = lax.dynamic_slice_in_dim(ids, section * (NB_LEN // 2), NB_LEN // 2, axis=1)
    wanted = mine.reshape(CHIPS, 2, NB_LEN // 2) - lax.axis_index(MP) * vocab_here

    def rows(at):
        picks = lax.dynamic_index_in_dim(wanted, at, 1, keepdims=False).reshape(-1)
        inside = (picks >= 0) & (picks < vocab_here)
        found = enc_embed[jnp.clip(picks, 0, vocab_here - 1)]
        found = jnp.where(inside[:, None], found, jnp.zeros((), bf16))
        return found.reshape(CHIPS, NB_LEN // 2, ENC_D)

    far = core_swap(rows(1 - core))
    return rows(core) + far


def join_halves(half, section):
    far = section_swap(half)
    return jnp.where(
        section == 0, jnp.concatenate([half, far], axis=0), jnp.concatenate([far, half], axis=0)
    )


def weight_parts(section, enc_qkv, enc_out, enc_up, enc_down):
    width = ENC_D // 2
    triple = lax.dynamic_slice_in_dim(enc_qkv, section * width, width, axis=2)
    up = enc_up.reshape(64, 16, 2, 2, 64)
    up = lax.dynamic_index_in_dim(up, section, 2, keepdims=False)
    up = jnp.transpose(up, (2, 0, 1, 3)).reshape(2, 64, 2, width)
    down = lax.dynamic_slice_in_dim(enc_down, section * 128, 128, axis=0)
    down = down.reshape(2, 64, 2, width)
    return jnp.concatenate(
        [
            jnp.transpose(up, (0, 2, 1, 3)).reshape(4, 64, width),
            jnp.transpose(down, (0, 2, 1, 3)).reshape(4, 64, width),
            jnp.transpose(triple, (1, 0, 2)),
            jnp.transpose(enc_out.reshape(64, 2, width), (1, 0, 2)),
        ],
        axis=0,
    )


def scaled_rows(values, gain):
    wide = values.astype(f32)
    root = jnp.sqrt(jnp.mean(wide * wide, axis=1, keepdims=True) + epsilon)
    return (wide * gain).astype(bf16), root


def enc_mix_kernel(section_ref, x_ref, gain_ref, q_ref, k_ref, v_ref, o0_ref, o1_ref, out_ref, mix_ref):
    scaled, root = scaled_rows(x_ref[...], gain_ref[...])
    triple = [
        (jnp.dot(scaled, ref[0], preferred_element_type=f32) / root).astype(bf16)
        for ref in (q_ref, k_ref, v_ref)
    ]
    for head in range(ENC_HEADS // 2):
        cols = slice(head * ENC_HEAD, (head + 1) * ENC_HEAD)
        scores = lax.dot_general(
            triple[0][:, cols],
            triple[1][:, cols],
            (((1,), (1,)), ((), ())),
            preferred_element_type=f32,
        )
        weights = jnp.exp(scores * ENC_HEAD ** (-0.5))
        denom = jnp.sum(weights, axis=1, keepdims=True)
        numer = jnp.dot(weights.astype(bf16), triple[2][:, cols], preferred_element_type=f32)
        mix_ref[:, cols] = (numer / denom).astype(bf16)
    mixed = mix_ref[...]
    width = ENC_D // 2
    rows = pl.ds(pl.multiple_of(section_ref[0] * width, width), width)
    for at, ref in enumerate((o0_ref, o1_ref)):
        part = jnp.dot(mixed, ref[0, rows, :], preferred_element_type=f32)
        out_ref[:, at * width : (at + 1) * width] = part.astype(bf16)


def enc_feed_kernel(x_ref, gain_ref, w_ref, out_ref):
    scaled, root = scaled_rows(x_ref[...], gain_ref[...])
    width = ENC_D // 2
    hidden = [
        jax.nn.gelu(
            jnp.dot(scaled, w_ref[piece], preferred_element_type=f32) / root, approximate=True
        ).astype(bf16)
        for piece in range(4)
    ]
    for at in range(2):
        part = jnp.zeros((NB_LEN, width), f32)
        for piece in range(4):
            rows = slice((piece % 2) * width, (piece % 2 + 1) * width)
            down = w_ref[4 + 2 * (piece // 2) + at, rows, :]
            part += jnp.dot(hidden[piece], down, preferred_element_type=f32)
        out_ref[:, at * width : (at + 1) * width] = part.astype(bf16)


def encode_mix(embedded, enc_norms, pieces, section):
    out = jax.ShapeDtypeStruct((NB_LEN, ENC_D), bf16)
    width = ENC_D // 2
    full = whole((NB_LEN, ENC_D))

    def piece(at):
        return pl.BlockSpec((1, ENC_D, width), lambda s: (at, 0, 0))

    mixed = pl.pallas_call(
        enc_mix_kernel,
        grid=(1,),
        in_specs=[SCALAR, full, whole((1, ENC_D))] + [piece(8 + at) for at in range(5)],
        out_specs=full,
        out_shape=out,
        scratch_shapes=[pltpu.VMEM((NB_LEN, width), bf16)],
        compiler_params=params(),
    )(section, embedded, enc_norms[:1], *([pieces] * 5))
    return embedded, mixed, section_swap(mixed)


def encode_feed(embedded, mixed, far, enc_norms, pieces):
    width = ENC_D // 2
    full = whole((NB_LEN, ENC_D))
    inner = (embedded.astype(f32) + (mixed.astype(f32) + far.astype(f32))).astype(bf16)
    fed = pl.pallas_call(
        enc_feed_kernel,
        grid=(1,),
        in_specs=[full, whole((1, ENC_D)), pl.BlockSpec((8, ENC_D, width), lambda s: (0, 0, 0))],
        out_specs=full,
        out_shape=jax.ShapeDtypeStruct((NB_LEN, ENC_D), bf16),
        compiler_params=params(28),
    )(inner, enc_norms[1:], pieces)
    return inner, fed, section_swap(fed)


def encode_end(inner, fed, far):
    return (inner.astype(f32) + (fed.astype(f32) + far.astype(f32))).astype(bf16)


def pairs_kernel(place_ref, *refs):
    x_refs, (w_ref, out_ref, left_ref) = refs[:4], refs[4:]
    for part in range(2):
        for block in range(CHIPS):
            chip = place_ref[1 + part * CHIPS + block]
            start = pl.multiple_of(chip * NB_LEN + ENC_STARTS[part], 16)
            value = x_refs[part + 2 * (block // 4)][block % 4]
            left_ref[pl.ds(start, ENC_PARTS[part]), :] = value
    out_ref[...] = jnp.dot(left_ref[...], w_ref[...], preferred_element_type=f32).astype(bf16)


def make_pairs(place, rows, weight):
    out = (CHIPS * NB_LEN, 2 * WIDTH)
    pairs = pl.pallas_call(
        pairs_kernel,
        grid_spec=pltpu.PrefetchScalarGridSpec(
            num_scalar_prefetch=1,
            grid=(1,),
            in_specs=[whole(value.shape) for value in rows] + [whole(weight.shape)],
            out_specs=whole(out),
            scratch_shapes=[pltpu.VMEM((CHIPS * NB_LEN, ENC_D), bf16)],
        ),
        out_shape=jax.ShapeDtypeStruct(out, bf16),
        compiler_params=params(20),
        cost_estimate=pl.CostEstimate(
            flops=2 * CHIPS * NB_LEN * ENC_D * 2 * WIDTH,
            bytes_accessed=2 * (CHIPS * NB_LEN + 2 * WIDTH) * ENC_D,
            transcendentals=0,
        ),
    )(place, *rows, weight)
    pairs = pairs.reshape(BATCH, CHIPS // BATCH, NB_LEN, 2 * WIDTH)
    count = lax.axis_size("seq")
    prev = lax.ppermute(pairs[:, -1], "seq", [(i, i + 1) for i in range(count - 1)])
    return prev, pairs


def attention(triple):
    triple = lax.all_to_all(triple, "seq", 0, 0, tiled=True)
    return lax.all_to_all(causal(triple), "seq", 0, 0, tiled=True)


def first_layer(places_both, states, weights, found, local, join, encoder):
    norms, triple_w, out_w, query_w, back_w = weights
    same, local = together(chips_to_chips(spread(states)), local)
    pieces = lax.all_gather(local, MP, axis=1, tiled=True)
    same, found = together(same, found)
    half = jnp.sum(chips_to_chips(found).astype(f32), axis=0).astype(bf16)
    triple = project(places_both, [same], [core_swap(same)], norms[0], triple_w, True)
    triple, half = together(triple, half)
    mixed = attention(triple)
    middle, embedded = add_product(places_both, states, mixed, out_w, join(half))
    rows, embedded = together(spread(middle), embedded)
    same = chips_to_chips(rows)
    encoded = encoder(embedded, pieces)
    parts = [encoded[start : start + count] for start, count in zip(ENC_STARTS, ENC_PARTS)]
    *got, same = together(*first_round(parts), same)
    asked = project(places_both, [same], [core_swap(same)], norms[1], query_w[None], False)
    return middle, asked, later_rounds(parts, got)


def second_layer(places_both, states, weights):
    norms, triple_w, out_w, query_w, back_w = weights
    triple = project(places_both, *gather_chips(states), norms[0], triple_w, True)
    middle, _ = add_product(places_both, states, attention(triple), out_w)
    asked = project(places_both, *gather_chips(middle), norms[1], query_w[None], False)
    return middle, asked


def cross_layer(places_both, middle, asked, prevs, pairs, weights):
    crossed = cross(asked, prevs, pairs)
    return add_product(places_both, middle, crossed, weights[4])[0]


def on_device(
    hidden_states,
    neighbour_ids,
    neighbour_table,
    enc_embed,
    enc_norms,
    enc_qkv,
    enc_out,
    enc_up,
    enc_down,
    dec_norms,
    dec_qkv,
    dec_out,
    cross_query,
    cross_pair,
    cross_out,
):
    section = lax.axis_index("section").astype(jnp.int32)
    core_at = lax.axis_index("core").astype(jnp.int32)
    chip = lax.axis_index(("z", "y")).astype(jnp.int32)
    places_both = [places(chip, core_at), places(chip, 1 - core_at)]
    local = weight_parts(section, enc_qkv, enc_out, enc_up, enc_down)
    slot_ids = neighbour_ids[neighbour_table.reshape(-1)]
    found = look_up(slot_ids, enc_embed, core_at, section)
    pair_w = cross_pair[0].reshape(ENC_D, 2 * WIDTH)

    def join(half):
        return join_halves(half, section)

    def encoder(embedded, pieces):
        mix = encode_mix(embedded, enc_norms, pieces, jnp.reshape(section, (1,)))
        return encode_end(*encode_feed(*mix, enc_norms, pieces))

    weights = (
        dec_norms[0],
        jnp.transpose(dec_qkv[0], (1, 0, 2)),
        dec_out[0],
        cross_query[0],
        cross_out[0],
    )

    states = hidden_states.reshape(BATCH * ROWS, WIDTH)
    middle, asked, encoded = first_layer(
        places_both, by_parts(states), weights, found, local, join, encoder
    )
    made = [make_pairs(place, rows, pair_w) for place, rows in zip(places_both, encoded)]
    prevs, pairs = [prev for prev, _ in made], [rows for _, rows in made]
    first = cross_layer(places_both, middle, asked, prevs, pairs, weights)
    handed = section_swap(jnp.concatenate(first))
    middle, asked = second_layer(places_both, by_parts(handed), weights)
    second = jnp.concatenate(cross_layer(places_both, middle, asked, prevs, pairs, weights))
    second = second.reshape(BATCH, ROWS, WIDTH)
    return jnp.where(section == 0, section_swap(second[0]), second[1])[None]


def solution(mesh):
    devices = mesh.devices
    sections, seqs = devices.shape[:2]
    split = Mesh(
        devices.reshape(sections, seqs, 2, 4, 2), ("section", "seq", "z", "y", "core")
    )
    mp = ("z", "y", "core")
    return jax.shard_map(
        on_device,
        mesh=split,
        in_specs=(
            P(None, "seq", mp),
            P(),
            P(None, "seq", None),
            P(mp, None),
            P(),
            P(mp, None, None),
            P(mp, None),
            P(mp, None),
            P(mp, None),
            P("section", None, None),
            P("section", None, None, mp),
            P("section", mp, None),
            P("section", None, mp),
            P("section", None, None, mp),
            P("section", mp, None),
        ),
        out_specs=P("section", "seq", mp),
        check_vma=False,
    )
```

```python
import functools

import jax
import jax.numpy as jnp
import numpy as np
from jax import lax
from jax.experimental import pallas as pl
from jax.experimental.pallas import tpu as pltpu
from jax.sharding import Mesh, PartitionSpec as P

D = 4096
HEAD = 128
ENC_D = 1024
ENC_HEADS = 16
ENC_HEAD = 64
BLOCK = 64
NB_LEN = 128
NEIGH = 2
BATCH = 2
CHIPS = 8
ROWS = 256
WIDTH = 256
UNITS = 4
GROUP = 4
MP = ("z", "y", "core")
KEYS = NEIGH * NB_LEN

epsilon = 1e-05
f32 = jnp.float32
bf16 = jnp.bfloat16


def params(mebibytes=16):
    return pltpu.CompilerParams(vmem_limit_bytes=mebibytes * 1024 * 1024)


def whole(shape):
    return pl.BlockSpec(shape, lambda *_: (0,) * len(shape))


SCALAR = pl.BlockSpec(memory_space=pltpu.SMEM)


PARTS = (352, 160)
STARTS = (0, 352)
ENC_PARTS = (80, 48)
ENC_STARTS = (0, 80)
PIECE = 512
MASKS = (((4, 1, 3), (1, 3, 4)), ((3, 4, 1), (3, 4, 1)))


def block_offsets(masks):
    return [
        (masks[0] * (b & 1)) ^ (masks[1] * (b >> 1 & 1)) ^ (masks[2] * (b >> 2 & 1))
        for b in range(CHIPS)
    ]


OFFSETS = np.array([[block_offsets(m) for m in part] for part in MASKS], np.int32)


def core_swap(value):
    return lax.ppermute(value, "core", [(0, 1), (1, 0)])


def section_swap(value):
    return lax.ppermute(value, "section", [(0, 1), (1, 0)])


def chips_to_chips(value):
    return lax.all_to_all(value, ("z", "y"), 0, 0, tiled=True)


def neighbour(value, part, turn):
    route = [
        (2 * chip + core, 2 * (chip ^ MASKS[part][core][turn]) + core)
        for chip in range(CHIPS)
        for core in range(2)
    ]
    return lax.ppermute(value, MP, route)


def places(chip, pick):
    offsets = lax.dynamic_index_in_dim(jnp.asarray(OFFSETS), pick, 1, keepdims=False)
    return jnp.concatenate([jnp.reshape(pick, (1,)), (chip ^ offsets).reshape(-1)]).astype(
        jnp.int32
    )


def together(*values):
    return lax.optimization_barrier(values)


def first_round(local):
    return [neighbour(value, part, 0) for part, value in enumerate(local)]


def later_rounds(local, got):
    near = [jnp.stack(pair) for pair in zip(local, got)]
    got = together(*[neighbour(value, part, 1) for part, value in enumerate(near)])
    near = [jnp.concatenate(pair) for pair in zip(near, got)]
    swaps = [core_swap(value) for value in near]
    far = [neighbour(value, part, 2) for part, value in enumerate(near)]
    swaps = list(together(*swaps))
    far = list(together(*far))
    return near + far, swaps + [core_swap(value) for value in far]


def gather_chips(local):
    return later_rounds(local, together(*first_round(local)))


def scatter_sum(places_both, mixed, weight):
    own, other = places_both
    other_far = [core_swap(value) for value in terms(other, mixed, weight, 1)]
    other_near = [core_swap(value) for value in terms(other, mixed, weight, 0)]
    own_far = terms(own, mixed, weight, 1)
    own_near = terms(own, mixed, weight, 0)
    other_far = together(*other_far)
    sums = [
        (mine.astype(f32) + got.astype(f32)).astype(bf16)
        for mine, got in zip(own_far, other_far)
    ]
    got = together(*[neighbour(sums[part], part, 2) for part in range(2)], *other_near)
    low = [
        own_near[part].astype(f32) + got[2 + part].astype(f32) + got[part].astype(f32)
        for part in range(2)
    ]
    got = together(*[neighbour(low[part][2:].astype(bf16), part, 1) for part in range(2)])
    low = [low[part][:2] + got[part].astype(f32) for part in range(2)]
    got = [neighbour(low[part][1].astype(bf16), part, 0) for part in range(2)]
    return [low[part][0] for part in range(2)], got


def project_kernel(last, units, place_ref, *refs):
    whole_rows = len(refs) == (8 if last else 6)
    count = 1 if whole_rows else 4
    x_refs, (gain_ref, w_ref), refs = refs[:count], refs[count : count + 2], refs[count + 2 :]
    if last:
        acc_in, sq_in, out_ref, sq_ref, left_ref = refs
    else:
        acc_ref, sq_ref, left_ref = refs
    step = pl.program_id(0)

    def place_rows(rows, blocks):
        total = sq_in[rows, :] if last else jnp.zeros((rows.stop - rows.start, 128), f32)
        for block, chip in blocks:
            wide = block.astype(f32)
            squares = wide * wide
            total += squares[:, :128] + squares[:, 128:]
            cols = pl.ds(pl.multiple_of(chip * WIDTH, WIDTH), WIDTH)
            left_ref[rows, cols] = (wide * gain_ref[chip, 0]).astype(bf16)
        sq_ref[rows, :] = total

    @pl.when(step == 0)
    def _():
        for part in range(2):
            rows = slice(STARTS[part], STARTS[part] + PARTS[part])
            if whole_rows:
                blocks = [(x_refs[0][chip, rows, :], chip) for chip in range(CHIPS)]
            else:
                blocks = [
                    (
                        x_refs[part + 2 * (block // 4)][block % 4],
                        place_ref[1 + part * CHIPS + block],
                    )
                    for block in range(CHIPS)
                ]
            place_rows(rows, blocks)

    right = w_ref[0].reshape(CHIPS * WIDTH, WIDTH)
    product = jnp.dot(left_ref[...], right, preferred_element_type=f32)
    if not last:
        acc_ref[0] = product
        return
    mean = jnp.sum(sq_ref[...], axis=1, keepdims=True) / D
    done = ((acc_in[0] + product) / jnp.sqrt(mean + epsilon)).astype(bf16)
    if units:
        for unit in range(UNITS):
            b, h = divmod(unit, 2)
            out_ref[unit, 0] = done[b * ROWS : (b + 1) * ROWS, h * HEAD : (h + 1) * HEAD]
    else:
        out_ref[...] = done


def project_half(place, rows, gains, weight, before, units):
    parts = weight.shape[0]
    count = BATCH * ROWS
    acc = (parts, count, WIDTH)
    sq = (count, 128)
    last = before is not None
    acc_spec = pl.BlockSpec((1, count, WIDTH), lambda s, place: (s, 0, 0))
    in_specs = [whole(value.shape) for value in rows] + [
        pl.BlockSpec((CHIPS, 1, 1, WIDTH), lambda s, place: (0, place[0], 0, 0)),
        pl.BlockSpec((1, CHIPS, 1, WIDTH, WIDTH), lambda s, place: (s, 0, place[0], 0, 0)),
    ]
    scratch = [pltpu.VMEM((count, CHIPS * WIDTH), bf16)]
    if last:
        in_specs += [acc_spec, whole(sq)]
        scratch = [pltpu.VMEM(sq, f32)] + scratch
        if units:
            out = (UNITS, parts, ROWS, HEAD)
            out_specs = pl.BlockSpec((UNITS, 1, ROWS, HEAD), lambda s, place: (0, s, 0, 0))
        else:
            out = (count, WIDTH)
            out_specs = whole(out)
        out_shape = jax.ShapeDtypeStruct(out, bf16)
    else:
        out_specs = [acc_spec, whole(sq)]
        out_shape = [jax.ShapeDtypeStruct(acc, f32), jax.ShapeDtypeStruct(sq, f32)]
    return pl.pallas_call(
        functools.partial(project_kernel, last, units),
        grid_spec=pltpu.PrefetchScalarGridSpec(
            num_scalar_prefetch=1,
            grid=(parts,),
            in_specs=in_specs,
            out_specs=out_specs,
            scratch_shapes=scratch,
        ),
        out_shape=out_shape,
        compiler_params=params(),
        cost_estimate=pl.CostEstimate(
            flops=2 * count * (D // 2) * WIDTH * parts,
            bytes_accessed=D * WIDTH * parts + D * count + 4 * count * WIDTH * parts,
            transcendentals=0,
        ),
    )(
        place,
        *rows,
        gains.reshape(CHIPS, 2, 1, WIDTH),
        weight.reshape(parts, CHIPS, 2, WIDTH, WIDTH),
        *(before or ()),
    )


def project(places_both, same, swap, gains, weight, units):
    before = project_half(places_both[0], same, gains, weight, None, units)
    return project_half(places_both[1], swap, gains, weight, before, units)


def causal_kernel(triple_ref, out_ref):
    scaling = HEAD ** (-0.5)
    row = lax.broadcasted_iota(jnp.int32, (ROWS, ROWS), 0)
    col = lax.broadcasted_iota(jnp.int32, (ROWS, ROWS), 1)
    for i in range(UNITS):
        queries = triple_ref[i, 0]
        numer = jnp.zeros((ROWS, HEAD), f32)
        denom = jnp.zeros((ROWS, 1), f32)
        for j in range(i + 1):
            scores = lax.dot_general(
                queries, triple_ref[j, 1], (((1,), (1,)), ((), ())), preferred_element_type=f32
            )
            weights = jnp.exp(scores * scaling)
            if i == j:
                weights = jnp.where(col <= row, weights, 0.0)
            denom += jnp.sum(weights, axis=1, keepdims=True)
            numer += jnp.dot(weights.astype(bf16), triple_ref[j, 2], preferred_element_type=f32)
        out_ref[i] = (numer / denom).astype(bf16)


def causal(triple):
    out = (UNITS, ROWS, HEAD)
    return pl.pallas_call(
        causal_kernel,
        out_shape=jax.ShapeDtypeStruct(out, bf16),
        compiler_params=params(),
    )(triple)


def crossed_kernel(asked_ref, *refs):
    (prev_refs, pairs_refs), out_ref = (refs[0:2], refs[2:4]), refs[4]
    scaling = HEAD ** (-0.5)
    row = lax.broadcasted_iota(jnp.int32, (BLOCK, 2 * KEYS), 0)
    col = lax.broadcasted_iota(jnp.int32, (BLOCK, 2 * KEYS), 1)
    allowed = (row < BLOCK - 1) == (col < KEYS)
    for unit in range(UNITS):
        b, h = divmod(unit, 2)

        def both_blocks(i, cols):
            before = [ref[b, :, cols] if i == 0 else pair[b, i - 1, :, cols]
                      for ref, pair in zip(prev_refs, pairs_refs)]
            return jnp.concatenate(before + [pair[b, i, :, cols] for pair in pairs_refs], axis=0)

        for i in range(ROWS // BLOCK):
            queries = asked_ref[
                b * ROWS + i * BLOCK : b * ROWS + (i + 1) * BLOCK, h * HEAD : (h + 1) * HEAD
            ]
            keys = both_blocks(i, slice(h * HEAD, (h + 1) * HEAD))
            values = both_blocks(i, slice((2 + h) * HEAD, (3 + h) * HEAD))
            scores = lax.dot_general(
                queries, keys, (((1,), (1,)), ((), ())), preferred_element_type=f32
            )
            weights = jnp.where(allowed, jnp.exp(scores * scaling), 0.0)
            denom = jnp.sum(weights, axis=1, keepdims=True)
            numer = jnp.dot(weights.astype(bf16), values, preferred_element_type=f32)
            out_ref[unit, i * BLOCK : (i + 1) * BLOCK, :] = (numer / denom).astype(bf16)


def cross(asked, prevs, pairs):
    out = (UNITS, ROWS, HEAD)
    return pl.pallas_call(
        crossed_kernel,
        out_shape=jax.ShapeDtypeStruct(out, bf16),
        compiler_params=params(),
    )(asked, *prevs, *pairs)


def terms_kernel(place_ref, mixed_ref, *refs):
    w_refs, out_refs, left_ref = refs[: 2 * GROUP], refs[2 * GROUP : 2 * GROUP + 2], refs[-1]
    for unit in range(UNITS):
        b, h = divmod(unit, 2)
        left_ref[b * ROWS : (b + 1) * ROWS, h * HEAD : (h + 1) * HEAD] = mixed_ref[unit]
    for part in range(2):
        left = left_ref[STARTS[part] : STARTS[part] + PARTS[part], :]
        for at in range(GROUP):
            right = w_refs[part * GROUP + at][...]
            out_refs[part][at] = jnp.dot(left, right, preferred_element_type=f32).astype(bf16)


def terms(place, mixed, weight, high):
    count = BATCH * ROWS

    def columns(part, at):
        index = 1 + part * CHIPS + GROUP * high + at
        return pl.BlockSpec((WIDTH, WIDTH), lambda s, place: (0, 2 * place[index] + place[0]))

    shapes = [(GROUP, PARTS[part], WIDTH) for part in range(2)]
    return pl.pallas_call(
        terms_kernel,
        grid_spec=pltpu.PrefetchScalarGridSpec(
            num_scalar_prefetch=1,
            grid=(1,),
            in_specs=[whole((UNITS, ROWS, HEAD))]
            + [columns(part, at) for part in range(2) for at in range(GROUP)],
            out_specs=[whole(shape) for shape in shapes],
            scratch_shapes=[pltpu.VMEM((count, WIDTH), bf16)],
        ),
        out_shape=[jax.ShapeDtypeStruct(shape, bf16) for shape in shapes],
        compiler_params=params(8),
        cost_estimate=pl.CostEstimate(
            flops=2 * count * WIDTH * D // 4,
            bytes_accessed=D * WIDTH + D * count // 2,
            transcendentals=0,
        ),
    )(place, mixed, *([weight] * (2 * GROUP)))


def add_product(places_both, states, mixed, weight, side=()):
    low, got = scatter_sum(places_both, mixed, weight)
    *got, side = together(*got, side)
    total = [
        (state.astype(f32) + (mine + far.astype(f32))).astype(bf16)
        for state, mine, far in zip(states, low, got)
    ]
    return total, side


def by_parts(rows):
    return [rows[start : start + count] for start, count in zip(STARTS, PARTS)]


def looked_up(own, other):
    total = own + core_swap(other)
    total = total[:4] + neighbour(total[4:], 0, 2)
    total = total[:2] + neighbour(total[2:], 0, 1)
    return total[0] + neighbour(total[1], 0, 0)


def weight_parts(enc_qkv, enc_out, enc_up, enc_down):
    up = enc_up.reshape(64, 16, 2, 2, 64)
    up = jnp.transpose(up, (2, 3, 0, 1, 4)).reshape(2, 2, 64, 2, PIECE)
    up = jnp.transpose(up, (0, 1, 3, 2, 4)).reshape(2, 4, 64, PIECE)
    down = enc_down.reshape(2, 2, 64, 2, PIECE)
    down = jnp.transpose(down, (0, 1, 3, 2, 4)).reshape(2, 4, 64, PIECE)
    triple = jnp.transpose(enc_qkv.reshape(64, 3, 2, PIECE), (2, 1, 0, 3)).reshape(6, 64, PIECE)
    out = jnp.transpose(enc_out.reshape(64, 2, PIECE), (1, 0, 2))
    feed = jnp.concatenate([up, down], axis=1).reshape(16, 64, PIECE)
    return [feed, jnp.concatenate([triple, out], axis=0)]


def assemble(place_refs, refs, part, piece, w_ref):
    for place_ref, (near, far) in zip(place_refs, (refs[:2], refs[2:])):
        for block in range(CHIPS):
            chip = place_ref[1 + part * CHIPS + block]
            start = pl.multiple_of((2 * chip + place_ref[0]) * 64, 64)
            w_ref[pl.ds(start, 64), :] = (near if block < 4 else far)[block % 4, piece]


def scaled_rows(values, gain):
    wide = values.astype(f32)
    root = jnp.sqrt(jnp.mean(wide * wide, axis=1, keepdims=True) + epsilon)
    return (wide * gain).astype(bf16), root


def enc_mix_kernel(own_ref, other_ref, x_ref, gain_ref, *refs):
    blocks, (out_ref, w_ref, mix_ref) = refs[:4], refs[4:]
    places_both = (own_ref, other_ref)
    for piece in range(8):
        assemble(places_both, blocks, 1, piece, w_ref.at[piece])
    scaled, root = scaled_rows(x_ref[...], gain_ref[...])
    for half in range(2):
        triple = []
        for part in range(3):
            product = jnp.dot(scaled, w_ref[3 * half + part], preferred_element_type=f32)
            triple.append((product / root).astype(bf16))
        for head in range(ENC_HEADS // 2):
            cols = slice(head * ENC_HEAD, (head + 1) * ENC_HEAD)
            scores = lax.dot_general(
                triple[0][:, cols],
                triple[1][:, cols],
                (((1,), (1,)), ((), ())),
                preferred_element_type=f32,
            )
            weights = jnp.exp(scores * ENC_HEAD ** (-0.5))
            denom = jnp.sum(weights, axis=1, keepdims=True)
            numer = jnp.dot(weights.astype(bf16), triple[2][:, cols], preferred_element_type=f32)
            start = half * PIECE + head * ENC_HEAD
            mix_ref[:, start : start + ENC_HEAD] = (numer / denom).astype(bf16)
    mixed = mix_ref[...]
    for at in range(2):
        cols = slice(at * PIECE, (at + 1) * PIECE)
        product = jnp.dot(mixed, w_ref[6 + at], preferred_element_type=f32)
        out_ref[:, cols] = (x_ref[:, cols].astype(f32) + product).astype(bf16)


def enc_feed_kernel(own_ref, other_ref, x_ref, gain_ref, *refs):
    blocks, (out_ref, w_ref, acc_ref) = refs[:4], refs[4:]
    places_both = (own_ref, other_ref)
    for piece in range(8):
        assemble(places_both, blocks, 0, piece, w_ref.at[piece])
    scaled, root = scaled_rows(x_ref[...], gain_ref[...])

    @pl.when(pl.program_id(0) == 0)
    def _():
        acc_ref[...] = x_ref[...].astype(f32)

    for row in range(2):
        hidden = []
        for piece in range(2):
            product = jnp.dot(scaled, w_ref[2 * row + piece], preferred_element_type=f32)
            hidden.append(jax.nn.gelu(product / root, approximate=True).astype(bf16))
        hidden = jnp.concatenate(hidden, axis=1)
        for at in range(2):
            cols = slice(at * PIECE, (at + 1) * PIECE)
            right = w_ref[4 + 2 * row + at]
            acc_ref[:, cols] += jnp.dot(hidden, right, preferred_element_type=f32)

    @pl.when(pl.program_id(0) == 1)
    def _():
        out_ref[...] = acc_ref[...].astype(bf16)


def encode(places_both, embedded, enc_norms, feed, mix):
    out = jax.ShapeDtypeStruct((NB_LEN, ENC_D), bf16)
    full = whole((NB_LEN, ENC_D))
    gain = whole((1, ENC_D))

    def call(kernel, steps, pieces, scratch, x, gains, rows):
        block = (4, rows[0].shape[1] // steps, 64, PIECE)
        return pl.pallas_call(
            kernel,
            grid_spec=pltpu.PrefetchScalarGridSpec(
                num_scalar_prefetch=2,
                grid=(steps,),
                in_specs=[full, gain]
                + [pl.BlockSpec(block, lambda s, *_: (0, s, 0, 0)) for _ in rows],
                out_specs=full,
                scratch_shapes=[pltpu.VMEM((pieces, ENC_D, PIECE), bf16), scratch],
            ),
            out_shape=out,
            compiler_params=params(40),
        )(*places_both, x, gains, *rows)

    inner = call(
        enc_mix_kernel, 1, 8, pltpu.VMEM((NB_LEN, ENC_D), bf16), embedded, enc_norms[:1], mix
    )
    return call(
        enc_feed_kernel, 2, 8, pltpu.VMEM((NB_LEN, ENC_D), f32), inner, enc_norms[1:], feed
    )


def encode_neighbour(places_both, ids, enc_embed, enc_norms, local):
    vocab_here = enc_embed.shape[0]
    wanted = ids - lax.axis_index(MP) * vocab_here

    def rows(place, wanted):
        picks = wanted[2 * place[1 : 1 + CHIPS] + place[0]].reshape(-1)
        inside = (picks >= 0) & (picks < vocab_here)
        found = enc_embed[jnp.clip(picks, 0, vocab_here - 1)]
        found = jnp.where(inside[:, None], found, jnp.zeros((), bf16))
        return found.reshape(CHIPS, NB_LEN, ENC_D)

    other = rows(places_both[1], wanted)
    *got, other, wanted = together(*first_round(local), other, wanted)
    near = [jnp.stack(pair) for pair in zip(local, got)]
    own = rows(places_both[0], wanted)
    *got, own = together(*[neighbour(value, part, 1) for part, value in enumerate(near)], own)
    near = [jnp.concatenate(pair) for pair in zip(near, got)]
    far = [neighbour(value, part, 2) for part, value in enumerate(near)]
    swaps = [core_swap(value) for value in near]
    *far, embedded = together(*far, looked_up(own, other))
    far_swaps = [core_swap(value) for value in far]
    feed, mix = [
        [near[part], far[part], swaps[part], far_swaps[part]] for part in range(2)
    ]
    return encode(places_both, embedded, enc_norms, feed, mix)


def pairs_kernel(place_ref, *refs):
    x_refs, (w_ref, out_ref, left_ref) = refs[:4], refs[4:]
    for part in range(2):
        for block in range(CHIPS):
            chip = place_ref[1 + part * CHIPS + block]
            start = pl.multiple_of(chip * NB_LEN + ENC_STARTS[part], 16)
            value = x_refs[part + 2 * (block // 4)][block % 4]
            left_ref[pl.ds(start, ENC_PARTS[part]), :] = value
    out_ref[...] = jnp.dot(left_ref[...], w_ref[...], preferred_element_type=f32).astype(bf16)


def make_pairs(place, rows, weight):
    out = (CHIPS * NB_LEN, 2 * WIDTH)
    pairs = pl.pallas_call(
        pairs_kernel,
        grid_spec=pltpu.PrefetchScalarGridSpec(
            num_scalar_prefetch=1,
            grid=(1,),
            in_specs=[whole(value.shape) for value in rows] + [whole(weight.shape)],
            out_specs=whole(out),
            scratch_shapes=[pltpu.VMEM((CHIPS * NB_LEN, ENC_D), bf16)],
        ),
        out_shape=jax.ShapeDtypeStruct(out, bf16),
        compiler_params=params(20),
        cost_estimate=pl.CostEstimate(
            flops=2 * CHIPS * NB_LEN * ENC_D * 2 * WIDTH,
            bytes_accessed=2 * (CHIPS * NB_LEN + 2 * WIDTH) * ENC_D,
            transcendentals=0,
        ),
    )(place, *rows, weight)
    pairs = pairs.reshape(BATCH, CHIPS // BATCH, NB_LEN, 2 * WIDTH)
    count = lax.axis_size("seq")
    prev = lax.ppermute(pairs[:, -1], "seq", [(i, i + 1) for i in range(count - 1)])
    return prev, pairs


def attention(triple):
    triple = lax.all_to_all(triple, "seq", 0, 0, tiled=True)
    return lax.all_to_all(causal(triple), "seq", 0, 0, tiled=True)


def to_queries(places_both, states, weights):
    norms, triple_w, out_w, query_w, back_w = weights
    triple = project(places_both, *gather_chips(states), norms[0], triple_w, True)
    middle, _ = add_product(places_both, states, attention(triple), out_w)
    asked = project(places_both, *gather_chips(middle), norms[1], query_w[None], False)
    return middle, asked


def cross_layer(places_both, middle, asked, prevs, pairs, weights):
    crossed = cross(asked, prevs, pairs)
    return add_product(places_both, middle, crossed, weights[4])[0]


def on_device(
    hidden_states,
    neighbour_ids,
    neighbour_table,
    enc_embed,
    enc_norms,
    enc_qkv,
    enc_out,
    enc_up,
    enc_down,
    dec_norms,
    dec_qkv,
    dec_out,
    cross_query,
    cross_pair,
    cross_out,
):
    section = lax.axis_index("section").astype(jnp.int32)
    core_at = lax.axis_index("core").astype(jnp.int32)
    chip = lax.axis_index(("z", "y")).astype(jnp.int32)
    places_both = [places(chip, core_at), places(chip, 1 - core_at)]
    slot_ids = neighbour_ids[neighbour_table.reshape(-1)]
    pair_w = cross_pair[0].reshape(ENC_D, 2 * WIDTH)
    weights = (
        dec_norms[0],
        jnp.transpose(dec_qkv[0], (1, 0, 2)),
        dec_out[0],
        cross_query[0],
        cross_out[0],
    )

    states = hidden_states.reshape(BATCH * ROWS, WIDTH)

    def decode():
        middle, asked = to_queries(places_both, by_parts(states), weights)
        return jnp.concatenate(middle), asked, jnp.zeros((NB_LEN, ENC_D), bf16)

    def encode_all():
        local = weight_parts(enc_qkv, enc_out, enc_up, enc_down)
        blank = jnp.zeros(states.shape, bf16)
        return blank, blank, encode_neighbour(places_both, slot_ids, enc_embed, enc_norms, local)

    middle, asked, encoded = lax.cond(section == 0, decode, encode_all)
    middle = by_parts(middle)
    encoded = jnp.where(section == 0, section_swap(encoded), encoded)
    encoded = gather_chips(
        [encoded[start : start + count] for start, count in zip(ENC_STARTS, ENC_PARTS)]
    )
    made = [make_pairs(place, rows, pair_w) for place, rows in zip(places_both, encoded)]
    prevs, pairs = [prev for prev, _ in made], [rows for _, rows in made]
    first = cross_layer(places_both, middle, asked, prevs, pairs, weights)
    handed = section_swap(jnp.concatenate(first))
    middle, asked = to_queries(places_both, by_parts(handed), weights)
    second = jnp.concatenate(cross_layer(places_both, middle, asked, prevs, pairs, weights))
    second = second.reshape(BATCH, ROWS, WIDTH)
    return jnp.where(section == 0, section_swap(second[0]), second[1])[None]


def solution(mesh):
    devices = mesh.devices
    sections, seqs = devices.shape[:2]
    split = Mesh(
        devices.reshape(sections, seqs, 2, 4, 2), ("section", "seq", "z", "y", "core")
    )
    mp = ("z", "y", "core")
    return jax.shard_map(
        on_device,
        mesh=split,
        in_specs=(
            P(None, "seq", mp),
            P(),
            P(None, "seq", None),
            P(mp, None),
            P(),
            P(mp, None, None),
            P(mp, None),
            P(mp, None),
            P(mp, None),
            P("section", None, None),
            P("section", None, None, mp),
            P("section", mp, None),
            P("section", None, mp),
            P("section", None, None, mp),
            P("section", mp, None),
        ),
        out_specs=P("section", "seq", mp),
        check_vma=False,
    )
```

```python
import functools

import jax
import jax.numpy as jnp
import numpy as np
from jax import lax
from jax.experimental import pallas as pl
from jax.experimental.pallas import tpu as pltpu
from jax.sharding import Mesh, PartitionSpec as P

D = 4096
HEAD = 128
ENC_D = 1024
ENC_HEADS = 16
ENC_HEAD = 64
BLOCK = 64
NB_LEN = 128
NEIGH = 2
BATCH = 2
CHIPS = 8
ROWS = 256
WIDTH = 256
UNITS = 4
GROUP = 4
MP = ("z", "y", "core")
KEYS = NEIGH * NB_LEN

epsilon = 1e-05
f32 = jnp.float32
bf16 = jnp.bfloat16


def params(mebibytes=16):
    return pltpu.CompilerParams(vmem_limit_bytes=mebibytes * 1024 * 1024)


def whole(shape):
    return pl.BlockSpec(shape, lambda *_: (0,) * len(shape))


SCALAR = pl.BlockSpec(memory_space=pltpu.SMEM)


PARTS = (352, 160)
STARTS = (0, 352)
ENC_PARTS = (80, 48)
ENC_STARTS = (0, 80)
PIECE = 512
MASKS = (((4, 1, 3), (1, 3, 4)), ((3, 4, 1), (3, 4, 1)))


def block_offsets(masks):
    return [
        (masks[0] * (b & 1)) ^ (masks[1] * (b >> 1 & 1)) ^ (masks[2] * (b >> 2 & 1))
        for b in range(CHIPS)
    ]


OFFSETS = np.array([[block_offsets(m) for m in part] for part in MASKS], np.int32)


def core_swap(value):
    return lax.ppermute(value, "core", [(0, 1), (1, 0)])


def section_swap(value):
    return lax.ppermute(value, "section", [(0, 1), (1, 0)])


def chips_to_chips(value):
    return lax.all_to_all(value, ("z", "y"), 0, 0, tiled=True)


def neighbour(value, part, turn):
    route = [
        (2 * chip + core, 2 * (chip ^ MASKS[part][core][turn]) + core)
        for chip in range(CHIPS)
        for core in range(2)
    ]
    return lax.ppermute(value, MP, route)


def places(chip, pick):
    offsets = lax.dynamic_index_in_dim(jnp.asarray(OFFSETS), pick, 1, keepdims=False)
    return jnp.concatenate([jnp.reshape(pick, (1,)), (chip ^ offsets).reshape(-1)]).astype(
        jnp.int32
    )


def together(*values):
    return lax.optimization_barrier(values)


def first_round(local):
    return [neighbour(value, part, 0) for part, value in enumerate(local)]


def later_rounds(local, got):
    near = [jnp.stack(pair) for pair in zip(local, got)]
    got = together(*[neighbour(value, part, 1) for part, value in enumerate(near)])
    near = [jnp.concatenate(pair) for pair in zip(near, got)]
    swaps = [core_swap(value) for value in near]
    far = [neighbour(value, part, 2) for part, value in enumerate(near)]
    swaps = list(together(*swaps))
    far = list(together(*far))
    return near + far, swaps + [core_swap(value) for value in far]


def gather_chips(local):
    return later_rounds(local, together(*first_round(local)))


def scatter_sum(places_both, mixed, weight):
    own, other = places_both
    other_far = [core_swap(value) for value in terms(other, mixed, weight, 1)]
    other_near = [core_swap(value) for value in terms(other, mixed, weight, 0)]
    own_far = terms(own, mixed, weight, 1)
    own_near = terms(own, mixed, weight, 0)
    other_far = together(*other_far)
    sums = [
        (mine.astype(f32) + got.astype(f32)).astype(bf16)
        for mine, got in zip(own_far, other_far)
    ]
    got = together(*[neighbour(sums[part], part, 2) for part in range(2)], *other_near)
    low = [
        own_near[part].astype(f32) + got[2 + part].astype(f32) + got[part].astype(f32)
        for part in range(2)
    ]
    got = together(*[neighbour(low[part][2:].astype(bf16), part, 1) for part in range(2)])
    low = [low[part][:2] + got[part].astype(f32) for part in range(2)]
    got = [neighbour(low[part][1].astype(bf16), part, 0) for part in range(2)]
    return [low[part][0] for part in range(2)], got


def project_kernel(last, units, place_ref, *refs):
    whole_rows = len(refs) == (8 if last else 6)
    count = 1 if whole_rows else 4
    x_refs, (gain_ref, w_ref), refs = refs[:count], refs[count : count + 2], refs[count + 2 :]
    if last:
        acc_in, sq_in, out_ref, sq_ref, left_ref = refs
    else:
        acc_ref, sq_ref, left_ref = refs
    step = pl.program_id(0)

    def place_rows(rows, blocks):
        total = sq_in[rows, :] if last else jnp.zeros((rows.stop - rows.start, 128), f32)
        for block, chip in blocks:
            wide = block.astype(f32)
            squares = wide * wide
            total += squares[:, :128] + squares[:, 128:]
            cols = pl.ds(pl.multiple_of(chip * WIDTH, WIDTH), WIDTH)
            left_ref[rows, cols] = (wide * gain_ref[chip, 0]).astype(bf16)
        sq_ref[rows, :] = total

    @pl.when(step == 0)
    def _():
        for part in range(2):
            rows = slice(STARTS[part], STARTS[part] + PARTS[part])
            if whole_rows:
                blocks = [(x_refs[0][chip, rows, :], chip) for chip in range(CHIPS)]
            else:
                blocks = [
                    (
                        x_refs[part + 2 * (block // 4)][block % 4],
                        place_ref[1 + part * CHIPS + block],
                    )
                    for block in range(CHIPS)
                ]
            place_rows(rows, blocks)

    right = w_ref[0].reshape(CHIPS * WIDTH, WIDTH)
    product = jnp.dot(left_ref[...], right, preferred_element_type=f32)
    if not last:
        acc_ref[0] = product
        return
    mean = jnp.sum(sq_ref[...], axis=1, keepdims=True) / D
    done = ((acc_in[0] + product) / jnp.sqrt(mean + epsilon)).astype(bf16)
    if units:
        for unit in range(UNITS):
            b, h = divmod(unit, 2)
            out_ref[unit, 0] = done[b * ROWS : (b + 1) * ROWS, h * HEAD : (h + 1) * HEAD]
    else:
        out_ref[...] = done


def project_half(place, rows, gains, weight, before, units):
    parts = weight.shape[0]
    count = BATCH * ROWS
    acc = (parts, count, WIDTH)
    sq = (count, 128)
    last = before is not None
    acc_spec = pl.BlockSpec((1, count, WIDTH), lambda s, place: (s, 0, 0))
    in_specs = [whole(value.shape) for value in rows] + [
        pl.BlockSpec((CHIPS, 1, 1, WIDTH), lambda s, place: (0, place[0], 0, 0)),
        pl.BlockSpec((1, CHIPS, 1, WIDTH, WIDTH), lambda s, place: (s, 0, place[0], 0, 0)),
    ]
    scratch = [pltpu.VMEM((count, CHIPS * WIDTH), bf16)]
    if last:
        in_specs += [acc_spec, whole(sq)]
        scratch = [pltpu.VMEM(sq, f32)] + scratch
        if units:
            out = (UNITS, parts, ROWS, HEAD)
            out_specs = pl.BlockSpec((UNITS, 1, ROWS, HEAD), lambda s, place: (0, s, 0, 0))
        else:
            out = (count, WIDTH)
            out_specs = whole(out)
        out_shape = jax.ShapeDtypeStruct(out, bf16)
    else:
        out_specs = [acc_spec, whole(sq)]
        out_shape = [jax.ShapeDtypeStruct(acc, f32), jax.ShapeDtypeStruct(sq, f32)]
    return pl.pallas_call(
        functools.partial(project_kernel, last, units),
        grid_spec=pltpu.PrefetchScalarGridSpec(
            num_scalar_prefetch=1,
            grid=(parts,),
            in_specs=in_specs,
            out_specs=out_specs,
            scratch_shapes=scratch,
        ),
        out_shape=out_shape,
        compiler_params=params(),
        cost_estimate=pl.CostEstimate(
            flops=2 * count * (D // 2) * WIDTH * parts,
            bytes_accessed=D * WIDTH * parts + D * count + 4 * count * WIDTH * parts,
            transcendentals=0,
        ),
    )(
        place,
        *rows,
        gains.reshape(CHIPS, 2, 1, WIDTH),
        weight.reshape(parts, CHIPS, 2, WIDTH, WIDTH),
        *(before or ()),
    )


def project(places_both, same, swap, gains, weight, units):
    before = project_half(places_both[0], same, gains, weight, None, units)
    return project_half(places_both[1], swap, gains, weight, before, units)


def causal_kernel(triple_ref, out_ref):
    scaling = HEAD ** (-0.5)
    row = lax.broadcasted_iota(jnp.int32, (ROWS, ROWS), 0)
    col = lax.broadcasted_iota(jnp.int32, (ROWS, ROWS), 1)
    for i in range(UNITS):
        queries = triple_ref[i, 0]
        numer = jnp.zeros((ROWS, HEAD), f32)
        denom = jnp.zeros((ROWS, 1), f32)
        for j in range(i + 1):
            scores = lax.dot_general(
                queries, triple_ref[j, 1], (((1,), (1,)), ((), ())), preferred_element_type=f32
            )
            weights = jnp.exp(scores * scaling)
            if i == j:
                weights = jnp.where(col <= row, weights, 0.0)
            denom += jnp.sum(weights, axis=1, keepdims=True)
            numer += jnp.dot(weights.astype(bf16), triple_ref[j, 2], preferred_element_type=f32)
        out_ref[i] = (numer / denom).astype(bf16)


def causal(triple):
    out = (UNITS, ROWS, HEAD)
    return pl.pallas_call(
        causal_kernel,
        out_shape=jax.ShapeDtypeStruct(out, bf16),
        compiler_params=params(),
    )(triple)


def crossed_kernel(asked_ref, prev_ref, *refs):
    pairs_refs, out_ref = refs[:2], refs[2]
    scaling = HEAD ** (-0.5)
    row = lax.broadcasted_iota(jnp.int32, (BLOCK, 2 * KEYS), 0)
    col = lax.broadcasted_iota(jnp.int32, (BLOCK, 2 * KEYS), 1)
    allowed = (row < BLOCK - 1) == (col < KEYS)
    for unit in range(UNITS):
        b, h = divmod(unit, 2)

        def both_blocks(i, cols):
            before = [
                prev_ref[pick, b, :, cols] if i == 0 else pair[b, i - 1, :, cols]
                for pick, pair in enumerate(pairs_refs)
            ]
            return jnp.concatenate(before + [pair[b, i, :, cols] for pair in pairs_refs], axis=0)

        for i in range(ROWS // BLOCK):
            queries = asked_ref[
                b * ROWS + i * BLOCK : b * ROWS + (i + 1) * BLOCK, h * HEAD : (h + 1) * HEAD
            ]
            keys = both_blocks(i, slice(h * HEAD, (h + 1) * HEAD))
            values = both_blocks(i, slice((2 + h) * HEAD, (3 + h) * HEAD))
            scores = lax.dot_general(
                queries, keys, (((1,), (1,)), ((), ())), preferred_element_type=f32
            )
            weights = jnp.where(allowed, jnp.exp(scores * scaling), 0.0)
            denom = jnp.sum(weights, axis=1, keepdims=True)
            numer = jnp.dot(weights.astype(bf16), values, preferred_element_type=f32)
            out_ref[unit, i * BLOCK : (i + 1) * BLOCK, :] = (numer / denom).astype(bf16)


def cross(asked, prevs, pairs):
    out = (UNITS, ROWS, HEAD)
    return pl.pallas_call(
        crossed_kernel,
        out_shape=jax.ShapeDtypeStruct(out, bf16),
        compiler_params=params(),
    )(asked, prevs, *pairs)


def terms_kernel(place_ref, mixed_ref, *refs):
    w_refs, out_refs, left_ref = refs[: 2 * GROUP], refs[2 * GROUP : 2 * GROUP + 2], refs[-1]
    for unit in range(UNITS):
        b, h = divmod(unit, 2)
        left_ref[b * ROWS : (b + 1) * ROWS, h * HEAD : (h + 1) * HEAD] = mixed_ref[unit]
    for part in range(2):
        left = left_ref[STARTS[part] : STARTS[part] + PARTS[part], :]
        for at in range(GROUP):
            right = w_refs[part * GROUP + at][...]
            out_refs[part][at] = jnp.dot(left, right, preferred_element_type=f32).astype(bf16)


def terms(place, mixed, weight, high):
    count = BATCH * ROWS

    def columns(part, at):
        index = 1 + part * CHIPS + GROUP * high + at
        return pl.BlockSpec((WIDTH, WIDTH), lambda s, place: (0, 2 * place[index] + place[0]))

    shapes = [(GROUP, PARTS[part], WIDTH) for part in range(2)]
    return pl.pallas_call(
        terms_kernel,
        grid_spec=pltpu.PrefetchScalarGridSpec(
            num_scalar_prefetch=1,
            grid=(1,),
            in_specs=[whole((UNITS, ROWS, HEAD))]
            + [columns(part, at) for part in range(2) for at in range(GROUP)],
            out_specs=[whole(shape) for shape in shapes],
            scratch_shapes=[pltpu.VMEM((count, WIDTH), bf16)],
        ),
        out_shape=[jax.ShapeDtypeStruct(shape, bf16) for shape in shapes],
        compiler_params=params(8),
        cost_estimate=pl.CostEstimate(
            flops=2 * count * WIDTH * D // 4,
            bytes_accessed=D * WIDTH + D * count // 2,
            transcendentals=0,
        ),
    )(place, mixed, *([weight] * (2 * GROUP)))


def add_product(places_both, states, mixed, weight, side=()):
    low, got = scatter_sum(places_both, mixed, weight)
    *got, side = together(*got, side)
    total = [
        (state.astype(f32) + (mine + far.astype(f32))).astype(bf16)
        for state, mine, far in zip(states, low, got)
    ]
    return total, side


def by_parts(rows):
    return [rows[start : start + count] for start, count in zip(STARTS, PARTS)]


def weight_parts(enc_qkv, enc_out, enc_up, enc_down):
    up = enc_up.reshape(64, 16, 2, 2, 64)
    up = jnp.transpose(up, (2, 3, 0, 1, 4)).reshape(2, 2, 64, 2, PIECE)
    up = jnp.transpose(up, (0, 1, 3, 2, 4)).reshape(2, 4, 64, PIECE)
    down = enc_down.reshape(2, 2, 64, 2, PIECE)
    down = jnp.transpose(down, (0, 1, 3, 2, 4)).reshape(2, 4, 64, PIECE)
    triple = jnp.transpose(enc_qkv.reshape(64, 3, 2, PIECE), (2, 1, 0, 3)).reshape(6, 64, PIECE)
    out = jnp.transpose(enc_out.reshape(64, 2, PIECE), (1, 0, 2))
    feed = jnp.concatenate([up, down], axis=1).reshape(16, 64, PIECE)
    return [feed, jnp.concatenate([triple, out], axis=0)]


def assemble(place_refs, refs, part, piece, w_ref):
    for place_ref, (near, far) in zip(place_refs, (refs[:2], refs[2:])):
        for block in range(CHIPS):
            chip = place_ref[1 + part * CHIPS + block]
            start = pl.multiple_of((2 * chip + place_ref[0]) * 64, 64)
            w_ref[pl.ds(start, 64), :] = (near if block < 4 else far)[block % 4, piece]


def scaled_rows(values, gain):
    wide = values.astype(f32)
    root = jnp.sqrt(jnp.mean(wide * wide, axis=1, keepdims=True) + epsilon)
    return (wide * gain).astype(bf16), root


def enc_mix_kernel(own_ref, other_ref, x_ref, gain_ref, *refs):
    blocks, (out_ref, w_ref, mix_ref) = refs[:4], refs[4:]
    places_both = (own_ref, other_ref)
    for piece in range(8):
        assemble(places_both, blocks, 1, piece, w_ref.at[piece])
    scaled, root = scaled_rows(x_ref[...], gain_ref[...])
    for half in range(2):
        triple = []
        for part in range(3):
            product = jnp.dot(scaled, w_ref[3 * half + part], preferred_element_type=f32)
            triple.append((product / root).astype(bf16))
        for head in range(ENC_HEADS // 2):
            cols = slice(head * ENC_HEAD, (head + 1) * ENC_HEAD)
            scores = lax.dot_general(
                triple[0][:, cols],
                triple[1][:, cols],
                (((1,), (1,)), ((), ())),
                preferred_element_type=f32,
            )
            weights = jnp.exp(scores * ENC_HEAD ** (-0.5))
            denom = jnp.sum(weights, axis=1, keepdims=True)
            numer = jnp.dot(weights.astype(bf16), triple[2][:, cols], preferred_element_type=f32)
            start = half * PIECE + head * ENC_HEAD
            mix_ref[:, start : start + ENC_HEAD] = (numer / denom).astype(bf16)
    mixed = mix_ref[...]
    for at in range(2):
        cols = slice(at * PIECE, (at + 1) * PIECE)
        product = jnp.dot(mixed, w_ref[6 + at], preferred_element_type=f32)
        out_ref[:, cols] = (x_ref[:, cols].astype(f32) + product).astype(bf16)


def enc_feed_kernel(own_ref, other_ref, x_ref, gain_ref, *refs):
    blocks, (out_ref, w_ref, acc_ref) = refs[:4], refs[4:]
    places_both = (own_ref, other_ref)
    for piece in range(8):
        assemble(places_both, blocks, 0, piece, w_ref.at[piece])
    scaled, root = scaled_rows(x_ref[...], gain_ref[...])

    @pl.when(pl.program_id(0) == 0)
    def _():
        acc_ref[...] = x_ref[...].astype(f32)

    for row in range(2):
        hidden = []
        for piece in range(2):
            product = jnp.dot(scaled, w_ref[2 * row + piece], preferred_element_type=f32)
            hidden.append(jax.nn.gelu(product / root, approximate=True).astype(bf16))
        hidden = jnp.concatenate(hidden, axis=1)
        for at in range(2):
            cols = slice(at * PIECE, (at + 1) * PIECE)
            right = w_ref[4 + 2 * row + at]
            acc_ref[:, cols] += jnp.dot(hidden, right, preferred_element_type=f32)

    @pl.when(pl.program_id(0) == 1)
    def _():
        out_ref[...] = acc_ref[...].astype(bf16)


def encode(places_both, embedded, enc_norms, feed, mix):
    out = jax.ShapeDtypeStruct((NB_LEN, ENC_D), bf16)
    full = whole((NB_LEN, ENC_D))
    gain = whole((1, ENC_D))

    def call(kernel, steps, pieces, scratch, x, gains, rows):
        block = (4, rows[0].shape[1] // steps, 64, PIECE)
        return pl.pallas_call(
            kernel,
            grid_spec=pltpu.PrefetchScalarGridSpec(
                num_scalar_prefetch=2,
                grid=(steps,),
                in_specs=[full, gain]
                + [pl.BlockSpec(block, lambda s, *_: (0, s, 0, 0)) for _ in rows],
                out_specs=full,
                scratch_shapes=[pltpu.VMEM((pieces, ENC_D, PIECE), bf16), scratch],
            ),
            out_shape=out,
            compiler_params=params(40),
        )(*places_both, x, gains, *rows)

    inner = call(
        enc_mix_kernel, 1, 8, pltpu.VMEM((NB_LEN, ENC_D), bf16), embedded, enc_norms[:1], mix
    )
    return call(
        enc_feed_kernel, 2, 8, pltpu.VMEM((NB_LEN, ENC_D), f32), inner, enc_norms[1:], feed
    )


def encode_neighbour(places_both, ids, enc_embed, enc_norms, local):
    vocab_here = enc_embed.shape[0]
    wanted = ids - lax.axis_index(MP) * vocab_here

    def rows(place, wanted):
        picks = wanted[2 * place[1 : 1 + CHIPS] + place[0]].reshape(-1)
        inside = (picks >= 0) & (picks < vocab_here)
        found = enc_embed[jnp.clip(picks, 0, vocab_here - 1)]
        found = jnp.where(inside[:, None], found, jnp.zeros((), bf16))
        return found.reshape(CHIPS, NB_LEN, ENC_D)

    other = rows(places_both[1], wanted)
    *got, other, wanted = together(*first_round(local), other, wanted)
    near = [jnp.stack(pair) for pair in zip(local, got)]
    sent = [neighbour(value, part, 1) for part, value in enumerate(near)]
    total = rows(places_both[0], wanted) + core_swap(other)
    summed = neighbour(total[4:], 0, 2)
    *got, summed = together(*sent, summed)
    near = [jnp.concatenate(pair) for pair in zip(near, got)]
    swaps = [core_swap(value) for value in near]
    far = together(*[neighbour(value, part, 2) for part, value in enumerate(near)])
    far_swaps = [core_swap(value) for value in far]
    total = total[:4] + summed
    total = total[:2] + neighbour(total[2:], 0, 1)
    embedded = total[0] + neighbour(total[1], 0, 0)
    feed, mix = [
        [near[part], far[part], swaps[part], far_swaps[part]] for part in range(2)
    ]
    return encode(places_both, embedded, enc_norms, feed, mix)


def pairs_kernel(place_ref, *refs):
    x_refs, (w_ref, out_ref, left_ref) = refs[:4], refs[4:]
    for part in range(2):
        for block in range(CHIPS):
            chip = place_ref[1 + part * CHIPS + block]
            start = pl.multiple_of(chip * NB_LEN + ENC_STARTS[part], 16)
            value = x_refs[part + 2 * (block // 4)][block % 4]
            left_ref[pl.ds(start, ENC_PARTS[part]), :] = value
    out_ref[...] = jnp.dot(left_ref[...], w_ref[...], preferred_element_type=f32).astype(bf16)


def make_pairs(place, rows, weight):
    out = (CHIPS * NB_LEN, 2 * WIDTH)
    pairs = pl.pallas_call(
        pairs_kernel,
        grid_spec=pltpu.PrefetchScalarGridSpec(
            num_scalar_prefetch=1,
            grid=(1,),
            in_specs=[whole(value.shape) for value in rows] + [whole(weight.shape)],
            out_specs=whole(out),
            scratch_shapes=[pltpu.VMEM((CHIPS * NB_LEN, ENC_D), bf16)],
        ),
        out_shape=jax.ShapeDtypeStruct(out, bf16),
        compiler_params=params(20),
        cost_estimate=pl.CostEstimate(
            flops=2 * CHIPS * NB_LEN * ENC_D * 2 * WIDTH,
            bytes_accessed=2 * (CHIPS * NB_LEN + 2 * WIDTH) * ENC_D,
            transcendentals=0,
        ),
    )(place, *rows, weight)
    return pairs.reshape(BATCH, CHIPS // BATCH, NB_LEN, 2 * WIDTH)


def attention(triple):
    triple = lax.all_to_all(triple, "seq", 0, 0, tiled=True)
    return lax.all_to_all(causal(triple), "seq", 0, 0, tiled=True)


def to_queries(places_both, states, weights):
    norms, triple_w, out_w, query_w, back_w = weights
    triple = project(places_both, *gather_chips(states), norms[0], triple_w, True)
    middle, _ = add_product(places_both, states, attention(triple), out_w)
    asked = project(places_both, *gather_chips(middle), norms[1], query_w[None], False)
    return middle, asked


def cross_layer(places_both, middle, asked, prevs, pairs, weights):
    crossed = cross(asked, prevs, pairs)
    return add_product(places_both, middle, crossed, weights[4])[0]


def on_device(
    hidden_states,
    neighbour_ids,
    neighbour_table,
    enc_embed,
    enc_norms,
    enc_qkv,
    enc_out,
    enc_up,
    enc_down,
    dec_norms,
    dec_qkv,
    dec_out,
    cross_query,
    cross_pair,
    cross_out,
):
    section = lax.axis_index("section").astype(jnp.int32)
    core_at = lax.axis_index("core").astype(jnp.int32)
    chip = lax.axis_index(("z", "y")).astype(jnp.int32)
    places_both = [places(chip, core_at), places(chip, 1 - core_at)]
    slot_ids = neighbour_ids[neighbour_table.reshape(-1)]
    pair_w = cross_pair[0].reshape(ENC_D, 2 * WIDTH)
    weights = (
        dec_norms[0],
        jnp.transpose(dec_qkv[0], (1, 0, 2)),
        dec_out[0],
        cross_query[0],
        cross_out[0],
    )

    states = hidden_states.reshape(BATCH * ROWS, WIDTH)

    def decode():
        middle, asked = to_queries(places_both, by_parts(states), weights)
        return jnp.concatenate(middle), asked, jnp.zeros((NB_LEN, ENC_D), bf16)

    def encode_all():
        local = weight_parts(enc_qkv, enc_out, enc_up, enc_down)
        blank = jnp.zeros(states.shape, bf16)
        return blank, blank, encode_neighbour(places_both, slot_ids, enc_embed, enc_norms, local)

    middle, asked, encoded = lax.cond(section == 0, decode, encode_all)
    middle = by_parts(middle)
    encoded = jnp.where(section == 0, section_swap(encoded), encoded)
    encoded = gather_chips(
        [encoded[start : start + count] for start, count in zip(ENC_STARTS, ENC_PARTS)]
    )
    pairs = [make_pairs(place, rows, pair_w) for place, rows in zip(places_both, encoded)]
    edges = jnp.stack([rows[:, -1] for rows in pairs])
    count = lax.axis_size("seq")
    prevs = lax.ppermute(edges, "seq", [(i, i + 1) for i in range(count - 1)])
    first = cross_layer(places_both, middle, asked, prevs, pairs, weights)
    handed = section_swap(jnp.concatenate(first))
    middle, asked = to_queries(places_both, by_parts(handed), weights)
    second = jnp.concatenate(cross_layer(places_both, middle, asked, prevs, pairs, weights))
    second = second.reshape(BATCH, ROWS, WIDTH)
    return jnp.where(section == 0, section_swap(second[0]), second[1])[None]


def solution(mesh):
    devices = mesh.devices
    sections, seqs = devices.shape[:2]
    split = Mesh(
        devices.reshape(sections, seqs, 2, 4, 2), ("section", "seq", "z", "y", "core")
    )
    mp = ("z", "y", "core")
    return jax.shard_map(
        on_device,
        mesh=split,
        in_specs=(
            P(None, "seq", mp),
            P(),
            P(None, "seq", None),
            P(mp, None),
            P(),
            P(mp, None, None),
            P(mp, None),
            P(mp, None),
            P(mp, None),
            P("section", None, None),
            P("section", None, None, mp),
            P("section", mp, None),
            P("section", None, mp),
            P("section", None, None, mp),
            P("section", mp, None),
        ),
        out_specs=P("section", "seq", mp),
        check_vma=False,
    )
```

```python
import functools

import jax
import jax.numpy as jnp
import numpy as np
from jax import lax
from jax.experimental import pallas as pl
from jax.experimental.pallas import tpu as pltpu
from jax.sharding import Mesh, PartitionSpec as P

D = 4096
HEAD = 128
ENC_D = 1024
ENC_HEADS = 16
ENC_HEAD = 64
BLOCK = 64
NB_LEN = 128
NEIGH = 2
BATCH = 2
CHIPS = 8
ROWS = 256
WIDTH = 256
UNITS = 4
GROUP = 4
MP = ("z", "y", "core")
KEYS = NEIGH * NB_LEN

epsilon = 1e-05
f32 = jnp.float32
bf16 = jnp.bfloat16


def params(mebibytes=16):
    return pltpu.CompilerParams(vmem_limit_bytes=mebibytes * 1024 * 1024)


def whole(shape):
    return pl.BlockSpec(shape, lambda *_: (0,) * len(shape))


SCALAR = pl.BlockSpec(memory_space=pltpu.SMEM)


PARTS = (352, 160)
STARTS = (0, 352)
ENC_PARTS = (80, 48)
ENC_STARTS = (0, 80)
PIECE = 512
MASKS = (((4, 1, 3), (1, 3, 4)), ((3, 4, 1), (3, 4, 1)))


def block_offsets(masks):
    return [
        (masks[0] * (b & 1)) ^ (masks[1] * (b >> 1 & 1)) ^ (masks[2] * (b >> 2 & 1))
        for b in range(CHIPS)
    ]


OFFSETS = np.array([[block_offsets(m) for m in part] for part in MASKS], np.int32)


def core_swap(value):
    return lax.ppermute(value, "core", [(0, 1), (1, 0)])


def section_swap(value):
    return lax.ppermute(value, "section", [(0, 1), (1, 0)])


def chips_to_chips(value):
    return lax.all_to_all(value, ("z", "y"), 0, 0, tiled=True)


def neighbour(value, part, turn):
    route = [
        (2 * chip + core, 2 * (chip ^ MASKS[part][core][turn]) + core)
        for chip in range(CHIPS)
        for core in range(2)
    ]
    return lax.ppermute(value, MP, route)


def places(chip, pick):
    offsets = lax.dynamic_index_in_dim(jnp.asarray(OFFSETS), pick, 1, keepdims=False)
    return jnp.concatenate([jnp.reshape(pick, (1,)), (chip ^ offsets).reshape(-1)]).astype(
        jnp.int32
    )


def together(*values):
    return lax.optimization_barrier(values)


def first_round(local):
    return [neighbour(value, part, 0) for part, value in enumerate(local)]


def later_rounds(local, got):
    near = [jnp.stack(pair) for pair in zip(local, got)]
    got = together(*[neighbour(value, part, 1) for part, value in enumerate(near)])
    near = [jnp.concatenate(pair) for pair in zip(near, got)]
    swaps = [core_swap(value) for value in near]
    far = [neighbour(value, part, 2) for part, value in enumerate(near)]
    swaps = list(together(*swaps))
    far = list(together(*far))
    return near + far, swaps + [core_swap(value) for value in far]


def gather_chips(local):
    return later_rounds(local, together(*first_round(local)))


def scatter_sum(places_both, mixed, weight):
    own, other = places_both
    other_far = [core_swap(value) for value in terms(other, mixed, weight, 1)]
    other_near = [core_swap(value) for value in terms(other, mixed, weight, 0)]
    own_far = terms(own, mixed, weight, 1)
    own_near = terms(own, mixed, weight, 0)
    other_far = together(*other_far)
    sums = [
        (mine.astype(f32) + got.astype(f32)).astype(bf16)
        for mine, got in zip(own_far, other_far)
    ]
    got = together(*[neighbour(sums[part], part, 2) for part in range(2)], *other_near)
    low = [
        own_near[part].astype(f32) + got[2 + part].astype(f32) + got[part].astype(f32)
        for part in range(2)
    ]
    got = together(*[neighbour(low[part][2:].astype(bf16), part, 1) for part in range(2)])
    low = [low[part][:2] + got[part].astype(f32) for part in range(2)]
    got = [neighbour(low[part][1].astype(bf16), part, 0) for part in range(2)]
    return [low[part][0] for part in range(2)], got


def project_kernel(last, units, place_ref, *refs):
    whole_rows = len(refs) == (8 if last else 6)
    count = 1 if whole_rows else 4
    x_refs, (gain_ref, w_ref), refs = refs[:count], refs[count : count + 2], refs[count + 2 :]
    if last:
        acc_in, sq_in, out_ref, sq_ref, left_ref = refs
    else:
        acc_ref, sq_ref, left_ref = refs
    step = pl.program_id(0)

    def place_rows(rows, blocks):
        total = sq_in[rows, :] if last else jnp.zeros((rows.stop - rows.start, 128), f32)
        for block, chip in blocks:
            wide = block.astype(f32)
            squares = wide * wide
            total += squares[:, :128] + squares[:, 128:]
            cols = pl.ds(pl.multiple_of(chip * WIDTH, WIDTH), WIDTH)
            left_ref[rows, cols] = (wide * gain_ref[chip, 0]).astype(bf16)
        sq_ref[rows, :] = total

    @pl.when(step == 0)
    def _():
        for part in range(2):
            rows = slice(STARTS[part], STARTS[part] + PARTS[part])
            if whole_rows:
                blocks = [(x_refs[0][chip, rows, :], chip) for chip in range(CHIPS)]
            else:
                blocks = [
                    (
                        x_refs[part + 2 * (block // 4)][block % 4],
                        place_ref[1 + part * CHIPS + block],
                    )
                    for block in range(CHIPS)
                ]
            place_rows(rows, blocks)

    right = w_ref[0].reshape(CHIPS * WIDTH, WIDTH)
    product = jnp.dot(left_ref[...], right, preferred_element_type=f32)
    if not last:
        acc_ref[0] = product
        return
    mean = jnp.sum(sq_ref[...], axis=1, keepdims=True) / D
    done = ((acc_in[0] + product) / jnp.sqrt(mean + epsilon)).astype(bf16)
    if units:
        for unit in range(UNITS):
            b, h = divmod(unit, 2)
            out_ref[unit, 0] = done[b * ROWS : (b + 1) * ROWS, h * HEAD : (h + 1) * HEAD]
    else:
        out_ref[...] = done


def project_half(place, rows, gains, weight, before, units):
    parts = weight.shape[0]
    count = BATCH * ROWS
    acc = (parts, count, WIDTH)
    sq = (count, 128)
    last = before is not None
    acc_spec = pl.BlockSpec((1, count, WIDTH), lambda s, place: (s, 0, 0))
    in_specs = [whole(value.shape) for value in rows] + [
        pl.BlockSpec((CHIPS, 1, 1, WIDTH), lambda s, place: (0, place[0], 0, 0)),
        pl.BlockSpec((1, CHIPS, 1, WIDTH, WIDTH), lambda s, place: (s, 0, place[0], 0, 0)),
    ]
    scratch = [pltpu.VMEM((count, CHIPS * WIDTH), bf16)]
    if last:
        in_specs += [acc_spec, whole(sq)]
        scratch = [pltpu.VMEM(sq, f32)] + scratch
        if units:
            out = (UNITS, parts, ROWS, HEAD)
            out_specs = pl.BlockSpec((UNITS, 1, ROWS, HEAD), lambda s, place: (0, s, 0, 0))
        else:
            out = (count, WIDTH)
            out_specs = whole(out)
        out_shape = jax.ShapeDtypeStruct(out, bf16)
    else:
        out_specs = [acc_spec, whole(sq)]
        out_shape = [jax.ShapeDtypeStruct(acc, f32), jax.ShapeDtypeStruct(sq, f32)]
    return pl.pallas_call(
        functools.partial(project_kernel, last, units),
        grid_spec=pltpu.PrefetchScalarGridSpec(
            num_scalar_prefetch=1,
            grid=(parts,),
            in_specs=in_specs,
            out_specs=out_specs,
            scratch_shapes=scratch,
        ),
        out_shape=out_shape,
        compiler_params=params(),
        cost_estimate=pl.CostEstimate(
            flops=2 * count * (D // 2) * WIDTH * parts,
            bytes_accessed=D * WIDTH * parts + D * count + 4 * count * WIDTH * parts,
            transcendentals=0,
        ),
    )(
        place,
        *rows,
        gains.reshape(CHIPS, 2, 1, WIDTH),
        weight.reshape(parts, CHIPS, 2, WIDTH, WIDTH),
        *(before or ()),
    )


def project(places_both, same, swap, gains, weight, units):
    before = project_half(places_both[0], same, gains, weight, None, units)
    return project_half(places_both[1], swap, gains, weight, before, units)


def causal_kernel(triple_ref, out_ref):
    scaling = HEAD ** (-0.5)
    row = lax.broadcasted_iota(jnp.int32, (ROWS, ROWS), 0)
    col = lax.broadcasted_iota(jnp.int32, (ROWS, ROWS), 1)
    for i in range(UNITS):
        queries = triple_ref[i, 0]
        numer = jnp.zeros((ROWS, HEAD), f32)
        denom = jnp.zeros((ROWS, 1), f32)
        for j in range(i + 1):
            scores = lax.dot_general(
                queries, triple_ref[j, 1], (((1,), (1,)), ((), ())), preferred_element_type=f32
            )
            weights = jnp.exp(scores * scaling)
            if i == j:
                weights = jnp.where(col <= row, weights, 0.0)
            denom += jnp.sum(weights, axis=1, keepdims=True)
            numer += jnp.dot(weights.astype(bf16), triple_ref[j, 2], preferred_element_type=f32)
        out_ref[i] = (numer / denom).astype(bf16)


def causal(triple):
    out = (UNITS, ROWS, HEAD)
    return pl.pallas_call(
        causal_kernel,
        out_shape=jax.ShapeDtypeStruct(out, bf16),
        compiler_params=params(),
    )(triple)


def crossed_kernel(asked_ref, prev_ref, *refs):
    pairs_refs, out_ref = refs[:2], refs[2]
    scaling = HEAD ** (-0.5)
    row = lax.broadcasted_iota(jnp.int32, (BLOCK, 2 * KEYS), 0)
    col = lax.broadcasted_iota(jnp.int32, (BLOCK, 2 * KEYS), 1)
    allowed = (row < BLOCK - 1) == (col < KEYS)
    for unit in range(UNITS):
        b, h = divmod(unit, 2)

        def both_blocks(i, cols):
            before = [
                prev_ref[pick, b, :, cols] if i == 0 else pair[b, i - 1, :, cols]
                for pick, pair in enumerate(pairs_refs)
            ]
            return jnp.concatenate(before + [pair[b, i, :, cols] for pair in pairs_refs], axis=0)

        for i in range(ROWS // BLOCK):
            queries = asked_ref[
                b * ROWS + i * BLOCK : b * ROWS + (i + 1) * BLOCK, h * HEAD : (h + 1) * HEAD
            ]
            keys = both_blocks(i, slice(h * HEAD, (h + 1) * HEAD))
            values = both_blocks(i, slice((2 + h) * HEAD, (3 + h) * HEAD))
            scores = lax.dot_general(
                queries, keys, (((1,), (1,)), ((), ())), preferred_element_type=f32
            )
            weights = jnp.where(allowed, jnp.exp(scores * scaling), 0.0)
            denom = jnp.sum(weights, axis=1, keepdims=True)
            numer = jnp.dot(weights.astype(bf16), values, preferred_element_type=f32)
            out_ref[unit, i * BLOCK : (i + 1) * BLOCK, :] = (numer / denom).astype(bf16)


def cross(asked, prevs, pairs):
    out = (UNITS, ROWS, HEAD)
    return pl.pallas_call(
        crossed_kernel,
        out_shape=jax.ShapeDtypeStruct(out, bf16),
        compiler_params=params(),
    )(asked, prevs, *pairs)


def terms_kernel(place_ref, mixed_ref, *refs):
    w_refs, out_refs, left_ref = refs[: 2 * GROUP], refs[2 * GROUP : 2 * GROUP + 2], refs[-1]
    for unit in range(UNITS):
        b, h = divmod(unit, 2)
        left_ref[b * ROWS : (b + 1) * ROWS, h * HEAD : (h + 1) * HEAD] = mixed_ref[unit]
    for part in range(2):
        left = left_ref[STARTS[part] : STARTS[part] + PARTS[part], :]
        for at in range(GROUP):
            right = w_refs[part * GROUP + at][...]
            out_refs[part][at] = jnp.dot(left, right, preferred_element_type=f32).astype(bf16)


def terms(place, mixed, weight, high):
    count = BATCH * ROWS

    def columns(part, at):
        index = 1 + part * CHIPS + GROUP * high + at
        return pl.BlockSpec((WIDTH, WIDTH), lambda s, place: (0, 2 * place[index] + place[0]))

    shapes = [(GROUP, PARTS[part], WIDTH) for part in range(2)]
    return pl.pallas_call(
        terms_kernel,
        grid_spec=pltpu.PrefetchScalarGridSpec(
            num_scalar_prefetch=1,
            grid=(1,),
            in_specs=[whole((UNITS, ROWS, HEAD))]
            + [columns(part, at) for part in range(2) for at in range(GROUP)],
            out_specs=[whole(shape) for shape in shapes],
            scratch_shapes=[pltpu.VMEM((count, WIDTH), bf16)],
        ),
        out_shape=[jax.ShapeDtypeStruct(shape, bf16) for shape in shapes],
        compiler_params=params(8),
        cost_estimate=pl.CostEstimate(
            flops=2 * count * WIDTH * D // 4,
            bytes_accessed=D * WIDTH + D * count // 2,
            transcendentals=0,
        ),
    )(place, mixed, *([weight] * (2 * GROUP)))


def add_product(places_both, states, mixed, weight, side=()):
    low, got = scatter_sum(places_both, mixed, weight)
    *got, side = together(*got, side)
    total = [
        (state.astype(f32) + (mine + far.astype(f32))).astype(bf16)
        for state, mine, far in zip(states, low, got)
    ]
    return total, side


def by_parts(rows):
    return [rows[start : start + count] for start, count in zip(STARTS, PARTS)]


def weight_parts(enc_qkv, enc_out, enc_up, enc_down):
    up = enc_up.reshape(64, 16, 2, 2, 64)
    up = jnp.transpose(up, (2, 3, 0, 1, 4)).reshape(2, 2, 64, 2, PIECE)
    up = jnp.transpose(up, (0, 1, 3, 2, 4)).reshape(2, 4, 64, PIECE)
    down = enc_down.reshape(2, 2, 64, 2, PIECE)
    down = jnp.transpose(down, (0, 1, 3, 2, 4)).reshape(2, 4, 64, PIECE)
    triple = jnp.transpose(enc_qkv.reshape(64, 3, 2, PIECE), (2, 1, 0, 3)).reshape(6, 64, PIECE)
    out = jnp.transpose(enc_out.reshape(64, 2, PIECE), (1, 0, 2))
    feed = jnp.concatenate([up, down], axis=1).reshape(16, 64, PIECE)
    return [feed, jnp.concatenate([triple, out], axis=0)]


def assemble(place_refs, refs, part, piece, w_ref):
    for place_ref, blocks in zip(place_refs, (refs[:CHIPS], refs[CHIPS:])):
        for at, block in enumerate(blocks):
            chip = place_ref[1 + part * CHIPS + at]
            start = pl.multiple_of((2 * chip + place_ref[0]) * 64, 64)
            w_ref[pl.ds(start, 64), :] = block[piece]


def scaled_rows(values, gain):
    wide = values.astype(f32)
    root = jnp.sqrt(jnp.mean(wide * wide, axis=1, keepdims=True) + epsilon)
    return (wide * gain).astype(bf16), root


def enc_mix_kernel(own_ref, other_ref, x_ref, gain_ref, *refs):
    blocks, (out_ref, w_ref, mix_ref) = refs[: 2 * CHIPS], refs[2 * CHIPS :]
    places_both = (own_ref, other_ref)
    for piece in range(8):
        assemble(places_both, blocks, 1, piece, w_ref.at[piece])
    scaled, root = scaled_rows(x_ref[...], gain_ref[...])
    for half in range(2):
        triple = []
        for part in range(3):
            product = jnp.dot(scaled, w_ref[3 * half + part], preferred_element_type=f32)
            triple.append((product / root).astype(bf16))
        for head in range(ENC_HEADS // 2):
            cols = slice(head * ENC_HEAD, (head + 1) * ENC_HEAD)
            scores = lax.dot_general(
                triple[0][:, cols],
                triple[1][:, cols],
                (((1,), (1,)), ((), ())),
                preferred_element_type=f32,
            )
            weights = jnp.exp(scores * ENC_HEAD ** (-0.5))
            denom = jnp.sum(weights, axis=1, keepdims=True)
            numer = jnp.dot(weights.astype(bf16), triple[2][:, cols], preferred_element_type=f32)
            start = half * PIECE + head * ENC_HEAD
            mix_ref[:, start : start + ENC_HEAD] = (numer / denom).astype(bf16)
    mixed = mix_ref[...]
    for at in range(2):
        cols = slice(at * PIECE, (at + 1) * PIECE)
        product = jnp.dot(mixed, w_ref[6 + at], preferred_element_type=f32)
        out_ref[:, cols] = (x_ref[:, cols].astype(f32) + product).astype(bf16)


def enc_feed_kernel(own_ref, other_ref, x_ref, gain_ref, *refs):
    blocks, (out_ref, w_ref, acc_ref) = refs[: 2 * CHIPS], refs[2 * CHIPS :]
    places_both = (own_ref, other_ref)
    for piece in range(8):
        assemble(places_both, blocks, 0, piece, w_ref.at[piece])
    scaled, root = scaled_rows(x_ref[...], gain_ref[...])

    @pl.when(pl.program_id(0) == 0)
    def _():
        acc_ref[...] = x_ref[...].astype(f32)

    for row in range(2):
        hidden = []
        for piece in range(2):
            product = jnp.dot(scaled, w_ref[2 * row + piece], preferred_element_type=f32)
            hidden.append(jax.nn.gelu(product / root, approximate=True).astype(bf16))
        hidden = jnp.concatenate(hidden, axis=1)
        for at in range(2):
            cols = slice(at * PIECE, (at + 1) * PIECE)
            right = w_ref[4 + 2 * row + at]
            acc_ref[:, cols] += jnp.dot(hidden, right, preferred_element_type=f32)

    @pl.when(pl.program_id(0) == 1)
    def _():
        out_ref[...] = acc_ref[...].astype(bf16)


def encode(places_both, embedded, enc_norms, feed, mix):
    out = jax.ShapeDtypeStruct((NB_LEN, ENC_D), bf16)
    full = whole((NB_LEN, ENC_D))
    gain = whole((1, ENC_D))

    def call(kernel, steps, pieces, scratch, x, gains, rows):
        block = (rows[0].shape[0] // steps, 64, PIECE)
        return pl.pallas_call(
            kernel,
            grid_spec=pltpu.PrefetchScalarGridSpec(
                num_scalar_prefetch=2,
                grid=(steps,),
                in_specs=[full, gain]
                + [pl.BlockSpec(block, lambda s, *_: (s, 0, 0)) for _ in rows],
                out_specs=full,
                scratch_shapes=[pltpu.VMEM((pieces, ENC_D, PIECE), bf16), scratch],
            ),
            out_shape=out,
            compiler_params=params(40),
        )(*places_both, x, gains, *rows)

    inner = call(
        enc_mix_kernel, 1, 8, pltpu.VMEM((NB_LEN, ENC_D), bf16), embedded, enc_norms[:1], mix
    )
    return call(
        enc_feed_kernel, 2, 8, pltpu.VMEM((NB_LEN, ENC_D), f32), inner, enc_norms[1:], feed
    )


def encode_neighbour(places_both, ids, enc_embed, enc_norms, local):
    vocab_here = enc_embed.shape[0]
    wanted = ids - lax.axis_index(MP) * vocab_here

    def rows(place, wanted):
        picks = wanted[2 * place[1 : 1 + CHIPS] + place[0]].reshape(-1)
        inside = (picks >= 0) & (picks < vocab_here)
        found = enc_embed[jnp.clip(picks, 0, vocab_here - 1)]
        found = jnp.where(inside[:, None], found, jnp.zeros((), bf16))
        return found.reshape(CHIPS, NB_LEN, ENC_D)

    sent = [[neighbour(value, part, turn) for part, value in enumerate(local)] for turn in range(3)]
    sent[1][0], sent[1][1], *first, wanted = together(*sent[1], *sent[0], wanted)
    passed = [
        [neighbour(value, part, turn) for part, value in enumerate(first)] for turn in (1, 2)
    ]
    other = core_swap(rows(places_both[1], wanted))
    total = rows(places_both[0], wanted) + other
    summed = neighbour(total[4:], 0, 2)
    blocks = []
    for part in range(2):
        second, third = sent[1][part], passed[0][part]
        blocks.append(
            [local[part], first[part], second, third, sent[2][part], passed[1][part]]
            + [neighbour(second, part, 2), neighbour(third, part, 2)]
        )
    total = total[:4] + summed
    total = total[:2] + neighbour(total[2:], 0, 1)
    embedded = total[0] + neighbour(total[1], 0, 0)
    feed, mix = [part + [core_swap(value) for value in part] for part in blocks]
    return encode(places_both, embedded, enc_norms, feed, mix)


def pairs_kernel(place_ref, *refs):
    x_refs, (w_ref, out_ref, left_ref) = refs[:4], refs[4:]
    for part in range(2):
        for block in range(CHIPS):
            chip = place_ref[1 + part * CHIPS + block]
            start = pl.multiple_of(chip * NB_LEN + ENC_STARTS[part], 16)
            value = x_refs[part + 2 * (block // 4)][block % 4]
            left_ref[pl.ds(start, ENC_PARTS[part]), :] = value
    out_ref[...] = jnp.dot(left_ref[...], w_ref[...], preferred_element_type=f32).astype(bf16)


def make_pairs(place, rows, weight):
    out = (CHIPS * NB_LEN, 2 * WIDTH)
    pairs = pl.pallas_call(
        pairs_kernel,
        grid_spec=pltpu.PrefetchScalarGridSpec(
            num_scalar_prefetch=1,
            grid=(1,),
            in_specs=[whole(value.shape) for value in rows] + [whole(weight.shape)],
            out_specs=whole(out),
            scratch_shapes=[pltpu.VMEM((CHIPS * NB_LEN, ENC_D), bf16)],
        ),
        out_shape=jax.ShapeDtypeStruct(out, bf16),
        compiler_params=params(20),
        cost_estimate=pl.CostEstimate(
            flops=2 * CHIPS * NB_LEN * ENC_D * 2 * WIDTH,
            bytes_accessed=2 * (CHIPS * NB_LEN + 2 * WIDTH) * ENC_D,
            transcendentals=0,
        ),
    )(place, *rows, weight)
    return pairs.reshape(BATCH, CHIPS // BATCH, NB_LEN, 2 * WIDTH)


def attention(triple):
    triple = lax.all_to_all(triple, "seq", 0, 0, tiled=True)
    return lax.all_to_all(causal(triple), "seq", 0, 0, tiled=True)


def to_queries(places_both, states, weights):
    norms, triple_w, out_w, query_w, back_w = weights
    triple = project(places_both, *gather_chips(states), norms[0], triple_w, True)
    middle, _ = add_product(places_both, states, attention(triple), out_w)
    asked = project(places_both, *gather_chips(middle), norms[1], query_w[None], False)
    return middle, asked


def cross_layer(places_both, middle, asked, prevs, pairs, weights):
    crossed = cross(asked, prevs, pairs)
    return add_product(places_both, middle, crossed, weights[4])[0]


def on_device(
    hidden_states,
    neighbour_ids,
    neighbour_table,
    enc_embed,
    enc_norms,
    enc_qkv,
    enc_out,
    enc_up,
    enc_down,
    dec_norms,
    dec_qkv,
    dec_out,
    cross_query,
    cross_pair,
    cross_out,
):
    section = lax.axis_index("section").astype(jnp.int32)
    core_at = lax.axis_index("core").astype(jnp.int32)
    chip = lax.axis_index(("z", "y")).astype(jnp.int32)
    places_both = [places(chip, core_at), places(chip, 1 - core_at)]
    slot_ids = neighbour_ids[neighbour_table.reshape(-1)]
    pair_w = cross_pair[0].reshape(ENC_D, 2 * WIDTH)
    weights = (
        dec_norms[0],
        jnp.transpose(dec_qkv[0], (1, 0, 2)),
        dec_out[0],
        cross_query[0],
        cross_out[0],
    )

    states = hidden_states.reshape(BATCH * ROWS, WIDTH)

    def decode():
        middle, asked = to_queries(places_both, by_parts(states), weights)
        return jnp.concatenate(middle), asked, jnp.zeros((NB_LEN, ENC_D), bf16)

    def encode_all():
        local = weight_parts(enc_qkv, enc_out, enc_up, enc_down)
        blank = jnp.zeros(states.shape, bf16)
        return blank, blank, encode_neighbour(places_both, slot_ids, enc_embed, enc_norms, local)

    middle, asked, encoded = lax.cond(section == 0, decode, encode_all)
    middle = by_parts(middle)
    encoded = jnp.where(section == 0, section_swap(encoded), encoded)
    encoded = gather_chips(
        [encoded[start : start + count] for start, count in zip(ENC_STARTS, ENC_PARTS)]
    )
    pairs = [make_pairs(place, rows, pair_w) for place, rows in zip(places_both, encoded)]
    edges = jnp.stack([rows[:, -1] for rows in pairs])
    count = lax.axis_size("seq")
    prevs = lax.ppermute(edges, "seq", [(i, i + 1) for i in range(count - 1)])
    first = cross_layer(places_both, middle, asked, prevs, pairs, weights)
    handed = section_swap(jnp.concatenate(first))
    middle, asked = to_queries(places_both, by_parts(handed), weights)
    second = jnp.concatenate(cross_layer(places_both, middle, asked, prevs, pairs, weights))
    second = second.reshape(BATCH, ROWS, WIDTH)
    return jnp.where(section == 0, section_swap(second[0]), second[1])[None]


def solution(mesh):
    devices = mesh.devices
    sections, seqs = devices.shape[:2]
    split = Mesh(
        devices.reshape(sections, seqs, 2, 4, 2), ("section", "seq", "z", "y", "core")
    )
    mp = ("z", "y", "core")
    return jax.shard_map(
        on_device,
        mesh=split,
        in_specs=(
            P(None, "seq", mp),
            P(),
            P(None, "seq", None),
            P(mp, None),
            P(),
            P(mp, None, None),
            P(mp, None),
            P(mp, None),
            P(mp, None),
            P("section", None, None),
            P("section", None, None, mp),
            P("section", mp, None),
            P("section", None, mp),
            P("section", None, None, mp),
            P("section", mp, None),
        ),
        out_specs=P("section", "seq", mp),
        check_vma=False,
    )
```

```python
import functools

import jax
import jax.numpy as jnp
import numpy as np
from jax import lax
from jax.experimental import pallas as pl
from jax.experimental.pallas import tpu as pltpu
from jax.sharding import Mesh, PartitionSpec as P

D = 4096
HEAD = 128
ENC_D = 1024
ENC_HEADS = 16
ENC_HEAD = 64
BLOCK = 64
NB_LEN = 128
NEIGH = 2
BATCH = 2
CHIPS = 8
ROWS = 256
WIDTH = 256
UNITS = 4
GROUP = 4
MP = ("z", "y", "core")
KEYS = NEIGH * NB_LEN

epsilon = 1e-05
f32 = jnp.float32
bf16 = jnp.bfloat16


def params(mebibytes=16):
    return pltpu.CompilerParams(vmem_limit_bytes=mebibytes * 1024 * 1024)


def whole(shape):
    return pl.BlockSpec(shape, lambda *_: (0,) * len(shape))


SCALAR = pl.BlockSpec(memory_space=pltpu.SMEM)


PARTS = (352, 160)
STARTS = (0, 352)
ENC_PARTS = (80, 48)
ENC_STARTS = (0, 80)
PIECE = 512
MASKS = (((4, 1, 3), (1, 3, 4)), ((3, 4, 1), (3, 4, 1)))


def block_offsets(masks):
    return [
        (masks[0] * (b & 1)) ^ (masks[1] * (b >> 1 & 1)) ^ (masks[2] * (b >> 2 & 1))
        for b in range(CHIPS)
    ]


OFFSETS = np.array([[block_offsets(m) for m in part] for part in MASKS], np.int32)


def core_swap(value):
    return lax.ppermute(value, "core", [(0, 1), (1, 0)])


def section_swap(value):
    return lax.ppermute(value, "section", [(0, 1), (1, 0)])


def chips_to_chips(value):
    return lax.all_to_all(value, ("z", "y"), 0, 0, tiled=True)


def neighbour(value, part, turn):
    route = [
        (2 * chip + core, 2 * (chip ^ MASKS[part][core][turn]) + core)
        for chip in range(CHIPS)
        for core in range(2)
    ]
    return lax.ppermute(value, MP, route)


def places(chip, pick):
    offsets = lax.dynamic_index_in_dim(jnp.asarray(OFFSETS), pick, 1, keepdims=False)
    return jnp.concatenate([jnp.reshape(pick, (1,)), (chip ^ offsets).reshape(-1)]).astype(
        jnp.int32
    )


def together(*values):
    return lax.optimization_barrier(values)


def first_round(local):
    return [neighbour(value, part, 0) for part, value in enumerate(local)]


def later_rounds(local, got):
    near = [jnp.stack(pair) for pair in zip(local, got)]
    got = together(*[neighbour(value, part, 1) for part, value in enumerate(near)])
    near = [jnp.concatenate(pair) for pair in zip(near, got)]
    swaps = [core_swap(value) for value in near]
    far = [neighbour(value, part, 2) for part, value in enumerate(near)]
    swaps = list(together(*swaps))
    far = list(together(*far))
    return near + far, swaps + [core_swap(value) for value in far]


def gather_chips(local):
    return later_rounds(local, together(*first_round(local)))


def scatter_sum(places_both, mixed, weight):
    own, other = places_both
    other_far = [core_swap(value) for value in terms(other, mixed, weight, 1)]
    other_near = [core_swap(value) for value in terms(other, mixed, weight, 0)]
    own_far = terms(own, mixed, weight, 1)
    own_near = terms(own, mixed, weight, 0)
    other_far = together(*other_far)
    sums = [
        (mine.astype(f32) + got.astype(f32)).astype(bf16)
        for mine, got in zip(own_far, other_far)
    ]
    got = together(*[neighbour(sums[part], part, 2) for part in range(2)], *other_near)
    low = [
        own_near[part].astype(f32) + got[2 + part].astype(f32) + got[part].astype(f32)
        for part in range(2)
    ]
    got = together(*[neighbour(low[part][2:].astype(bf16), part, 1) for part in range(2)])
    low = [low[part][:2] + got[part].astype(f32) for part in range(2)]
    got = [neighbour(low[part][1].astype(bf16), part, 0) for part in range(2)]
    return [low[part][0] for part in range(2)], got


def project_kernel(last, units, place_ref, *refs):
    whole_rows = len(refs) == (8 if last else 6)
    count = 1 if whole_rows else 4
    x_refs, (gain_ref, w_ref), refs = refs[:count], refs[count : count + 2], refs[count + 2 :]
    if last:
        acc_in, sq_in, out_ref, sq_ref, left_ref = refs
    else:
        acc_ref, sq_ref, left_ref = refs
    step = pl.program_id(0)

    def place_rows(rows, blocks):
        total = sq_in[rows, :] if last else jnp.zeros((rows.stop - rows.start, 128), f32)
        for block, chip in blocks:
            wide = block.astype(f32)
            squares = wide * wide
            total += squares[:, :128] + squares[:, 128:]
            cols = pl.ds(pl.multiple_of(chip * WIDTH, WIDTH), WIDTH)
            left_ref[rows, cols] = (wide * gain_ref[chip, 0]).astype(bf16)
        sq_ref[rows, :] = total

    @pl.when(step == 0)
    def _():
        for part in range(2):
            rows = slice(STARTS[part], STARTS[part] + PARTS[part])
            if whole_rows:
                blocks = [(x_refs[0][chip, rows, :], chip) for chip in range(CHIPS)]
            else:
                blocks = [
                    (
                        x_refs[part + 2 * (block // 4)][block % 4],
                        place_ref[1 + part * CHIPS + block],
                    )
                    for block in range(CHIPS)
                ]
            place_rows(rows, blocks)

    right = w_ref[0].reshape(CHIPS * WIDTH, WIDTH)
    product = jnp.dot(left_ref[...], right, preferred_element_type=f32)
    if not last:
        acc_ref[0] = product
        return
    mean = jnp.sum(sq_ref[...], axis=1, keepdims=True) / D
    done = ((acc_in[0] + product) / jnp.sqrt(mean + epsilon)).astype(bf16)
    if units:
        for unit in range(UNITS):
            b, h = divmod(unit, 2)
            out_ref[unit, 0] = done[b * ROWS : (b + 1) * ROWS, h * HEAD : (h + 1) * HEAD]
    else:
        out_ref[...] = done


def project_half(place, rows, gains, weight, before, units):
    parts = weight.shape[0]
    count = BATCH * ROWS
    acc = (parts, count, WIDTH)
    sq = (count, 128)
    last = before is not None
    acc_spec = pl.BlockSpec((1, count, WIDTH), lambda s, place: (s, 0, 0))
    in_specs = [whole(value.shape) for value in rows] + [
        pl.BlockSpec((CHIPS, 1, 1, WIDTH), lambda s, place: (0, place[0], 0, 0)),
        pl.BlockSpec((1, CHIPS, 1, WIDTH, WIDTH), lambda s, place: (s, 0, place[0], 0, 0)),
    ]
    scratch = [pltpu.VMEM((count, CHIPS * WIDTH), bf16)]
    if last:
        in_specs += [acc_spec, whole(sq)]
        scratch = [pltpu.VMEM(sq, f32)] + scratch
        if units:
            out = (UNITS, parts, ROWS, HEAD)
            out_specs = pl.BlockSpec((UNITS, 1, ROWS, HEAD), lambda s, place: (0, s, 0, 0))
        else:
            out = (count, WIDTH)
            out_specs = whole(out)
        out_shape = jax.ShapeDtypeStruct(out, bf16)
    else:
        out_specs = [acc_spec, whole(sq)]
        out_shape = [jax.ShapeDtypeStruct(acc, f32), jax.ShapeDtypeStruct(sq, f32)]
    return pl.pallas_call(
        functools.partial(project_kernel, last, units),
        grid_spec=pltpu.PrefetchScalarGridSpec(
            num_scalar_prefetch=1,
            grid=(parts,),
            in_specs=in_specs,
            out_specs=out_specs,
            scratch_shapes=scratch,
        ),
        out_shape=out_shape,
        compiler_params=params(),
        cost_estimate=pl.CostEstimate(
            flops=2 * count * (D // 2) * WIDTH * parts,
            bytes_accessed=D * WIDTH * parts + D * count + 4 * count * WIDTH * parts,
            transcendentals=0,
        ),
    )(
        place,
        *rows,
        gains.reshape(CHIPS, 2, 1, WIDTH),
        weight.reshape(parts, CHIPS, 2, WIDTH, WIDTH),
        *(before or ()),
    )


def project(places_both, same, swap, gains, weight, units):
    before = project_half(places_both[0], same, gains, weight, None, units)
    return project_half(places_both[1], swap, gains, weight, before, units)


def causal_kernel(triple_ref, out_ref):
    scaling = HEAD ** (-0.5)
    row = lax.broadcasted_iota(jnp.int32, (ROWS, ROWS), 0)
    col = lax.broadcasted_iota(jnp.int32, (ROWS, ROWS), 1)
    for i in range(UNITS):
        queries = triple_ref[i, 0]
        numer = jnp.zeros((ROWS, HEAD), f32)
        denom = jnp.zeros((ROWS, 1), f32)
        for j in range(i + 1):
            scores = lax.dot_general(
                queries, triple_ref[j, 1], (((1,), (1,)), ((), ())), preferred_element_type=f32
            )
            weights = jnp.exp(scores * scaling)
            if i == j:
                weights = jnp.where(col <= row, weights, 0.0)
            denom += jnp.sum(weights, axis=1, keepdims=True)
            numer += jnp.dot(weights.astype(bf16), triple_ref[j, 2], preferred_element_type=f32)
        out_ref[i] = (numer / denom).astype(bf16)


def causal(triple):
    out = (UNITS, ROWS, HEAD)
    return pl.pallas_call(
        causal_kernel,
        out_shape=jax.ShapeDtypeStruct(out, bf16),
        compiler_params=params(),
    )(triple)


def crossed_kernel(asked_ref, *refs):
    prev_refs, pairs_refs, out_ref = refs[:2], refs[2:4], refs[4]
    scaling = HEAD ** (-0.5)
    row = lax.broadcasted_iota(jnp.int32, (BLOCK, 2 * KEYS), 0)
    col = lax.broadcasted_iota(jnp.int32, (BLOCK, 2 * KEYS), 1)
    allowed = (row < BLOCK - 1) == (col < KEYS)
    for unit in range(UNITS):
        b, h = divmod(unit, 2)

        def both_blocks(i, cols):
            before = [
                prev[b, :, cols] if i == 0 else pair[b, i - 1, :, cols]
                for prev, pair in zip(prev_refs, pairs_refs)
            ]
            return jnp.concatenate(before + [pair[b, i, :, cols] for pair in pairs_refs], axis=0)

        for i in range(ROWS // BLOCK):
            queries = asked_ref[
                b * ROWS + i * BLOCK : b * ROWS + (i + 1) * BLOCK, h * HEAD : (h + 1) * HEAD
            ]
            keys = both_blocks(i, slice(h * HEAD, (h + 1) * HEAD))
            values = both_blocks(i, slice((2 + h) * HEAD, (3 + h) * HEAD))
            scores = lax.dot_general(
                queries, keys, (((1,), (1,)), ((), ())), preferred_element_type=f32
            )
            weights = jnp.where(allowed, jnp.exp(scores * scaling), 0.0)
            denom = jnp.sum(weights, axis=1, keepdims=True)
            numer = jnp.dot(weights.astype(bf16), values, preferred_element_type=f32)
            out_ref[unit, i * BLOCK : (i + 1) * BLOCK, :] = (numer / denom).astype(bf16)


def cross(asked, prevs, pairs):
    out = (UNITS, ROWS, HEAD)
    return pl.pallas_call(
        crossed_kernel,
        out_shape=jax.ShapeDtypeStruct(out, bf16),
        compiler_params=params(),
    )(asked, *prevs, *pairs)


def terms_kernel(place_ref, mixed_ref, *refs):
    w_refs, out_refs, left_ref = refs[: 2 * GROUP], refs[2 * GROUP : 2 * GROUP + 2], refs[-1]
    for unit in range(UNITS):
        b, h = divmod(unit, 2)
        left_ref[b * ROWS : (b + 1) * ROWS, h * HEAD : (h + 1) * HEAD] = mixed_ref[unit]
    for part in range(2):
        left = left_ref[STARTS[part] : STARTS[part] + PARTS[part], :]
        for at in range(GROUP):
            right = w_refs[part * GROUP + at][...]
            out_refs[part][at] = jnp.dot(left, right, preferred_element_type=f32).astype(bf16)


def terms(place, mixed, weight, high):
    count = BATCH * ROWS

    def columns(part, at):
        index = 1 + part * CHIPS + GROUP * high + at
        return pl.BlockSpec((WIDTH, WIDTH), lambda s, place: (0, 2 * place[index] + place[0]))

    shapes = [(GROUP, PARTS[part], WIDTH) for part in range(2)]
    return pl.pallas_call(
        terms_kernel,
        grid_spec=pltpu.PrefetchScalarGridSpec(
            num_scalar_prefetch=1,
            grid=(1,),
            in_specs=[whole((UNITS, ROWS, HEAD))]
            + [columns(part, at) for part in range(2) for at in range(GROUP)],
            out_specs=[whole(shape) for shape in shapes],
            scratch_shapes=[pltpu.VMEM((count, WIDTH), bf16)],
        ),
        out_shape=[jax.ShapeDtypeStruct(shape, bf16) for shape in shapes],
        compiler_params=params(8),
        cost_estimate=pl.CostEstimate(
            flops=2 * count * WIDTH * D // 4,
            bytes_accessed=D * WIDTH + D * count // 2,
            transcendentals=0,
        ),
    )(place, mixed, *([weight] * (2 * GROUP)))


def add_product(places_both, states, mixed, weight, side=()):
    low, got = scatter_sum(places_both, mixed, weight)
    *got, side = together(*got, side)
    total = [
        (state.astype(f32) + (mine + far.astype(f32))).astype(bf16)
        for state, mine, far in zip(states, low, got)
    ]
    return total, side


def by_parts(rows):
    return [rows[start : start + count] for start, count in zip(STARTS, PARTS)]


def weight_parts(enc_qkv, enc_out, enc_up, enc_down):
    up = enc_up.reshape(64, 16, 2, 2, 64)
    up = jnp.transpose(up, (2, 3, 0, 1, 4)).reshape(2, 2, 64, 2, PIECE)
    up = jnp.transpose(up, (0, 1, 3, 2, 4)).reshape(2, 4, 64, PIECE)
    down = enc_down.reshape(2, 2, 64, 2, PIECE)
    down = jnp.transpose(down, (0, 1, 3, 2, 4)).reshape(2, 4, 64, PIECE)
    triple = jnp.transpose(enc_qkv.reshape(64, 3, 2, PIECE), (2, 1, 0, 3)).reshape(6, 64, PIECE)
    out = jnp.transpose(enc_out.reshape(64, 2, PIECE), (1, 0, 2))
    feed = jnp.concatenate([up, down], axis=1).reshape(16, 64, PIECE)
    return [feed, jnp.concatenate([triple, out], axis=0)]


def assemble(place_refs, refs, part, piece, w_ref):
    for place_ref, (near, far) in zip(place_refs, (refs[:2], refs[2:])):
        for block in range(CHIPS):
            chip = place_ref[1 + part * CHIPS + block]
            start = pl.multiple_of((2 * chip + place_ref[0]) * 64, 64)
            w_ref[pl.ds(start, 64), :] = (near if block < 4 else far)[block % 4, piece]


def scaled_rows(values, gain):
    wide = values.astype(f32)
    root = jnp.sqrt(jnp.mean(wide * wide, axis=1, keepdims=True) + epsilon)
    return (wide * gain).astype(bf16), root


def enc_mix_kernel(own_ref, other_ref, x_ref, gain_ref, *refs):
    blocks, (out_ref, w_ref, mix_ref) = refs[:4], refs[4:]
    places_both = (own_ref, other_ref)
    for piece in range(8):
        assemble(places_both, blocks, 1, piece, w_ref.at[piece])
    scaled, root = scaled_rows(x_ref[...], gain_ref[...])
    for half in range(2):
        triple = []
        for part in range(3):
            product = jnp.dot(scaled, w_ref[3 * half + part], preferred_element_type=f32)
            triple.append((product / root).astype(bf16))
        for head in range(ENC_HEADS // 2):
            cols = slice(head * ENC_HEAD, (head + 1) * ENC_HEAD)
            scores = lax.dot_general(
                triple[0][:, cols],
                triple[1][:, cols],
                (((1,), (1,)), ((), ())),
                preferred_element_type=f32,
            )
            weights = jnp.exp(scores * ENC_HEAD ** (-0.5))
            denom = jnp.sum(weights, axis=1, keepdims=True)
            numer = jnp.dot(weights.astype(bf16), triple[2][:, cols], preferred_element_type=f32)
            start = half * PIECE + head * ENC_HEAD
            mix_ref[:, start : start + ENC_HEAD] = (numer / denom).astype(bf16)
    mixed = mix_ref[...]
    for at in range(2):
        cols = slice(at * PIECE, (at + 1) * PIECE)
        product = jnp.dot(mixed, w_ref[6 + at], preferred_element_type=f32)
        out_ref[:, cols] = (x_ref[:, cols].astype(f32) + product).astype(bf16)


def enc_feed_kernel(own_ref, other_ref, x_ref, gain_ref, *refs):
    blocks, (out_ref, w_ref, acc_ref) = refs[:4], refs[4:]
    places_both = (own_ref, other_ref)
    for piece in range(8):
        assemble(places_both, blocks, 0, piece, w_ref.at[piece])
    scaled, root = scaled_rows(x_ref[...], gain_ref[...])

    @pl.when(pl.program_id(0) == 0)
    def _():
        acc_ref[...] = x_ref[...].astype(f32)

    for row in range(2):
        hidden = []
        for piece in range(2):
            product = jnp.dot(scaled, w_ref[2 * row + piece], preferred_element_type=f32)
            hidden.append(jax.nn.gelu(product / root, approximate=True).astype(bf16))
        hidden = jnp.concatenate(hidden, axis=1)
        for at in range(2):
            cols = slice(at * PIECE, (at + 1) * PIECE)
            right = w_ref[4 + 2 * row + at]
            acc_ref[:, cols] += jnp.dot(hidden, right, preferred_element_type=f32)

    @pl.when(pl.program_id(0) == 1)
    def _():
        out_ref[...] = acc_ref[...].astype(bf16)


def encode(places_both, embedded, enc_norms, feed, mix):
    out = jax.ShapeDtypeStruct((NB_LEN, ENC_D), bf16)
    full = whole((NB_LEN, ENC_D))
    gain = whole((1, ENC_D))

    def call(kernel, steps, pieces, scratch, x, gains, rows):
        block = (4, rows[0].shape[1] // steps, 64, PIECE)
        return pl.pallas_call(
            kernel,
            grid_spec=pltpu.PrefetchScalarGridSpec(
                num_scalar_prefetch=2,
                grid=(steps,),
                in_specs=[full, gain]
                + [pl.BlockSpec(block, lambda s, *_: (0, s, 0, 0)) for _ in rows],
                out_specs=full,
                scratch_shapes=[pltpu.VMEM((pieces, ENC_D, PIECE), bf16), scratch],
            ),
            out_shape=out,
            compiler_params=params(40),
        )(*places_both, x, gains, *rows)

    inner = call(
        enc_mix_kernel, 1, 8, pltpu.VMEM((NB_LEN, ENC_D), bf16), embedded, enc_norms[:1], mix
    )
    return call(
        enc_feed_kernel, 2, 8, pltpu.VMEM((NB_LEN, ENC_D), f32), inner, enc_norms[1:], feed
    )


def encode_neighbour(places_both, ids, enc_embed, enc_norms, local):
    vocab_here = enc_embed.shape[0]
    wanted = ids - lax.axis_index(MP) * vocab_here

    def rows(place, wanted):
        picks = wanted[2 * place[1 : 1 + CHIPS] + place[0]].reshape(-1)
        inside = (picks >= 0) & (picks < vocab_here)
        found = enc_embed[jnp.clip(picks, 0, vocab_here - 1)]
        found = jnp.where(inside[:, None], found, jnp.zeros((), bf16))
        return found.reshape(CHIPS, NB_LEN, ENC_D)

    other = rows(places_both[1], wanted)
    *got, other, wanted = together(*first_round(local), other, wanted)
    near = [jnp.stack(pair) for pair in zip(local, got)]
    sent = [neighbour(value, part, 1) for part, value in enumerate(near)]
    total = rows(places_both[0], wanted) + core_swap(other)
    summed = neighbour(total[4:], 0, 2)
    *got, summed = together(*sent, summed)
    near = [jnp.concatenate(pair) for pair in zip(near, got)]
    swaps = [core_swap(value) for value in near]
    far = together(*[neighbour(value, part, 2) for part, value in enumerate(near)])
    far_swaps = [core_swap(value) for value in far]
    total = total[:4] + summed
    total = total[:2] + neighbour(total[2:], 0, 1)
    embedded = total[0] + neighbour(total[1], 0, 0)
    feed, mix = [
        [near[part], far[part], swaps[part], far_swaps[part]] for part in range(2)
    ]
    return encode(places_both, embedded, enc_norms, feed, mix)


def pairs_kernel(place_ref, *refs):
    x_refs, (w_ref, out_ref, left_ref) = refs[:4], refs[4:]
    for part in range(2):
        for block in range(CHIPS):
            chip = place_ref[1 + part * CHIPS + block]
            start = pl.multiple_of(chip * NB_LEN + ENC_STARTS[part], 16)
            value = x_refs[part + 2 * (block // 4)][block % 4]
            left_ref[pl.ds(start, ENC_PARTS[part]), :] = value
    out_ref[...] = jnp.dot(left_ref[...], w_ref[...], preferred_element_type=f32).astype(bf16)


def make_pairs(place, rows, weight):
    out = (CHIPS * NB_LEN, 2 * WIDTH)
    pairs = pl.pallas_call(
        pairs_kernel,
        grid_spec=pltpu.PrefetchScalarGridSpec(
            num_scalar_prefetch=1,
            grid=(1,),
            in_specs=[whole(value.shape) for value in rows] + [whole(weight.shape)],
            out_specs=whole(out),
            scratch_shapes=[pltpu.VMEM((CHIPS * NB_LEN, ENC_D), bf16)],
        ),
        out_shape=jax.ShapeDtypeStruct(out, bf16),
        compiler_params=params(20),
        cost_estimate=pl.CostEstimate(
            flops=2 * CHIPS * NB_LEN * ENC_D * 2 * WIDTH,
            bytes_accessed=2 * (CHIPS * NB_LEN + 2 * WIDTH) * ENC_D,
            transcendentals=0,
        ),
    )(place, *rows, weight)
    return pairs.reshape(BATCH, CHIPS // BATCH, NB_LEN, 2 * WIDTH)


def attention(triple):
    triple = lax.all_to_all(triple, "seq", 0, 0, tiled=True)
    return lax.all_to_all(causal(triple), "seq", 0, 0, tiled=True)


def to_queries(places_both, states, weights):
    norms, triple_w, out_w, query_w, back_w = weights
    triple = project(places_both, *gather_chips(states), norms[0], triple_w, True)
    middle, _ = add_product(places_both, states, attention(triple), out_w)
    asked = project(places_both, *gather_chips(middle), norms[1], query_w[None], False)
    return middle, asked


def cross_layer(places_both, middle, asked, prevs, pairs, weights):
    crossed = cross(asked, prevs, pairs)
    return add_product(places_both, middle, crossed, weights[4])[0]


def on_device(
    hidden_states,
    neighbour_ids,
    neighbour_table,
    enc_embed,
    enc_norms,
    enc_qkv,
    enc_out,
    enc_up,
    enc_down,
    dec_norms,
    dec_qkv,
    dec_out,
    cross_query,
    cross_pair,
    cross_out,
):
    section = lax.axis_index("section").astype(jnp.int32)
    core_at = lax.axis_index("core").astype(jnp.int32)
    chip = lax.axis_index(("z", "y")).astype(jnp.int32)
    places_both = [places(chip, core_at), places(chip, 1 - core_at)]
    slot_ids = neighbour_ids[neighbour_table.reshape(-1)]
    pair_w = cross_pair[0].reshape(ENC_D, 2 * WIDTH)
    weights = (
        dec_norms[0],
        jnp.transpose(dec_qkv[0], (1, 0, 2)),
        dec_out[0],
        cross_query[0],
        cross_out[0],
    )

    states = hidden_states.reshape(BATCH * ROWS, WIDTH)

    def decode():
        middle, asked = to_queries(places_both, by_parts(states), weights)
        return jnp.concatenate(middle), asked, jnp.zeros((NB_LEN, ENC_D), bf16)

    def encode_all():
        local = weight_parts(enc_qkv, enc_out, enc_up, enc_down)
        blank = jnp.zeros(states.shape, bf16)
        return blank, blank, encode_neighbour(places_both, slot_ids, enc_embed, enc_norms, local)

    middle, asked, encoded = lax.cond(section != 0, encode_all, decode)
    middle = by_parts(middle)
    encoded = jnp.where(section == 0, section_swap(encoded), encoded)
    encoded = gather_chips(
        [encoded[start : start + count] for start, count in zip(ENC_STARTS, ENC_PARTS)]
    )
    pairs = [make_pairs(place, rows, pair_w) for place, rows in zip(places_both, encoded)]
    count = lax.axis_size("seq")
    prevs = [
        lax.ppermute(rows[:, -1], "seq", [(i, i + 1) for i in range(count - 1)]) for rows in pairs
    ]
    first = cross_layer(places_both, middle, asked, prevs, pairs, weights)
    handed = section_swap(jnp.concatenate(first))
    middle, asked = to_queries(places_both, by_parts(handed), weights)
    second = jnp.concatenate(cross_layer(places_both, middle, asked, prevs, pairs, weights))
    second = second.reshape(BATCH, ROWS, WIDTH)
    return jnp.where(section == 0, section_swap(second[0]), second[1])[None]


def solution(mesh):
    devices = mesh.devices
    sections, seqs = devices.shape[:2]
    split = Mesh(
        devices.reshape(sections, seqs, 2, 4, 2), ("section", "seq", "z", "y", "core")
    )
    mp = ("z", "y", "core")
    return jax.shard_map(
        on_device,
        mesh=split,
        in_specs=(
            P(None, "seq", mp),
            P(),
            P(None, "seq", None),
            P(mp, None),
            P(),
            P(mp, None, None),
            P(mp, None),
            P(mp, None),
            P(mp, None),
            P("section", None, None),
            P("section", None, None, mp),
            P("section", mp, None),
            P("section", None, mp),
            P("section", None, None, mp),
            P("section", mp, None),
        ),
        out_specs=P("section", "seq", mp),
        check_vma=False,
    )
```
